32 devices in a mesh: section: 4 (over y, core), edge: 8 (over z, x).
Axes of the slice: x: 2, y: 2, z: 4, core: 2. Of those that a mesh axis runs over, the one named last changes fastest.
Arguments:
- layer_nodes: bfloat16 [4, 2, 256, 512], P('section'), may hold values from -6 to 6
- layer_edges: bfloat16 [4, 2, 2048, 512], P('section', None, 'edge'), may hold values from -6 to 6
- top_nodes: bfloat16 [2, 256, 512], replicated, may hold values from -1.5 to 1.5
- top_edges: bfloat16 [2, 2048, 512], P(None, 'edge'), may hold values from -1.5 to 1.5
- tile_blocks: int32 [2, 16, 2], P(None, 'edge'), may hold values from 0 to 1
- senders: int32 [2, 2048], P(None, 'edge'), may hold values from 0 to 127
- receivers: int32 [2, 2048], P(None, 'edge'), may hold values from 0 to 127
- w_send: bfloat16 [4, 512, 512], P('section'), may hold values from -0.0625 to 0.0625
- w_recv: bfloat16 [4, 512, 512], P('section'), may hold values from -0.0625 to 0.0625
- w_edge: bfloat16 [4, 512, 512], P('section'), may hold values from -0.25 to 0.25
- w_msg: bfloat16 [4, 512, 512], P('section'), may hold values from -0.125 to 0.125
- w_node: bfloat16 [4, 512, 512], P('section'), may hold values from -0.25 to 0.25
- w_agg: bfloat16 [4, 512, 512], P('section'), may hold values from -0.25 to 0.25
- w_out: bfloat16 [4, 512, 512], P('section'), may hold values from -0.125 to 0.125
Outputs:
- node_grads: bfloat16 [4, 2, 256, 512], P('section', None, 'edge')
- edge_grads: bfloat16 [4, 2, 2048, 512], P('section', None, 'edge')
- g_send: float32 [4, 512, 512], P('section', 'edge')
- g_recv: float32 [4, 512, 512], P('section', 'edge')
- g_edge: float32 [4, 512, 512], P('section', 'edge')
- g_msg: float32 [4, 512, 512], P('section', 'edge')
- g_node: float32 [4, 512, 512], P('section', 'edge')
- g_agg: float32 [4, 512, 512], P('section', 'edge')
- g_out: float32 [4, 512, 512], P('section', 'edge')
The draws below stay inside these ranges and needn't reach their ends.
All inputs are finite; a program needn't handle non-finite values.
Results may differ from the reference program's by a relative error of at most 0.029.
Values may be sent and summed in bfloat16 or wider, within the bound.
No kernel may reach another device: no remote copies, remote signals or barrier semaphores. Data moves between devices by JAX's collectives and lax.ppermute only.
A program may use at most 64 MiB of HBM per device.

```python
import jax
import jax.numpy as jnp

D = 512
HIDDEN_SIZE = 512
BLOCK = 128
TILE_E = 128
MB = 2
NODE_BLOCKS = 2
LAYERS = 4
NODES_MB = 256
TILES = 16
EDGES = 2048


def with_ends(result, stream_key, low, top_value):
    extent = result.shape
    index_at = [jax.random.randint(jax.random.fold_in(stream_key, axis), (), 0, extent[axis]) for axis in range(len(extent))]
    result = result.at[tuple(index_at)].set(low)
    longest = extent.index(max(extent))
    index_at[longest] = (index_at[longest] + 1) % extent[longest]
    return result.at[tuple(index_at)].set(top_value)


def level_of(stream_key, shape, cuts, least, largest):
    level = 1.0
    for axis_at, shards_of in cuts:
        heights = jax.random.uniform(jax.random.fold_in(jax.random.fold_in(stream_key, 6), axis_at), (shards_of,), jnp.float32, least / len(cuts), largest / len(cuts))
        level = level * jnp.repeat(jnp.exp(heights), shape[axis_at] // shards_of).reshape((-1,) + (1,) * (len(shape) - 1 - axis_at))
    return level


def noise(rng, shape, scale, limit, cuts=(), held_as=jnp.bfloat16):
    gain = level_of(rng, shape, cuts, -0.22, 0.18) if cuts else 1.0
    drawn = jax.random.normal(rng, shape, jnp.float32) * scale * gain
    return jnp.minimum(jnp.maximum(drawn, -limit), limit).astype(held_as)


def setup_inputs(seed: int = 0) -> dict:
    key_of = jax.random.split(jax.random.key(seed), 15)
    layer_nodes = noise(key_of[0], (LAYERS, MB, NODES_MB, D), 1.0, 6.0, ((0, 4),))
    layer_edges = noise(key_of[1], (LAYERS, MB, EDGES, D), 1.0, 6.0, ((0, 4), (2, 8)))
    top_nodes = noise(key_of[2], (MB, NODES_MB, D), 0.25, 1.5)
    top_edges = noise(key_of[3], (MB, EDGES, D), 0.25, 1.5, ((1, 8),))
    tile_blocks = with_ends(jax.random.randint(key_of[4], (MB, TILES, 2), 0, NODE_BLOCKS), jax.random.fold_in(key_of[4], 1), 0, NODE_BLOCKS - 1).astype(jnp.int32)
    senders = with_ends(jax.random.randint(key_of[5], (MB, EDGES), 0, BLOCK), jax.random.fold_in(key_of[5], 1), 0, BLOCK - 1).astype(jnp.int32)
    receivers = with_ends(jax.random.randint(key_of[6], (MB, EDGES), 0, BLOCK), jax.random.fold_in(key_of[6], 1), 0, BLOCK - 1).astype(jnp.int32)
    w_send = noise(key_of[7], (LAYERS, D, HIDDEN_SIZE), (16 * D) ** -0.5, 0.0625, ((0, 4),))
    w_recv = noise(key_of[8], (LAYERS, D, HIDDEN_SIZE), (16 * D) ** -0.5, 0.0625, ((0, 4),))
    w_edge = noise(key_of[9], (LAYERS, D, HIDDEN_SIZE), D ** -0.5, 0.25, ((0, 4),))
    w_msg = noise(key_of[10], (LAYERS, HIDDEN_SIZE, D), (4 * HIDDEN_SIZE) ** -0.5, 0.125, ((0, 4),))
    w_node = noise(key_of[11], (LAYERS, D, HIDDEN_SIZE), D ** -0.5, 0.25, ((0, 4),))
    w_agg = noise(key_of[12], (LAYERS, D, HIDDEN_SIZE), D ** -0.5, 0.25, ((0, 4),))
    w_out = noise(key_of[13], (LAYERS, HIDDEN_SIZE, D), (4 * HIDDEN_SIZE) ** -0.5, 0.125, ((0, 4),))
    return dict(layer_nodes=layer_nodes, layer_edges=layer_edges, top_nodes=top_nodes, top_edges=top_edges, tile_blocks=tile_blocks, senders=senders, receivers=receivers, w_send=w_send, w_recv=w_recv, w_edge=w_edge, w_msg=w_msg, w_node=w_node, w_agg=w_agg, w_out=w_out)


def silu_slope(values):
    sigma = jax.nn.sigmoid(values)
    return sigma * (1.0 + values * (1.0 - sigma))


def matmul(left, right):
    return jnp.dot(left, right, preferred_element_type=jnp.float32)


def layer_back(feats, edge_feats, grad_nodes, grad_edges, send_index, recv_index, weights):
    w_send, w_recv, w_edge, w_msg, w_node, w_agg, w_out = weights
    send_feats = feats[send_index]
    recv_feats = feats[recv_index]
    pre = matmul(send_feats, w_send) + matmul(recv_feats, w_recv) + matmul(edge_feats, w_edge)
    act = jax.nn.silu(pre).astype(jnp.bfloat16)
    message = matmul(act, w_msg).astype(jnp.bfloat16)
    aggregate = jax.ops.segment_sum(message.astype(jnp.float32), recv_index, num_segments=NODES_MB)
    agg_b = aggregate.astype(jnp.bfloat16)
    node_pre = matmul(feats, w_node) + matmul(agg_b, w_agg)
    node_act = jax.nn.silu(node_pre).astype(jnp.bfloat16)
    node_delta = (matmul(grad_nodes, w_out.T) * silu_slope(node_pre)).astype(jnp.bfloat16)
    agg_grad = matmul(node_delta, w_agg.T).astype(jnp.bfloat16)
    message_grad = (grad_edges.astype(jnp.float32) + agg_grad[recv_index].astype(jnp.float32)).astype(jnp.bfloat16)
    edge_delta = (matmul(message_grad, w_msg.T) * silu_slope(pre)).astype(jnp.bfloat16)
    edge_out = (grad_edges.astype(jnp.float32) + matmul(edge_delta, w_edge.T)).astype(jnp.bfloat16)
    send_grad = matmul(edge_delta, w_send.T).astype(jnp.bfloat16)
    recv_grad = matmul(edge_delta, w_recv.T).astype(jnp.bfloat16)
    scattered = jax.ops.segment_sum(send_grad.astype(jnp.float32), send_index, num_segments=NODES_MB)
    scattered = scattered + jax.ops.segment_sum(recv_grad.astype(jnp.float32), recv_index, num_segments=NODES_MB)
    node_out = (grad_nodes.astype(jnp.float32) + matmul(node_delta, w_node.T) + scattered).astype(jnp.bfloat16)
    grads = (matmul(send_feats.T, edge_delta), matmul(recv_feats.T, edge_delta), matmul(edge_feats.T, edge_delta),
             matmul(act.T, message_grad), matmul(feats.T, node_delta), matmul(agg_b.T, node_delta),
             matmul(node_act.T, grad_nodes))
    return node_out, edge_out, grads


def reference(layer_nodes, layer_edges, top_nodes, top_edges, tile_blocks, senders, receivers,
              w_send, w_recv, w_edge, w_msg, w_node, w_agg, w_out):
    tile_of_edge = jnp.arange(EDGES, dtype=jnp.int32) // TILE_E
    node_table = [[None] * MB for layer in range(LAYERS)]
    edge_table = [[None] * MB for layer in range(LAYERS)]
    grad_table = [None] * LAYERS
    for batch in range(MB):
        send_index = (tile_blocks[batch, :, 0][tile_of_edge] * BLOCK + senders[batch]).astype(jnp.int32)
        recv_index = (tile_blocks[batch, :, 1][tile_of_edge] * BLOCK + receivers[batch]).astype(jnp.int32)
        grad_nodes = top_nodes[batch]
        grad_edges = top_edges[batch]
        for layer in reversed(range(LAYERS)):
            weights = (w_send[layer], w_recv[layer], w_edge[layer], w_msg[layer],
                       w_node[layer], w_agg[layer], w_out[layer])
            grad_nodes, grad_edges, grads = layer_back(layer_nodes[layer, batch], layer_edges[layer, batch],
                                                       grad_nodes, grad_edges, send_index, recv_index, weights)
            node_table[layer][batch] = grad_nodes
            edge_table[layer][batch] = grad_edges
            if grad_table[layer] is None:
                grad_table[layer] = grads
            else:
                grad_table[layer] = tuple(before + extra for before, extra in zip(grad_table[layer], grads))
    node_grads = jnp.stack([jnp.stack(node_table[layer]) for layer in range(LAYERS)])
    edge_grads = jnp.stack([jnp.stack(edge_table[layer]) for layer in range(LAYERS)])
    stacked = [jnp.stack([grad_table[layer][index] for layer in range(LAYERS)]) for index in range(7)]
    return (node_grads, edge_grads, stacked[0], stacked[1], stacked[2], stacked[3], stacked[4], stacked[5], stacked[6])
```

```python
import functools

import jax
import jax.numpy as jnp
from jax import lax
from jax.experimental import pallas as pl
from jax.experimental.pallas import tpu as pltpu
from jax.sharding import PartitionSpec as P

BLOCK = 128
PARTS = 2
PAD = 16
BF = jnp.bfloat16
F32 = jnp.float32
ANY = pl.BlockSpec(memory_space=pl.ANY)
SMEM = pl.BlockSpec(memory_space=pltpu.SMEM)
VMEM = pl.BlockSpec(memory_space=pltpu.VMEM)


def matmul(left, right):
    return jnp.dot(left, right, preferred_element_type=F32)


def times_transposed(left, right):
    return lax.dot_general(left, right, (((1,), (1,)), ((), ())), preferred_element_type=F32)


def transposed_times(left, right):
    return lax.dot_general(left, right, (((0,), (0,)), ((), ())), preferred_element_type=F32)


class Copies:
    def __init__(self, sems):
        self.sems = sems
        self.count = 0

    def start(self, source, target):
        copy = pltpu.make_async_copy(source, target, self.sems.at[self.count])
        self.count += 1
        copy.start()
        return copy


def base_of(half, span, batches):
    return jnp.where(half == 0, span - batches, 0)


def place_of(batch, half, span, batches):
    return (span - batches if half == 0 else 0) + batch


def worker_of(batch, half, span, batches):
    return half * span + place_of(batch, half, span, batches)


def own_batch(member, span, batches):
    half = lax.div(member, span)
    batch = lax.rem(member, span) - base_of(half, span, batches)
    return jnp.clip(batch, 0, batches - 1)


def pick_row(table, row, lanes):
    value = table[0:1, lanes]
    for other in range(1, table.shape[0]):
        value = jnp.where(row == other, table[other : other + 1, lanes], value)
    return value


def hot_rows(index_rows, row, nodes):
    index = index_rows[row : row + 1, :]
    rows = lax.broadcasted_iota(jnp.int32, (nodes, index_rows.shape[1]), 0)
    return jnp.where(rows == index, 1.0, 0.0).astype(BF)


def pack_kernel(span, batches, info, senders, receivers, tiles, edges, *refs):
    index_out = refs[0]
    outs = refs[1 : 1 + span - 1]
    rows, sems = refs[span:]
    copies = Copies(sems)
    member = info[1]
    half = lax.div(member, span)
    offset = lax.rem(member, span)
    count = senders.shape[1]
    tile_count = tiles.shape[1]
    tile_len = count // tile_count
    waits = []
    picks = []
    for step in range(span):
        batch = lax.rem(offset - step + span, span) - base_of(half, span, batches)
        batch = jnp.clip(batch, 0, batches - 1)
        picks.append(batch)
        if step:
            waits.append(copies.start(edges.at[0, batch], outs[step - 1].at[pl.ds(0, count)]))
    rows[...] = jnp.zeros_like(rows)
    for step in range(span):
        batch = picks[step]
        for tile in range(tile_count):
            lanes = slice(tile * tile_len, (tile + 1) * tile_len)
            send = pick_row(senders, batch, lanes) + tiles[batch, tile, 0] * BLOCK
            recv = pick_row(receivers, batch, lanes) + tiles[batch, tile, 1] * BLOCK
            which = lax.broadcasted_iota(jnp.int32, (PAD, tile_len), 0)
            block = jnp.where(which == 0, send, jnp.where(which == 1, recv, 0))
            rows[step, :, lanes] = block.astype(F32).astype(BF)
        target = index_out if step == 0 else outs[step - 1].at[pl.ds(count, PAD)]
        waits.append(copies.start(rows.at[step], target))
    for wait in waits:
        wait.wait()


def forward_kernel(span, batches, info, nodes, edges, own_index, *refs):
    others = refs[: span - 1]
    w_send, w_recv, w_edge, w_msg = refs[span - 1 : span + 3]
    act_out, slope_out, part_out, index_out = refs[span + 3 : span + 7]
    feats, pieces, weights, hidden, acts, slopes, part, sems = refs[span + 7 :]
    copies = Copies(sems)
    batch = own_batch(info[1], span, batches)
    count = edges.shape[2]
    node_count = nodes.shape[2]
    get_feats = copies.start(nodes.at[0, batch], feats)
    get_w = [copies.start(w.at[0], weights.at[k]) for k, w in enumerate((w_send, w_recv, w_edge, w_msg))]
    get_piece = [
        [
            copies.start(edges.at[0, batch], pieces.at[0, pl.ds(0, count)]),
            copies.start(own_index, pieces.at[0, pl.ds(count, PAD)]),
        ]
    ]
    for step in range(1, span):
        get_piece.append([copies.start(others[step - 1], pieces.at[step])])
    get_feats.wait()
    get_w[0].wait()
    hidden[:node_count] = matmul(feats[...], weights[0]).astype(BF)
    get_w[1].wait()
    hidden[node_count:] = matmul(feats[...], weights[1]).astype(BF)
    get_w[2].wait()
    puts = []
    total = None
    for step in range(span):
        for get in get_piece[step]:
            get.wait()
        puts.append(copies.start(pieces.at[step, pl.ds(count, PAD)], index_out.at[step]))
        index_rows = pieces[step, count : count + PAD, :count].astype(F32).astype(jnp.int32)
        send_hot = hot_rows(index_rows, 0, node_count)
        recv_hot = hot_rows(index_rows, 1, node_count)
        both = jnp.concatenate([send_hot, recv_hot], axis=0)
        pre = transposed_times(both, hidden[...]) + matmul(pieces[step, :count], weights[2])
        sigma = jax.nn.sigmoid(pre)
        act = (pre * sigma).astype(BF)
        acts[step * count : (step + 1) * count] = act
        slopes[step * count : (step + 1) * count] = (sigma * (1.0 + pre * (1.0 - sigma))).astype(BF)
        run = pl.ds(step * count, count)
        puts.append(copies.start(acts.at[run], act_out.at[run]))
        puts.append(copies.start(slopes.at[run], slope_out.at[run]))
        added = matmul(recv_hot, act)
        total = added if total is None else total + added
    get_w[3].wait()
    part[...] = matmul(total.astype(BF), weights[3]).astype(BF)
    puts.append(copies.start(part, part_out))
    for put in puts:
        put.wait()


def node_kernel(span, batches, info, nodes, part_own, part_other, w_node, w_agg, out):
    batch = own_batch(info[1], span, batches)
    count = nodes.shape[2]
    agg = (part_own[...].astype(F32) + part_other[...].astype(F32)).astype(BF)
    pre = matmul(nodes[0, batch], w_node[0]) + matmul(agg, w_agg[0])
    sigma = jax.nn.sigmoid(pre)
    out[:count] = agg
    out[count : 2 * count] = (pre * sigma).astype(BF)
    out[2 * count :] = (sigma * (1.0 + pre * (1.0 - sigma))).astype(BF)


def chain_kernel(span, batches, count, active, info, *refs):
    if active is None:
        chain_step(span, batches, count, True, info, *refs)
    else:
        refs = refs[:2] + refs[4:]

        @pl.when(info[0] == active)
        def _():
            chain_step(span, batches, count, False, info, *refs)


def chain_step(span, batches, count, first, info, *refs):
    if first:
        top_nodes, top_edges = refs[:2]
        others = refs[2 : span + 1]
        refs = refs[span + 1 :]
    else:
        came, cross = refs[:2]
        refs = refs[2:]
    index, slope, node_pack = refs[:3]
    w_out, w_agg, w_msg, w_edge, w_node, w_send, w_recv = refs[3:10]
    pay_out, part_out, keep_out = refs[10:13]
    grad_a, grad_b, pay, rows, slopes, node_slope, weights, hots, keep, sems = refs[13:]
    copies = Copies(sems)
    member = info[1]
    batch = own_batch(member, span, batches)
    half = lax.div(member, span)
    node_count = grad_a.shape[0]
    total = span * count
    if first:
        get_grad = [copies.start(top_nodes.at[batch], grad_a)]
    else:
        get_grad = [copies.start(came.at[pl.ds(total, node_count)], grad_a), copies.start(cross, grad_b)]
    get_w = {}

    def fetch(slot, ref):
        get_w[slot] = copies.start(ref.at[0], weights.at[slot])

    fetch(0, w_out)
    get_slope_n = copies.start(node_pack.at[pl.ds(2 * node_count, node_count)], node_slope)
    fetch(1, w_agg)
    get_index = copies.start(index, rows)
    fetch(2, w_msg)
    get_edge, get_slope = [], []
    for step in range(span):
        run = pl.ds(step * count, count)
        if first:
            source = top_edges.at[batch] if step == 0 else others[step - 1]
        else:
            source = came.at[run]
        get_edge.append(copies.start(source, pay.at[run]))
        get_slope.append(copies.start(slope.at[run], slopes.at[run]))
        if step == 0:
            fetch(3, w_edge)
    fetch(4, w_node)
    fetch(5, w_send)
    fetch(6, w_recv)
    puts = []

    for get in get_grad:
        get.wait()
    if first:
        grad = grad_a[...]
    else:
        grad = (grad_a[...].astype(F32) + grad_b[...].astype(F32)).astype(BF)
    node_at = 2 * total
    get_w[0].wait()
    get_slope_n.wait()
    delta = (times_transposed(grad, weights[0]) * node_slope[...].astype(F32)).astype(BF)
    get_w[1].wait()
    agg_grad = times_transposed(delta, weights[1]).astype(BF)
    keep[node_at : node_at + node_count] = delta
    keep[node_at + node_count : node_at + 2 * node_count] = grad
    get_index.wait()
    get_w[2].wait()
    for step in range(span):
        at = step * count
        run = slice(at, at + count)
        index_rows = rows[step, :, :count].astype(F32).astype(jnp.int32)
        send_hot = hot_rows(index_rows, 0, node_count)
        recv_hot = hot_rows(index_rows, 1, node_count)
        hots[:node_count, run] = send_hot
        hots[node_count:, run] = recv_hot
        get_edge[step].wait()
        incoming = pay[run].astype(F32)
        spread = transposed_times(recv_hot, agg_grad)
        message_grad = (incoming + spread).astype(BF)
        keep[run] = message_grad
        get_slope[step].wait()
        edge_delta = (times_transposed(message_grad, weights[2]) * slopes[run].astype(F32)).astype(BF)
        keep[total + at : total + at + count] = edge_delta
        if step == 0:
            get_w[3].wait()
        pay[run] = (incoming + times_transposed(edge_delta, weights[3])).astype(BF)
        piece = pl.ds(at, count)
        puts.append(copies.start(pay.at[piece], pay_out.at[piece]))
    sums = matmul(hots[...], keep[total : 2 * total]).astype(BF)
    keep[node_at + 2 * node_count :] = sums
    get_w[4].wait()
    get_w[5].wait()
    get_w[6].wait()
    own = grad.astype(F32) + times_transposed(delta, weights[4])
    own = own * jnp.where(half == 0, 1.0, 0.0)
    part = times_transposed(sums[:node_count], weights[5]) + times_transposed(sums[node_count:], weights[6])
    pay[total:] = (own + part).astype(BF)
    tail = pl.ds(total, node_count)
    puts.append(copies.start(pay.at[tail], pay_out.at[tail]))
    puts.append(copies.start(pay.at[tail], part_out))
    puts.append(copies.start(keep, keep_out))
    for put in puts:
        put.wait()


def grads_kernel(span, batches, groups, info, nodes, edges, *refs):
    others = refs[: span - 1]
    act, node_pack = refs[span - 1 : span + 1]
    kept, paid = refs[span + 1 : span + 3]
    refs = refs[span + 3 :]
    blocks = refs[:groups]
    returns = refs[groups : groups + span]
    feats, pieces, acts, packs, keep, part, sums, sems = refs[groups + span :]
    copies = Copies(sems)
    member = info[1]
    batch = own_batch(member, span, batches)
    half = lax.div(member, span)
    count = edges.shape[2]
    node_count = nodes.shape[2]
    width = nodes.shape[3]
    total = span * count
    gets = [copies.start(nodes.at[0, batch], feats), copies.start(node_pack, packs), copies.start(act, acts)]
    gets.append(copies.start(edges.at[0, batch], pieces.at[0]))
    for step in range(1, span):
        gets.append(copies.start(others[step - 1].at[pl.ds(0, count)], pieces.at[step]))
    gets.append(copies.start(kept, keep))
    gets.append(copies.start(paid.at[pl.ds(total, node_count)], part))
    puts = [copies.start(paid.at[pl.ds(step * count, count)], returns[step]) for step in range(span)]
    for get in gets:
        get.wait()
    node_at = 2 * total
    delta = keep[node_at : node_at + node_count]
    grad = keep[node_at + node_count : node_at + 2 * node_count]
    sent = keep[node_at + 2 * node_count : node_at + 3 * node_count]
    received = keep[node_at + 3 * node_count :]
    sums[0] = transposed_times(feats[...], sent).astype(BF)
    sums[1] = transposed_times(feats[...], received).astype(BF)
    edge_sum = None
    for step in range(span):
        added = transposed_times(pieces[step], keep[total + step * count : total + (step + 1) * count])
        edge_sum = added if edge_sum is None else edge_sum + added
    sums[2] = edge_sum.astype(BF)
    sums[3] = transposed_times(acts[...], keep[:total]).astype(BF)
    sums[5] = transposed_times(packs[:node_count], delta).astype(BF)

    @pl.when(half == 0)
    def _():
        sums[4] = transposed_times(feats[...], delta).astype(BF)

    @pl.when(half != 0)
    def _():
        sums[4] = transposed_times(packs[node_count : 2 * node_count], grad).astype(BF)

    share = width // groups
    node_share = node_count // groups
    for step in range(groups):
        owner = lax.rem(member + step, groups)
        at = pl.multiple_of(owner * share, share)
        for slot in range(5):
            puts.append(copies.start(sums.at[slot, pl.ds(at, share)], blocks[step].at[pl.ds(slot * share, share)]))
        at_half = pl.multiple_of(owner * share + half * (share // 2), share // 2)
        puts.append(
            copies.start(sums.at[5, pl.ds(at_half, share // 2)], blocks[step].at[pl.ds(5 * share, share // 2)])
        )
        at_node = pl.multiple_of(owner * node_share, node_share)
        puts.append(
            copies.start(
                part.at[pl.ds(at_node, node_share)], blocks[step].at[pl.ds(5 * share + share // 2, node_share)]
            )
        )
    for put in puts:
        put.wait()


def finish_kernel(span, batches, groups, info, *refs):
    blocks = refs[:groups]
    returns = refs[groups : groups + span]
    refs = refs[groups + span :]
    nodes_out, edges_out, send_out, recv_out, edge_out, msg_out, node_out, agg_out, out_out = refs[:9]
    held, sems = refs[9:]
    copies = Copies(sems)
    member = info[1]
    half = lax.div(member, span)
    offset = lax.rem(member, span)
    back_sems = copies.count
    copies.count += batches
    for batch in range(batches):
        turn = lax.rem(offset - base_of(half, span, batches) - batch + 2 * span, span)
        for step in range(span):

            @pl.when(turn == step)
            def _(batch=batch, step=step):
                pltpu.make_async_copy(returns[step], edges_out.at[0, batch], sems.at[back_sems + batch]).start()

    for batch in range(batches):
        for part in range(PARTS):
            worker = worker_of(batch, part, span, batches)
            turn = lax.rem(member - worker + groups, groups)
            slot = copies.count
            copies.count += 1
            for step in range(groups):

                @pl.when(turn == step)
                def _(batch=batch, part=part, step=step, slot=slot):
                    pltpu.make_async_copy(blocks[step], held.at[batch, part], sems.at[slot]).start()

            pltpu.make_async_copy(blocks[0], held.at[batch, part], sems.at[slot]).wait()
    share = send_out.shape[1]
    for slot, out in enumerate((send_out, recv_out, edge_out, msg_out)):
        rows = slice(slot * share, (slot + 1) * share)
        value = None
        for batch in range(batches):
            for part in range(PARTS):
                piece = held[batch, part, rows].astype(F32)
                value = piece if value is None else value + piece
        out[0] = value

    def over_batches(part, start, length):
        value = None
        for batch in range(batches):
            piece = held[batch, part, start : start + length].astype(F32)
            value = piece if value is None else value + piece
        return value

    node_out[0] = over_batches(0, 4 * share, share)
    out_out[0] = over_batches(1, 4 * share, share)
    for part in range(PARTS):
        agg_out[0, part * (share // 2) : (part + 1) * (share // 2)] = over_batches(part, 5 * share, share // 2)
    at = 5 * share + share // 2
    for batch in range(batches):
        rows = held[batch, 0, at:].astype(F32) + held[batch, 1, at:].astype(F32)
        nodes_out[0, batch] = rows.astype(BF)
    for batch in range(batches):
        pltpu.make_async_copy(returns[0], edges_out.at[0, batch], sems.at[back_sems + batch]).wait()


def call(kernel, name, in_specs, out_shapes, out_specs, scratch, flops, touched, aliases={}):
    return pl.pallas_call(
        kernel,
        name=name,
        out_shape=out_shapes,
        in_specs=in_specs,
        out_specs=out_specs,
        scratch_shapes=scratch,
        input_output_aliases=aliases,
        compiler_params=pltpu.CompilerParams(vmem_limit_bytes=48 * 1024 * 1024),
        cost_estimate=pl.CostEstimate(flops=flops, bytes_accessed=touched, transcendentals=0),
    )


def body(
    layer_nodes,
    layer_edges,
    top_nodes,
    top_edges,
    tile_blocks,
    senders,
    receivers,
    w_send,
    w_recv,
    w_edge,
    w_msg,
    w_node,
    w_agg,
    w_out,
):
    sections = lax.axis_size("section")
    groups = lax.axis_size("edge")
    section = lax.axis_index("section")
    member = lax.axis_index("edge")
    span = groups // PARTS
    _, batches, node_count, width = layer_nodes.shape
    count = layer_edges.shape[2]
    total = span * count
    share = width // groups
    node_share = node_count // groups
    info = jnp.stack([section, member]).astype(jnp.int32)
    axes = ("section", "edge")
    works = [(m, h) for h in range(PARTS) for m in range(batches)]

    def worker(m, h):
        return worker_of(m, h, span, batches)

    def source(m, h, step):
        return h * span + (place_of(m, h, span, batches) + step) % span

    def move(value, layers, links, shift=0):
        pairs = [(s * groups + a, (s + shift) * groups + b) for s in layers for a, b in links]
        return lax.ppermute(value, axes, pairs)

    every = list(range(sections))
    last = [sections - 1]
    collect = [[(source(m, h, step), worker(m, h)) for m, h in works] for step in range(span)]
    deliver = [[(b, a) for a, b in links] for links in collect]

    def like(rows, cols=width, kind=BF):
        return jax.ShapeDtypeStruct((rows, cols), kind)

    def sems(n):
        return pltpu.SemaphoreType.DMA((n,))

    packed = call(
        functools.partial(pack_kernel, span, batches),
        "pack",
        [SMEM, VMEM, VMEM, SMEM, ANY],
        [like(PAD)] + [like(count + PAD)] * (span - 1),
        [ANY] * span,
        [pltpu.VMEM((span, PAD, width), BF), sems(2 * span)],
        0,
        2**20,
    )(info, senders, receivers, tile_blocks, layer_edges)
    own_index, pieces = packed[0], packed[1:]
    pieces = [move(piece, every, collect[step + 1]) for step, piece in enumerate(pieces)]
    half = member // span
    offset = member % span
    tops = []
    for step in range(1, span):
        pick = jnp.clip((offset - step) % span - base_of(half, span, batches), 0, batches - 1)
        tops.append(
            move(lax.dynamic_index_in_dim(top_edges, pick, 0, keepdims=False), last, collect[step])
        )

    act, slope, part, index = call(
        functools.partial(forward_kernel, span, batches),
        "forward",
        [SMEM] + [ANY] * (span + 6),
        [like(total), like(total), like(node_count), jax.ShapeDtypeStruct((span, PAD, width), BF)],
        [ANY] * 4,
        [
            pltpu.VMEM((node_count, width), BF),
            pltpu.VMEM((span, count + PAD, width), BF),
            pltpu.VMEM((4, width, width), BF),
            pltpu.VMEM((2 * node_count, width), BF),
            pltpu.VMEM((total, width), BF),
            pltpu.VMEM((total, width), BF),
            pltpu.VMEM((node_count, width), BF),
            sems(8 + 5 * span),
        ],
        2 * 10**9,
        6 * 2**20,
    )(info, layer_nodes, layer_edges, own_index, *pieces, w_send, w_recv, w_edge, w_msg)

    swap = [(worker(m, h), worker(m, 1 - h)) for m, h in works]
    part_other = move(part, every, swap)
    node_pack = call(
        functools.partial(node_kernel, span, batches),
        "node_forward",
        [SMEM] + [VMEM] * 5,
        like(3 * node_count),
        VMEM,
        [],
        3 * 10**8,
        3 * 2**20,
    )(info, layer_nodes, part, part_other, w_node, w_agg)

    pay = keep = None
    incoming = None
    for moment in range(sections):
        first = moment == 0
        inputs = (top_nodes, top_edges, *tops) if first else (*incoming, pay, keep)
        pay, part, keep = call(
            functools.partial(chain_kernel, span, batches, count, None if first else sections - 1 - moment),
            "chain",
            [SMEM] + [ANY] * (len(inputs) + 10),
            [like(total + node_count), like(node_count), like(2 * total + 4 * node_count)],
            [ANY] * 3,
            [
                pltpu.VMEM((node_count, width), BF),
                pltpu.VMEM((node_count, width), BF),
                pltpu.VMEM((total + node_count, width), BF),
                pltpu.VMEM((span, PAD, width), BF),
                pltpu.VMEM((total, width), BF),
                pltpu.VMEM((node_count, width), BF),
                pltpu.VMEM((7, width, width), BF),
                pltpu.VMEM((2 * node_count, total), BF),
                pltpu.VMEM((2 * total + 4 * node_count, width), BF),
                sems(16 + 3 * span),
            ],
            3 * 10**9,
            10 * 2**20,
            {} if first else {3: 0, 4: 2},
        )(info, *inputs, index, slope, node_pack, w_out, w_agg, w_msg, w_edge, w_node, w_send, w_recv)
        if moment < sections - 1:
            here = [sections - 1 - moment]
            cross = move(part, here, swap, -1)
            came = move(pay, here, [(worker(m, h), worker(m, h)) for m, h in works], -1)
            incoming = (came, cross)

    rows = 5 * share + share // 2 + node_share
    out = call(
        functools.partial(grads_kernel, span, batches, groups),
        "weight_grads",
        [SMEM] + [ANY] * (span + 5),
        [like(rows)] * groups + [like(count)] * span,
        [ANY] * (groups + span),
        [
            pltpu.VMEM((node_count, width), BF),
            pltpu.VMEM((span, count, width), BF),
            pltpu.VMEM((total, width), BF),
            pltpu.VMEM((3 * node_count, width), BF),
            pltpu.VMEM((2 * total + 4 * node_count, width), BF),
            pltpu.VMEM((node_count, width), BF),
            pltpu.VMEM((6, width, width), BF),
            sems(5 + 2 * span + 7 * groups),
        ],
        2 * 10**9,
        10 * 2**20,
    )(info, layer_nodes, layer_edges, *pieces, act, node_pack, keep, pay)
    blocks, returns = out[:groups], out[groups:]
    blocks = [blocks[0]] + [
        move(blocks[step], every, [(worker(m, h), (worker(m, h) + step) % groups) for m, h in works])
        for step in range(1, groups)
    ]
    returns = [returns[0]] + [move(returns[step], every, deliver[step]) for step in range(1, span)]
    grad_shape = jax.ShapeDtypeStruct((1, share, width), F32)
    return call(
        functools.partial(finish_kernel, span, batches, groups),
        "finish",
        [SMEM] + [ANY] * (groups + span),
        [
            jax.ShapeDtypeStruct((1, batches, node_share, width), BF),
            jax.ShapeDtypeStruct((1, batches, count, width), BF),
        ]
        + [grad_shape] * 7,
        [VMEM, ANY] + [VMEM] * 7,
        [pltpu.VMEM((batches, PARTS, rows, width), BF), sems(batches + batches * PARTS)],
        0,
        5 * 2**20,
    )(info, *blocks, *returns)


def solution(mesh):
    in_specs = (
        P("section", None, None, None),
        P("section", None, "edge", None),
        P(),
        P(None, "edge", None),
        P(None, "edge", None),
        P(None, "edge"),
        P(None, "edge"),
        P("section", None, None),
        P("section", None, None),
        P("section", None, None),
        P("section", None, None),
        P("section", None, None),
        P("section", None, None),
        P("section", None, None),
    )
    out_specs = (
        P("section", None, "edge", None),
        P("section", None, "edge", None),
        P("section", "edge", None),
        P("section", "edge", None),
        P("section", "edge", None),
        P("section", "edge", None),
        P("section", "edge", None),
        P("section", "edge", None),
        P("section", "edge", None),
    )
    return jax.shard_map(body, mesh=mesh, in_specs=in_specs, out_specs=out_specs, check_vma=False)
```

```python
import functools

import jax
import jax.numpy as jnp
from jax import lax
from jax.experimental import pallas as pl
from jax.experimental.pallas import tpu as pltpu
from jax.sharding import PartitionSpec as P

BLOCK = 128
PARTS = 2
PAD = 16
VMEM_MIB = 32
BF = jnp.bfloat16
F32 = jnp.float32
SMEM = pl.BlockSpec(memory_space=pltpu.SMEM)
VMEM = pl.BlockSpec(memory_space=pltpu.VMEM)


def matmul(left, right):
    return jnp.dot(left, right, preferred_element_type=F32)


def times_transposed(left, right):
    return lax.dot_general(left, right, (((1,), (1,)), ((), ())), preferred_element_type=F32)


def transposed_times(left, right):
    return lax.dot_general(left, right, (((0,), (0,)), ((), ())), preferred_element_type=F32)


def base_of(half, span, batches):
    return jnp.where(half == 0, span - batches, 0)


def place_of(batch, half, span, batches):
    return (span - batches if half == 0 else 0) + batch


def worker_of(batch, half, span, batches):
    return half * span + place_of(batch, half, span, batches)


def own_batch(member, span, batches):
    half = lax.div(member, span)
    batch = lax.rem(member, span) - base_of(half, span, batches)
    return jnp.clip(batch, 0, batches - 1)


def pick_row(table, row, lanes):
    value = table[0:1, lanes]
    for other in range(1, table.shape[0]):
        value = jnp.where(row == other, table[other : other + 1, lanes], value)
    return value


def hot_rows(index_rows, row, nodes):
    index = index_rows[row : row + 1, :].astype(F32).astype(jnp.int32)
    rows = lax.broadcasted_iota(jnp.int32, (nodes, index_rows.shape[1]), 0)
    return jnp.where(rows == index, 1.0, 0.0).astype(BF)


def hot_columns(index_rows, row, nodes):
    pick = lax.broadcasted_iota(jnp.int32, (index_rows.shape[0], nodes), 0) == row
    index = transposed_times(index_rows, jnp.where(pick, 1.0, 0.0).astype(BF))
    columns = lax.broadcasted_iota(jnp.int32, index.shape, 1).astype(F32)
    return jnp.where(columns == index, 1.0, 0.0).astype(BF)


def slope_of(pre, sigma):
    return (sigma * (1.0 + pre * (1.0 - sigma))).astype(BF)


def pack_kernel(span, batches, info, senders, receivers, tiles, edges, *refs):
    index_out = refs[0]
    outs = refs[1:]
    member = info[1]
    half = lax.div(member, span)
    offset = lax.rem(member, span)
    count = senders.shape[1]
    tile_count = tiles.shape[1]
    tile_len = count // tile_count
    for step in range(span):
        batch = lax.rem(offset - step + span, span) - base_of(half, span, batches)
        batch = jnp.clip(batch, 0, batches - 1)
        if step:
            out, start = outs[step - 1], count
            out[:count] = edges[0, batch]
        else:
            out, start = index_out, 0
        out[start : start + PAD] = jnp.zeros((PAD, out.shape[1]), BF)
        for tile in range(tile_count):
            lanes = slice(tile * tile_len, (tile + 1) * tile_len)
            send = pick_row(senders, batch, lanes) + tiles[batch, tile, 0] * BLOCK
            recv = pick_row(receivers, batch, lanes) + tiles[batch, tile, 1] * BLOCK
            which = lax.broadcasted_iota(jnp.int32, (PAD, tile_len), 0)
            block = jnp.where(which == 0, send, jnp.where(which == 1, recv, 0))
            out[start : start + PAD, lanes] = block.astype(F32).astype(BF)


def ready_kernel(span, batches, info, nodes, w_send, w_recv, w_node, *refs):
    w_edge, w_msg, w_agg, w_out = refs[:4]
    turned, plain, hidden, node_pre, feats_turned = refs[4:]
    batch = own_batch(info[1], span, batches)
    node_count = nodes.shape[2]
    feats = nodes[0, batch]
    hidden[:node_count] = matmul(feats, w_send[0]).astype(BF)
    hidden[node_count:] = matmul(feats, w_recv[0]).astype(BF)
    node_pre[...] = matmul(feats, w_node[0])
    feats_turned[...] = feats.T
    for slot, weight in enumerate((w_edge, w_msg, w_agg)):
        plain[slot] = weight[0]
    for slot, weight in enumerate((w_out, w_agg, w_msg, w_edge, w_node, w_send, w_recv)):
        turned[slot] = weight[0].T


def forward_kernel(span, batches, chunk, info, edges, own_index, *refs):
    others = refs[: span - 1]
    hidden, plain = refs[span - 1 : span + 1]
    act_out, slope_out, part_out, hot_out, hots_out, pieces, both = refs[span + 1 :]
    batch = own_batch(info[1], span, batches)
    count = edges.shape[2]
    node_count = part_out.shape[0]
    for step in range(span):
        run = slice(step * count, (step + 1) * count)
        if step:
            pieces[run] = others[step - 1][:count]
            index_rows = others[step - 1][count : count + PAD, :count]
        else:
            pieces[run] = edges[0, batch]
            index_rows = own_index[:, :count]
        hots_out[:node_count, run] = hot_rows(index_rows, 0, node_count)
        hots_out[node_count:, run] = hot_rows(index_rows, 1, node_count)
        both[run, :node_count] = hot_columns(index_rows, 0, node_count)
        recv_hot = hot_columns(index_rows, 1, node_count)
        both[run, node_count:] = recv_hot
        hot_out[run] = recv_hot
    for at in range(0, span * count, chunk):
        run = slice(at, at + chunk)
        pre = matmul(both[run], hidden[...]) + matmul(pieces[run], plain[0])
        sigma = jax.nn.sigmoid(pre)
        act_out[run] = (pre * sigma).astype(BF)
        slope_out[run] = slope_of(pre, sigma)
    total = matmul(hots_out[node_count:], act_out[...])
    part_out[...] = matmul(total.astype(BF), plain[1]).astype(BF)


def turn_kernel(span, batches, info, edges, act, *refs):
    others = refs[: span - 1]
    edges_turned, act_turned = refs[span - 1 :]
    batch = own_batch(info[1], span, batches)
    count = edges.shape[2]
    for step in range(span):
        run = slice(step * count, (step + 1) * count)
        piece = others[step - 1][:count] if step else edges[0, batch]
        edges_turned[:, run] = piece.T
        act_turned[:, run] = act[run].T


def node_kernel(node_pre, part_own, part_other, plain, turned_first, out):
    count = part_own.shape[0]
    agg = (part_own[...].astype(F32) + part_other[...].astype(F32)).astype(BF)
    pre = node_pre[...] + matmul(agg, plain[2])
    sigma = jax.nn.sigmoid(pre)
    out[:count] = agg
    out[count : 2 * count] = (pre * sigma).astype(BF)
    out[2 * count :] = slope_of(pre, sigma)


def chain_kernel(span, batches, chunk, first, active, info, *refs):
    if active is None:
        chain_step(span, batches, chunk, first, info, *refs)
        return
    kept = None
    if len(refs) == 12:
        kept = refs[2:4]
        refs = refs[:2] + refs[4:]

    @pl.when(info[0] == active)
    def _():
        chain_step(span, batches, chunk, first, info, *refs)

    if kept is not None:

        @pl.when(info[0] != active)
        def _():
            refs[-3][...] = kept[0][...]
            refs[-1][...] = kept[1][...]


def chain_step(span, batches, chunk, first, info, *refs):
    member = info[1]
    batch = own_batch(member, span, batches)
    half = lax.div(member, span)
    if first:
        top_nodes, top_edges = refs[:2]
        others = refs[2 : span + 1]
        hot, hots, slope, node_pack, turned, pay, part_out, keep, came = refs[span + 1 :]
        count = top_edges.shape[1]
        for step in range(span):
            came[step * count : (step + 1) * count] = others[step - 1][...] if step else top_edges[batch]
        grad = top_nodes[batch]
    else:
        came, cross = refs[:2]
        hot, hots, slope, node_pack, turned, pay, part_out, keep = refs[2:]
        total = slope.shape[0]
        grad = (came[total:].astype(F32) + cross[...].astype(F32)).astype(BF)
    total = slope.shape[0]
    node_count = part_out.shape[0]
    node_at = 2 * total
    delta = (matmul(grad, turned[0]) * node_pack[2 * node_count :].astype(F32)).astype(BF)
    agg_grad = matmul(delta, turned[1]).astype(BF)
    keep[node_at : node_at + node_count] = delta
    keep[node_at + node_count : node_at + 2 * node_count] = grad
    for at in range(0, total, chunk):
        run = slice(at, at + chunk)
        incoming = came[run].astype(F32)
        message_grad = (incoming + matmul(hot[run], agg_grad)).astype(BF)
        keep[run] = message_grad
        edge_delta = (matmul(message_grad, turned[2]) * slope[run].astype(F32)).astype(BF)
        keep[total + at : total + at + chunk] = edge_delta
        pay[run] = (incoming + matmul(edge_delta, turned[3])).astype(BF)
    sums = matmul(hots[...], keep[total : 2 * total]).astype(BF)
    keep[node_at + 2 * node_count :] = sums
    own = grad.astype(F32) + matmul(delta, turned[4])
    own = own * jnp.where(half == 0, 1.0, 0.0)
    part = matmul(sums[:node_count], turned[5]) + matmul(sums[node_count:], turned[6])
    part = (own + part).astype(BF)
    pay[total:] = part
    part_out[...] = part


def grads_kernel(span, groups, low, high, info, *refs):
    section = info[0]

    @pl.when((section >= low) & (section < high))
    def _():
        grads_step(span, groups, info, *refs)


def grads_step(span, groups, info, edges_turned, act_turned, feats_turned, node_pack, keep, pay, *refs):
    blocks = refs[:groups]
    returns = refs[groups : groups + span]
    sums = refs[groups + span]
    member = info[1]
    half = lax.div(member, span)
    total = edges_turned.shape[1]
    node_count = feats_turned.shape[1]
    width = feats_turned.shape[0]
    count = total // span
    node_at = 2 * total
    delta = keep[node_at : node_at + node_count]
    grad = keep[node_at + node_count : node_at + 2 * node_count]
    sums[0] = matmul(feats_turned[...], keep[node_at + 2 * node_count : node_at + 3 * node_count]).astype(BF)
    sums[1] = matmul(feats_turned[...], keep[node_at + 3 * node_count :]).astype(BF)
    sums[2] = matmul(edges_turned[...], keep[total : 2 * total]).astype(BF)
    sums[3] = matmul(act_turned[...], keep[:total]).astype(BF)
    sums[5] = transposed_times(node_pack[:node_count], delta).astype(BF)

    @pl.when(half == 0)
    def _():
        sums[4] = matmul(feats_turned[...], delta).astype(BF)

    @pl.when(half != 0)
    def _():
        sums[4] = transposed_times(node_pack[node_count : 2 * node_count], grad).astype(BF)

    for step in range(span):
        returns[step][...] = pay[step * count : (step + 1) * count]
    share = width // groups
    node_share = node_count // groups
    for step in range(groups):
        owner = lax.rem(member + step, groups)
        at = pl.multiple_of(owner * share, share)
        block = blocks[step]
        for slot in range(5):
            block[slot * share : (slot + 1) * share] = sums[slot, pl.ds(at, share)]
        at_half = pl.multiple_of(owner * share + half * (share // 2), share // 2)
        block[5 * share : 5 * share + share // 2] = sums[5, pl.ds(at_half, share // 2)]
        at_node = pl.multiple_of(total + owner * node_share, node_share)
        block[5 * share + share // 2 :] = pay[pl.ds(at_node, node_share)]


def finish_kernel(span, batches, groups, info, *refs):
    per_set = groups + span
    sets = (refs[:per_set], refs[per_set : 2 * per_set])
    refs = refs[2 * per_set :]
    nodes_out, edges_out, send_out, recv_out, edge_out, msg_out, node_out, agg_out, out_out = refs[:9]
    held = refs[9]
    section = info[0]
    member = info[1]
    half = lax.div(member, span)
    offset = lax.rem(member, span)
    for which in range(2):

        @pl.when((section == 0) == (which == 1))
        def _(which=which):
            blocks, returns = sets[which][:groups], sets[which][groups:]
            for batch in range(batches):
                turn = lax.rem(offset - base_of(half, span, batches) - batch + 2 * span, span)
                for step in range(span):

                    @pl.when(turn == step)
                    def _(step=step):
                        edges_out[0, batch] = returns[step][...]

                for part in range(PARTS):
                    turn_b = lax.rem(member - worker_of(batch, part, span, batches) + groups, groups)
                    for step in range(groups):

                        @pl.when(turn_b == step)
                        def _(step=step, part=part):
                            held[batch, part] = blocks[step][...]

    share = send_out.shape[1]
    for slot, out in enumerate((send_out, recv_out, edge_out, msg_out)):
        rows = slice(slot * share, (slot + 1) * share)
        value = None
        for batch in range(batches):
            for part in range(PARTS):
                piece = held[batch, part, rows].astype(F32)
                value = piece if value is None else value + piece
        out[0] = value

    def over_batches(part, start, length):
        value = None
        for batch in range(batches):
            piece = held[batch, part, start : start + length].astype(F32)
            value = piece if value is None else value + piece
        return value

    node_out[0] = over_batches(0, 4 * share, share)
    out_out[0] = over_batches(1, 4 * share, share)
    for part in range(PARTS):
        agg_out[0, part * (share // 2) : (part + 1) * (share // 2)] = over_batches(part, 5 * share, share // 2)
    at = 5 * share + share // 2
    for batch in range(batches):
        rows = held[batch, 0, at:].astype(F32) + held[batch, 1, at:].astype(F32)
        nodes_out[0, batch] = rows.astype(BF)


def call(kernel, name, in_specs, out_shapes, scratch, flops, touched, aliases={}):
    many = isinstance(out_shapes, list)
    return pl.pallas_call(
        kernel,
        name=name,
        out_shape=out_shapes,
        in_specs=in_specs,
        out_specs=[VMEM] * len(out_shapes) if many else VMEM,
        scratch_shapes=scratch,
        input_output_aliases=aliases,
        compiler_params=pltpu.CompilerParams(vmem_limit_bytes=VMEM_MIB * 1024 * 1024),
        cost_estimate=pl.CostEstimate(flops=flops, bytes_accessed=touched, transcendentals=0),
    )


def body(
    layer_nodes,
    layer_edges,
    top_nodes,
    top_edges,
    tile_blocks,
    senders,
    receivers,
    w_send,
    w_recv,
    w_edge,
    w_msg,
    w_node,
    w_agg,
    w_out,
):
    sections = lax.axis_size("section")
    groups = lax.axis_size("edge")
    section = lax.axis_index("section")
    member = lax.axis_index("edge")
    span = groups // PARTS
    _, batches, node_count, width = layer_nodes.shape
    count = layer_edges.shape[2]
    total = span * count
    chunk = 2 * count
    share = width // groups
    node_share = node_count // groups
    info = jnp.stack([section, member]).astype(jnp.int32)
    axes = ("section", "edge")
    works = [(m, h) for h in range(PARTS) for m in range(batches)]

    def worker(m, h):
        return worker_of(m, h, span, batches)

    def source(m, h, step):
        return h * span + (place_of(m, h, span, batches) + step) % span

    def move(value, layers, links, shift=0):
        pairs = [(s * groups + a, (s + shift) * groups + b) for s in layers for a, b in links]
        return lax.ppermute(value, axes, pairs)

    every = list(range(sections))
    last = [sections - 1]
    collect = [[(source(m, h, step), worker(m, h)) for m, h in works] for step in range(span)]
    deliver = [[(b, a) for a, b in links] for links in collect]

    def like(rows, cols=width, kind=BF):
        return jax.ShapeDtypeStruct((rows, cols), kind)

    packed = call(
        functools.partial(pack_kernel, span, batches),
        "pack",
        [SMEM, VMEM, VMEM, SMEM, VMEM],
        [like(PAD)] + [like(count + PAD)] * (span - 1),
        [],
        0,
        2**20,
    )(info, senders, receivers, tile_blocks, layer_edges)
    own_index, pieces = packed[0], packed[1:]
    pieces = [move(piece, every, collect[step + 1]) for step, piece in enumerate(pieces)]
    half = member // span
    offset = member % span
    tops = []
    for step in range(1, span):
        pick = jnp.clip((offset - step) % span - base_of(half, span, batches), 0, batches - 1)
        tops.append(move(lax.dynamic_index_in_dim(top_edges, pick, 0, keepdims=False), last, collect[step]))

    turned, plain, hidden, node_pre, feats_turned = call(
        functools.partial(ready_kernel, span, batches),
        "ready",
        [SMEM] + [VMEM] * 8,
        [
            jax.ShapeDtypeStruct((7, width, width), BF),
            jax.ShapeDtypeStruct((3, width, width), BF),
            like(2 * node_count),
            like(node_count, kind=F32),
            like(width, node_count),
        ],
        [],
        4 * 10**8,
        10 * 2**20,
    )(info, layer_nodes, w_send, w_recv, w_node, w_edge, w_msg, w_agg, w_out)

    act, slope, part, hot, hots = call(
        functools.partial(forward_kernel, span, batches, chunk),
        "forward",
        [SMEM] + [VMEM] * (span + 3),
        [like(total), like(total), like(node_count), like(total, node_count), like(2 * node_count, total)],
        [pltpu.VMEM((total, width), BF), pltpu.VMEM((total, 2 * node_count), BF)],
        2 * 10**9,
        6 * 2**20,
    )(info, layer_edges, own_index, *pieces, hidden, plain)

    swap = [(worker(m, h), worker(m, 1 - h)) for m, h in works]
    part_other = move(part, every, swap)
    edges_turned, act_turned = call(
        functools.partial(turn_kernel, span, batches),
        "turn",
        [SMEM] + [VMEM] * (span + 1),
        [like(width, total), like(width, total)],
        [],
        0,
        4 * 2**20,
    )(info, layer_edges, act, *pieces)
    node_pack = call(
        node_kernel,
        "node_forward",
        [VMEM] * 4 + [pl.BlockSpec(memory_space=pl.ANY)],
        like(3 * node_count),
        [],
        10**5,
        2**10,
    )(node_pre, part, part_other, plain, edges_turned)

    kept = [like(total + node_count), like(node_count), like(2 * total + 4 * node_count)]
    both_ways = [(worker(m, h), worker(m, h)) for m, h in works]
    rows = 5 * share + share // 2 + node_share
    pay = keep = None
    incoming = None
    sets = []

    def weight_grads(low, high, keep, pay):
        out = call(
            functools.partial(grads_kernel, span, groups, low, high),
            "weight_grads",
            [SMEM] + [VMEM] * 6,
            [like(rows)] * groups + [like(count)] * span,
            [pltpu.VMEM((6, width, width), BF)],
            2 * 10**9,
            10 * 2**20,
        )(info, edges_turned, act_turned, feats_turned, node_pack, keep, pay)
        blocks, returns = out[:groups], out[groups:]
        layers = list(range(low, high))
        blocks = [blocks[0]] + [
            move(blocks[step], layers, [(worker(m, h), (worker(m, h) + step) % groups) for m, h in works])
            for step in range(1, groups)
        ]
        returns = [returns[0]] + [move(returns[step], layers, deliver[step]) for step in range(1, span)]
        return blocks + returns

    for moment in range(sections):
        first = moment == 0
        layer = sections - 1 - moment
        in_place = 0 < moment < sections - 1
        if first:
            inputs = (top_nodes, top_edges, *tops)
        elif in_place:
            inputs = (*incoming, pay, keep)
        else:
            inputs = incoming
        pay, part, keep = call(
            functools.partial(chain_kernel, span, batches, chunk, first, None if first else layer),
            "chain",
            [SMEM] + [VMEM] * (len(inputs) + 5),
            kept,
            [pltpu.VMEM((total, width), BF)] if first else [],
            3 * 10**9,
            10 * 2**20,
            {3: 0, 4: 2} if in_place else {},
        )(info, *inputs, hot, hots, slope, node_pack, turned)
        if layer > 0:
            cross = move(part, [layer], swap, -1)
            came = move(pay, [layer], both_ways, -1)
            incoming = (came, cross)
        if layer <= 1:
            sets.append(weight_grads(layer, sections if layer == 1 else 1, keep, pay))

    grad_shape = jax.ShapeDtypeStruct((1, share, width), F32)
    return call(
        functools.partial(finish_kernel, span, batches, groups),
        "finish",
        [SMEM] + [VMEM] * (2 * (groups + span)),
        [
            jax.ShapeDtypeStruct((1, batches, node_share, width), BF),
            jax.ShapeDtypeStruct((1, batches, count, width), BF),
        ]
        + [grad_shape] * 7,
        [pltpu.VMEM((batches, PARTS, rows, width), BF)],
        0,
        5 * 2**20,
    )(info, *sets[0], *sets[1])


def solution(mesh):
    in_specs = (
        P("section", None, None, None),
        P("section", None, "edge", None),
        P(),
        P(None, "edge", None),
        P(None, "edge", None),
        P(None, "edge"),
        P(None, "edge"),
        P("section", None, None),
        P("section", None, None),
        P("section", None, None),
        P("section", None, None),
        P("section", None, None),
        P("section", None, None),
        P("section", None, None),
    )
    out_specs = (
        P("section", None, "edge", None),
        P("section", None, "edge", None),
        P("section", "edge", None),
        P("section", "edge", None),
        P("section", "edge", None),
        P("section", "edge", None),
        P("section", "edge", None),
        P("section", "edge", None),
        P("section", "edge", None),
    )
    return jax.shard_map(body, mesh=mesh, in_specs=in_specs, out_specs=out_specs, check_vma=False)
```

```python
import functools

import jax
import jax.numpy as jnp
from jax import lax
from jax.experimental import pallas as pl
from jax.experimental.pallas import tpu as pltpu
from jax.sharding import PartitionSpec as P

BLOCK = 128
PARTS = 2
PAD = 16
GRANT = 32
BF = jnp.bfloat16
F32 = jnp.float32
ANY = pl.BlockSpec(memory_space=pl.ANY)
SMEM = pl.BlockSpec(memory_space=pltpu.SMEM)
VMEM = pl.BlockSpec(memory_space=pltpu.VMEM)


def matmul(left, right):
    return jnp.dot(left, right, preferred_element_type=F32)


def times_transposed(left, right):
    return lax.dot_general(left, right, (((1,), (1,)), ((), ())), preferred_element_type=F32)


def transposed_times(left, right):
    return lax.dot_general(left, right, (((0,), (0,)), ((), ())), preferred_element_type=F32)


def base_of(half, span, batches):
    return jnp.where(half == 0, span - batches, 0)


def place_of(batch, half, span, batches):
    return (span - batches if half == 0 else 0) + batch


def worker_of(batch, half, span, batches):
    return half * span + place_of(batch, half, span, batches)


def own_batch(member, span, batches):
    half = lax.div(member, span)
    batch = lax.rem(member, span) - base_of(half, span, batches)
    return jnp.clip(batch, 0, batches - 1)


def pick_row(table, row, lanes):
    value = table[0:1, lanes]
    for other in range(1, table.shape[0]):
        value = jnp.where(row == other, table[other : other + 1, lanes], value)
    return value


def hot_rows(index_rows, row, nodes):
    index = index_rows[row : row + 1, :].astype(F32).astype(jnp.int32)
    rows = lax.broadcasted_iota(jnp.int32, (nodes, index_rows.shape[1]), 0)
    return jnp.where(rows == index, 1.0, 0.0).astype(BF)


def hot_columns(index_rows, row, nodes):
    pick = lax.broadcasted_iota(jnp.int32, (index_rows.shape[0], nodes), 0) == row
    index = transposed_times(index_rows, jnp.where(pick, 1.0, 0.0).astype(BF))
    columns = lax.broadcasted_iota(jnp.int32, index.shape, 1).astype(F32)
    return jnp.where(columns == index, 1.0, 0.0).astype(BF)


def slope_of(pre, sigma):
    return (sigma * (1.0 + pre * (1.0 - sigma))).astype(BF)


def pack_kernel(span, batches, info, senders, receivers, tiles, edges, *refs):
    index_out = refs[0]
    outs = refs[1:span]
    send_in, recv_in, rows, sems = refs[span:]
    member = info[1]
    half = lax.div(member, span)
    offset = lax.rem(member, span)
    count = senders.shape[1]
    tile_count = tiles.shape[1]
    tile_len = count // tile_count
    gets = [
        pltpu.make_async_copy(senders, send_in, sems.at[0]),
        pltpu.make_async_copy(receivers, recv_in, sems.at[1]),
    ]
    picks, puts = [], []
    for step in range(span):
        batch = lax.rem(offset - step + span, span) - base_of(half, span, batches)
        picks.append(jnp.clip(batch, 0, batches - 1))
        if step:
            puts.append(
                pltpu.make_async_copy(
                    edges.at[0, picks[step]], outs[step - 1].at[pl.ds(0, count)], sems.at[1 + step]
                )
            )
    for copy in gets + puts:
        copy.start()
    for copy in gets:
        copy.wait()
    rows[...] = jnp.zeros_like(rows)
    for step in range(span):
        batch = picks[step]
        for tile in range(tile_count):
            lanes = slice(tile * tile_len, (tile + 1) * tile_len)
            send = pick_row(send_in, batch, lanes) + tiles[batch, tile, 0] * BLOCK
            recv = pick_row(recv_in, batch, lanes) + tiles[batch, tile, 1] * BLOCK
            which = lax.broadcasted_iota(jnp.int32, (PAD, tile_len), 0)
            block = jnp.where(which == 0, send, jnp.where(which == 1, recv, 0))
            rows[step, :, lanes] = block.astype(F32).astype(BF)
        target = outs[step - 1].at[pl.ds(count, PAD)] if step else index_out
        copy = pltpu.make_async_copy(rows.at[step], target, sems.at[1 + span + step])
        copy.start()
        puts.append(copy)
    for copy in puts:
        copy.wait()


def ready_kernel(span, batches, info, nodes, w_send, w_recv, w_node, *refs):
    w_edge, w_msg, w_agg, w_out = refs[:4]
    turned, plain, hidden, node_pre, feats_turned = refs[4:]
    batch = own_batch(info[1], span, batches)
    node_count = nodes.shape[2]
    feats = nodes[0, batch]
    hidden[:node_count] = matmul(feats, w_send[0]).astype(BF)
    hidden[node_count:] = matmul(feats, w_recv[0]).astype(BF)
    node_pre[...] = matmul(feats, w_node[0])
    feats_turned[...] = feats.T
    for slot, weight in enumerate((w_edge, w_msg, w_agg)):
        plain[slot] = weight[0]
    for slot, weight in enumerate((w_out, w_agg, w_msg, w_edge, w_node, w_send, w_recv)):
        turned[slot] = weight[0].T


def forward_kernel(span, batches, chunk, info, edges, own_index, *refs):
    others = refs[: span - 1]
    hidden, plain = refs[span - 1 : span + 1]
    act_out, slope_out, part_out, hot_out, hots_out, pieces, both = refs[span + 1 :]
    batch = own_batch(info[1], span, batches)
    count = edges.shape[2]
    node_count = part_out.shape[0]
    for step in range(span):
        run = slice(step * count, (step + 1) * count)
        if step:
            pieces[run] = others[step - 1][:count]
            index_rows = others[step - 1][count : count + PAD, :count]
        else:
            pieces[run] = edges[0, batch]
            index_rows = own_index[:, :count]
        hots_out[:node_count, run] = hot_rows(index_rows, 0, node_count)
        hots_out[node_count:, run] = hot_rows(index_rows, 1, node_count)
        both[run, :node_count] = hot_columns(index_rows, 0, node_count)
        recv_hot = hot_columns(index_rows, 1, node_count)
        both[run, node_count:] = recv_hot
        hot_out[run] = recv_hot
    for at in range(0, span * count, chunk):
        run = slice(at, at + chunk)
        pre = matmul(both[run], hidden[...]) + matmul(pieces[run], plain[0])
        sigma = jax.nn.sigmoid(pre)
        act_out[run] = (pre * sigma).astype(BF)
        slope_out[run] = slope_of(pre, sigma)
    total = matmul(hots_out[node_count:], act_out[...])
    part_out[...] = matmul(total.astype(BF), plain[1]).astype(BF)


def turn_kernel(span, batches, info, edges, act, *refs):
    others = refs[: span - 1]
    edges_turned, act_turned = refs[span - 1 :]
    batch = own_batch(info[1], span, batches)
    count = edges.shape[2]
    for step in range(span):
        run = slice(step * count, (step + 1) * count)
        piece = others[step - 1][:count] if step else edges[0, batch]
        edges_turned[:, run] = piece.T
        act_turned[:, run] = act[run].T


def node_kernel(node_pre, part_own, part_other, plain, turned_first, out):
    count = part_own.shape[0]
    agg = (part_own[...].astype(F32) + part_other[...].astype(F32)).astype(BF)
    pre = node_pre[...] + matmul(agg, plain[2])
    sigma = jax.nn.sigmoid(pre)
    out[:count] = agg
    out[count : 2 * count] = (pre * sigma).astype(BF)
    out[2 * count :] = slope_of(pre, sigma)


def chain_kernel(span, batches, chunk, first, active, info, *refs):
    kept = None
    if not first and len(refs) == 12:
        kept = refs[2:4]
        refs = refs[:2] + refs[4:]

    @pl.when(info[0] == active)
    def _():
        chain_step(span, batches, chunk, first, info, *refs)

    if kept is not None:

        @pl.when(info[0] != active)
        def _():
            refs[-3][...] = kept[0][...]
            refs[-1][...] = kept[1][...]


def chain_step(span, batches, chunk, first, info, *refs):
    member = info[1]
    batch = own_batch(member, span, batches)
    half = lax.div(member, span)
    if first:
        top_nodes, top_edges = refs[:2]
        others = refs[2 : span + 1]
        hot, hots, slope, node_pack, turned, pay, part_out, keep, came = refs[span + 1 :]
        count = top_edges.shape[1]
        for step in range(span):
            came[step * count : (step + 1) * count] = others[step - 1][...] if step else top_edges[batch]
        grad = top_nodes[batch]
    else:
        came, cross = refs[:2]
        hot, hots, slope, node_pack, turned, pay, part_out, keep = refs[2:]
        total = slope.shape[0]
        grad = (came[total:].astype(F32) + cross[...].astype(F32)).astype(BF)
    total = slope.shape[0]
    node_count = part_out.shape[0]
    node_at = 2 * total
    delta = (matmul(grad, turned[0]) * node_pack[2 * node_count :].astype(F32)).astype(BF)
    agg_grad = matmul(delta, turned[1]).astype(BF)
    keep[node_at : node_at + node_count] = delta
    keep[node_at + node_count : node_at + 2 * node_count] = grad
    for at in range(0, total, chunk):
        run = slice(at, at + chunk)
        incoming = came[run].astype(F32)
        message_grad = (incoming + matmul(hot[run], agg_grad)).astype(BF)
        keep[run] = message_grad
        edge_delta = (matmul(message_grad, turned[2]) * slope[run].astype(F32)).astype(BF)
        keep[total + at : total + at + chunk] = edge_delta
        pay[run] = (incoming + matmul(edge_delta, turned[3])).astype(BF)
    sums = matmul(hots[...], keep[total : 2 * total]).astype(BF)
    keep[node_at + 2 * node_count :] = sums
    own = grad.astype(F32) + matmul(delta, turned[4])
    own = own * jnp.where(half == 0, 1.0, 0.0)
    part = matmul(sums[:node_count], turned[5]) + matmul(sums[node_count:], turned[6])
    part = (own + part).astype(BF)
    pay[total:] = part
    part_out[...] = part


def grads_kernel(span, batches, groups, info, edges_turned, act_turned, feats_turned, node_pack, keep, pay, *refs):
    near, far = refs[:span], refs[span : 2 * span]
    sums = refs[2 * span]
    member = info[1]
    half = lax.div(member, span)
    offset = lax.rem(member, span)
    batch = own_batch(member, span, batches)
    total = edges_turned.shape[1]
    node_count = feats_turned.shape[1]
    width = feats_turned.shape[0]
    count = total // span
    node_at = 2 * total
    delta = keep[node_at : node_at + node_count]
    grad = keep[node_at + node_count : node_at + 2 * node_count]
    sums[0] = matmul(feats_turned[...], keep[node_at + 2 * node_count : node_at + 3 * node_count]).astype(BF)
    sums[1] = matmul(feats_turned[...], keep[node_at + 3 * node_count :]).astype(BF)
    sums[2] = matmul(edges_turned[...], keep[total : 2 * total]).astype(BF)
    sums[3] = matmul(act_turned[...], keep[:total]).astype(BF)
    sums[5] = transposed_times(node_pack[:node_count], delta).astype(BF)

    @pl.when(half == 0)
    def _():
        sums[4] = matmul(feats_turned[...], delta).astype(BF)

    @pl.when(half != 0)
    def _():
        sums[4] = transposed_times(node_pack[node_count : 2 * node_count], grad).astype(BF)

    share = width // groups
    node_share = node_count // groups

    def fill(block, start, owner):
        at = pl.multiple_of(owner * share, share)
        for slot in range(5):
            block[start + slot * share : start + (slot + 1) * share] = sums[slot, pl.ds(at, share)]
        at_half = pl.multiple_of(owner * share + half * (share // 2), share // 2)
        block[start + 5 * share : start + 5 * share + share // 2] = sums[5, pl.ds(at_half, share // 2)]
        at_node = pl.multiple_of(total + owner * node_share, node_share)
        block[start + 5 * share + share // 2 :] = pay[pl.ds(at_node, node_share)]

    for step in range(span):
        near[step][:count] = pay[step * count : (step + 1) * count]
        fill(near[step], count, half * span + lax.rem(offset + step, span))
        fill(far[step], 0, (1 - half) * span + lax.rem(batch + step, span))


def finish_kernel(span, batches, groups, info, *refs):
    near, far = refs[:span], refs[span : 2 * span]
    refs = refs[2 * span :]
    nodes_out, edges_out, send_out, recv_out, edge_out, msg_out, node_out, agg_out, out_out = refs[:9]
    held = refs[9]
    member = info[1]
    half = lax.div(member, span)
    offset = lax.rem(member, span)
    count = edges_out.shape[2]
    for batch in range(batches):
        turn = lax.rem(offset - base_of(half, span, batches) - batch + 2 * span, span)
        turn_far = lax.rem(offset - batch + span, span)
        for step in range(span):

            @pl.when(turn == step)
            def _(step=step, batch=batch):
                edges_out[0, batch] = near[step][:count]
                held[batch, half] = near[step][count:]

            @pl.when(turn_far == step)
            def _(step=step, batch=batch):
                held[batch, 1 - half] = far[step][...]

    share = send_out.shape[1]
    for slot, out in enumerate((send_out, recv_out, edge_out, msg_out)):
        rows = slice(slot * share, (slot + 1) * share)
        value = None
        for batch in range(batches):
            for part in range(PARTS):
                piece = held[batch, part, rows].astype(F32)
                value = piece if value is None else value + piece
        out[0] = value

    def over_batches(part, start, length):
        value = None
        for batch in range(batches):
            piece = held[batch, part, start : start + length].astype(F32)
            value = piece if value is None else value + piece
        return value

    node_out[0] = over_batches(0, 4 * share, share)
    out_out[0] = over_batches(1, 4 * share, share)
    for part in range(PARTS):
        agg_out[0, part * (share // 2) : (part + 1) * (share // 2)] = over_batches(part, 5 * share, share // 2)
    at = 5 * share + share // 2
    for batch in range(batches):
        rows = held[batch, 0, at:].astype(F32) + held[batch, 1, at:].astype(F32)
        nodes_out[0, batch] = rows.astype(BF)


def call(kernel, name, in_specs, out_shapes, scratch, flops, touched, aliases={}, grant=GRANT, out_spec=VMEM):
    many = isinstance(out_shapes, list)
    return pl.pallas_call(
        kernel,
        name=name,
        out_shape=out_shapes,
        in_specs=in_specs,
        out_specs=[out_spec] * len(out_shapes) if many else out_spec,
        scratch_shapes=scratch,
        input_output_aliases=aliases,
        compiler_params=pltpu.CompilerParams(vmem_limit_bytes=grant * 2**20),
        cost_estimate=pl.CostEstimate(flops=flops, bytes_accessed=touched, transcendentals=0),
    )


def body(
    layer_nodes,
    layer_edges,
    top_nodes,
    top_edges,
    tile_blocks,
    senders,
    receivers,
    w_send,
    w_recv,
    w_edge,
    w_msg,
    w_node,
    w_agg,
    w_out,
):
    sections = lax.axis_size("section")
    groups = lax.axis_size("edge")
    section = lax.axis_index("section")
    member = lax.axis_index("edge")
    span = groups // PARTS
    _, batches, node_count, width = layer_nodes.shape
    count = layer_edges.shape[2]
    total = span * count
    chunk = 2 * count
    share = width // groups
    node_share = node_count // groups
    info = jnp.stack([section, member]).astype(jnp.int32)
    axes = ("section", "edge")
    works = [(m, h) for h in range(PARTS) for m in range(batches)]

    def worker(m, h):
        return worker_of(m, h, span, batches)

    def source(m, h, step):
        return h * span + (place_of(m, h, span, batches) + step) % span

    def move(value, layers, links, shift=0):
        pairs = [(s * groups + a, (s + shift) * groups + b) for s in layers for a, b in links]
        return lax.ppermute(value, axes, pairs)

    every = list(range(sections))
    last = [sections - 1]
    collect = [[(source(m, h, step), worker(m, h)) for m, h in works] for step in range(span)]
    deliver = [[(b, a) for a, b in links] for links in collect]

    def like(rows, cols=width, kind=BF):
        return jax.ShapeDtypeStruct((rows, cols), kind)

    packed = call(
        functools.partial(pack_kernel, span, batches),
        "pack",
        [SMEM, ANY, ANY, SMEM, ANY],
        [like(PAD)] + [like(count + PAD)] * (span - 1),
        [
            pltpu.VMEM((batches, count), jnp.int32),
            pltpu.VMEM((batches, count), jnp.int32),
            pltpu.VMEM((span, PAD, width), BF),
            pltpu.SemaphoreType.DMA((2 + 2 * span,)),
        ],
        0,
        2**20,
        grant=62,
        out_spec=ANY,
    )(info, senders, receivers, tile_blocks, layer_edges)
    own_index, pieces = packed[0], packed[1:]
    pieces = [move(piece, every, collect[step + 1]) for step, piece in enumerate(pieces)]
    half = member // span
    offset = member % span
    tops = []
    for step in range(1, span):
        pick = jnp.clip((offset - step) % span - base_of(half, span, batches), 0, batches - 1)
        tops.append(move(lax.dynamic_index_in_dim(top_edges, pick, 0, keepdims=False), last, collect[step]))

    turned, plain, hidden, node_pre, feats_turned = call(
        functools.partial(ready_kernel, span, batches),
        "ready",
        [SMEM] + [VMEM] * 8,
        [
            jax.ShapeDtypeStruct((7, width, width), BF),
            jax.ShapeDtypeStruct((3, width, width), BF),
            like(2 * node_count),
            like(node_count, kind=F32),
            like(width, node_count),
        ],
        [],
        4 * 10**8,
        10 * 2**20,
    )(info, layer_nodes, w_send, w_recv, w_node, w_edge, w_msg, w_agg, w_out)

    act, slope, part, hot, hots = call(
        functools.partial(forward_kernel, span, batches, chunk),
        "forward",
        [SMEM] + [VMEM] * (span + 3),
        [like(total), like(total), like(node_count), like(total, node_count), like(2 * node_count, total)],
        [pltpu.VMEM((total, width), BF), pltpu.VMEM((total, 2 * node_count), BF)],
        2 * 10**9,
        6 * 2**20,
    )(info, layer_edges, own_index, *pieces, hidden, plain)

    swap = [(worker(m, h), worker(m, 1 - h)) for m, h in works]
    part_other = move(part, every, swap)
    edges_turned, act_turned = call(
        functools.partial(turn_kernel, span, batches),
        "turn",
        [SMEM] + [VMEM] * (span + 1),
        [like(width, total), like(width, total)],
        [],
        0,
        4 * 2**20,
    )(info, layer_edges, act, *pieces)
    node_pack = call(
        node_kernel,
        "node_forward",
        [VMEM] * 4 + [ANY],
        like(3 * node_count),
        [],
        10**5,
        2**10,
    )(node_pre, part, part_other, plain, edges_turned)

    kept = [like(total + node_count), like(node_count), like(2 * total + 4 * node_count)]
    both_ways = [(worker(m, h), worker(m, h)) for m, h in works]
    rows = 5 * share + share // 2 + node_share
    pay = keep = None
    incoming = None
    for moment in range(sections):
        first = moment == 0
        layer = sections - 1 - moment
        in_place = not first
        if first:
            inputs = (top_nodes, top_edges, *tops)
        else:
            inputs = (*incoming, pay, keep)
        pay, part, keep = call(
            functools.partial(chain_kernel, span, batches, chunk, first, layer),
            "chain",
            [SMEM] + [VMEM] * (len(inputs) + 5),
            kept,
            [pltpu.VMEM((total, width), BF)] if first else [],
            3 * 10**9,
            10 * 2**20,
            {3: 0, 4: 2} if in_place else {},
        )(info, *inputs, hot, hots, slope, node_pack, turned)
        if layer > 0:
            cross = move(part, [layer], swap, -1)
            came = move(pay, [layer], both_ways, -1)
            incoming = (came, cross)

    out = call(
        functools.partial(grads_kernel, span, batches, groups),
        "weight_grads",
        [SMEM] + [VMEM] * 6,
        [like(count + rows)] * span + [like(rows)] * span,
        [pltpu.VMEM((6, width, width), BF)],
        2 * 10**9,
        10 * 2**20,
    )(info, edges_turned, act_turned, feats_turned, node_pack, keep, pay)
    across = [[(worker(m, h), (1 - h) * span + (m + step) % span) for m, h in works] for step in range(span)]
    far = [move(block, every, across[step]) for step, block in enumerate(out[span:])]
    near = [out[0]] + [move(out[step], every, deliver[step]) for step in range(1, span)]
    grad_shape = jax.ShapeDtypeStruct((1, share, width), F32)
    return call(
        functools.partial(finish_kernel, span, batches, groups),
        "finish",
        [SMEM] + [VMEM] * (2 * span),
        [
            jax.ShapeDtypeStruct((1, batches, node_share, width), BF),
            jax.ShapeDtypeStruct((1, batches, count, width), BF),
        ]
        + [grad_shape] * 7,
        [pltpu.VMEM((batches, PARTS, rows, width), BF)],
        0,
        5 * 2**20,
    )(info, *near, *far)


def solution(mesh):
    in_specs = (
        P("section", None, None, None),
        P("section", None, "edge", None),
        P(),
        P(None, "edge", None),
        P(None, "edge", None),
        P(None, "edge"),
        P(None, "edge"),
        P("section", None, None),
        P("section", None, None),
        P("section", None, None),
        P("section", None, None),
        P("section", None, None),
        P("section", None, None),
        P("section", None, None),
    )
    out_specs = (
        P("section", None, "edge", None),
        P("section", None, "edge", None),
        P("section", "edge", None),
        P("section", "edge", None),
        P("section", "edge", None),
        P("section", "edge", None),
        P("section", "edge", None),
        P("section", "edge", None),
        P("section", "edge", None),
    )
    return jax.shard_map(body, mesh=mesh, in_specs=in_specs, out_specs=out_specs, check_vma=False)
```

```python
import functools

import jax
import jax.numpy as jnp
from jax import lax
from jax.experimental import pallas as pl
from jax.experimental.pallas import tpu as pltpu
from jax.sharding import PartitionSpec as P

BLOCK = 128
PARTS = 2
PAD = 16
SEND, RECV, EDGE, MSG, NODE, AGG, OUT = range(7)
GRANT = 32
BF = jnp.bfloat16
F32 = jnp.float32
ANY = pl.BlockSpec(memory_space=pl.ANY)
SMEM = pl.BlockSpec(memory_space=pltpu.SMEM)
VMEM = pl.BlockSpec(memory_space=pltpu.VMEM)


def matmul(left, right):
    return jnp.dot(left, right, preferred_element_type=F32)


def times_transposed(left, right):
    return lax.dot_general(left, right, (((1,), (1,)), ((), ())), preferred_element_type=F32)


def transposed_times(left, right):
    return lax.dot_general(left, right, (((0,), (0,)), ((), ())), preferred_element_type=F32)


def base_of(half, span, batches):
    return jnp.where(half == 0, span - batches, 0)


def place_of(batch, half, span, batches):
    return (span - batches if half == 0 else 0) + batch


def worker_of(batch, half, span, batches):
    return half * span + place_of(batch, half, span, batches)


def own_batch(member, span, batches):
    half = lax.div(member, span)
    batch = lax.rem(member, span) - base_of(half, span, batches)
    return jnp.clip(batch, 0, batches - 1)


def pick_row(table, row, lanes):
    value = table[0:1, lanes]
    for other in range(1, table.shape[0]):
        value = jnp.where(row == other, table[other : other + 1, lanes], value)
    return value


def hot_rows(index_rows, row, nodes):
    index = index_rows[row : row + 1, :].astype(F32).astype(jnp.int32)
    rows = lax.broadcasted_iota(jnp.int32, (nodes, index_rows.shape[1]), 0)
    return jnp.where(rows == index, 1.0, 0.0).astype(BF)


def hot_columns(index_rows, row, nodes):
    pick = lax.broadcasted_iota(jnp.int32, (index_rows.shape[0], nodes), 0) == row
    index = transposed_times(index_rows, jnp.where(pick, 1.0, 0.0).astype(BF))
    columns = lax.broadcasted_iota(jnp.int32, index.shape, 1).astype(F32)
    return jnp.where(columns == index, 1.0, 0.0).astype(BF)


def slope_of(pre, sigma):
    return (sigma * (1.0 + pre * (1.0 - sigma))).astype(BF)


def pack_kernel(span, batches, info, senders, receivers, tiles, edges, *refs):
    outs, seconds = refs[:span], refs[span : 2 * span - 1]
    send_in, recv_in, sems = refs[2 * span - 1 :]
    member = info[1]
    half = lax.div(member, span)
    offset = lax.rem(member, span)
    count = senders.shape[1]
    tile_count = tiles.shape[1]
    tile_len = count // tile_count
    gets = [
        pltpu.make_async_copy(senders, send_in, sems.at[0]),
        pltpu.make_async_copy(receivers, recv_in, sems.at[1]),
    ]
    picks, loads = [], []
    for step in range(span):
        batch = lax.rem(offset - step + span, span) - base_of(half, span, batches)
        picks.append(jnp.clip(batch, 0, batches - 1))
        loads.append(
            pltpu.make_async_copy(edges.at[0, picks[step]], outs[step].at[pl.ds(0, count)], sems.at[2 + step])
        )
    for copy in gets + loads:
        copy.start()
    for copy in gets:
        copy.wait()
    for step in range(span):
        batch = picks[step]
        out = outs[step]
        out[count:] = jnp.zeros((PAD, out.shape[1]), BF)
        for tile in range(tile_count):
            lanes = slice(tile * tile_len, (tile + 1) * tile_len)
            send = pick_row(send_in, batch, lanes) + tiles[batch, tile, 0] * BLOCK
            recv = pick_row(recv_in, batch, lanes) + tiles[batch, tile, 1] * BLOCK
            which = lax.broadcasted_iota(jnp.int32, (PAD, tile_len), 0)
            block = jnp.where(which == 0, send, jnp.where(which == 1, recv, 0))
            out[count:, lanes] = block.astype(F32).astype(BF)
    for step in range(span):
        loads[step].wait()
        if step:
            seconds[step - 1][...] = outs[step][...]


def ready_kernel(span, batches, info, nodes, weights, *refs):
    turned, hidden, node_pre, feats_turned = refs[span - 1 : span + 3]
    batch = own_batch(info[1], span, batches)
    node_count = nodes.shape[2]
    feats = nodes[0, batch]
    hidden[:node_count] = matmul(feats, weights[SEND]).astype(BF)
    hidden[node_count:] = matmul(feats, weights[RECV]).astype(BF)
    node_pre[...] = matmul(feats, weights[NODE])
    feats_turned[...] = feats.T
    for slot in range(weights.shape[0]):
        turned[slot] = weights[slot].T


def forward_kernel(span, batches, chunk, sections, info, own, *refs):
    groups = (refs[: span - 1], refs[span - 1 : 2 * span - 2])
    hidden, weights = refs[2 * span - 2 : 2 * span]
    act_out, slope_out, part_out, hot_out, hots_out, pieces, both, index = refs[2 * span :]
    count = own.shape[0] - PAD
    node_count = part_out.shape[0]
    for which, others in enumerate(groups):

        @pl.when(lax.rem(sections - 1 - info[0], 2) == which)
        def _(others=others):
            for step in range(1, span):
                pieces[step * count : (step + 1) * count] = others[step - 1][:count]
                index[step] = others[step - 1][count:, :count]

    pieces[:count] = own[:count]
    index[0] = own[count:, :count]
    for step in range(span):
        run = slice(step * count, (step + 1) * count)
        index_rows = index[step]
        hots_out[:node_count, run] = hot_rows(index_rows, 0, node_count)
        hots_out[node_count:, run] = hot_rows(index_rows, 1, node_count)
        both[run, :node_count] = hot_columns(index_rows, 0, node_count)
        recv_hot = hot_columns(index_rows, 1, node_count)
        both[run, node_count:] = recv_hot
        hot_out[run] = recv_hot
    for at in range(0, span * count, chunk):
        run = slice(at, at + chunk)
        pre = matmul(both[run], hidden[...]) + matmul(pieces[run], weights[EDGE])
        sigma = jax.nn.sigmoid(pre)
        act_out[run] = (pre * sigma).astype(BF)
        slope_out[run] = slope_of(pre, sigma)
    total = matmul(hots_out[node_count:], act_out[...])
    part_out[...] = matmul(total.astype(BF), weights[MSG]).astype(BF)


def turn_kernel(pieces, act, edges_turned, act_turned):
    rows = 2 * BLOCK
    for at in range(0, act.shape[0], rows):
        run = slice(at, at + rows)
        edges_turned[:, run] = pieces[run].T
        act_turned[:, run] = act[run].T


def node_kernel(node_pre, part_own, part_other, weights, turned_first, out):
    count = part_own.shape[0]
    agg = (part_own[...].astype(F32) + part_other[...].astype(F32)).astype(BF)
    pre = node_pre[...] + matmul(agg, weights[AGG])
    sigma = jax.nn.sigmoid(pre)
    out[:count] = agg
    out[count : 2 * count] = (pre * sigma).astype(BF)
    out[2 * count :] = slope_of(pre, sigma)


def chain_kernel(span, batches, chunk, first, active, info, *refs):
    kept = None
    if not first and len(refs) == 12:
        kept = refs[2:4]
        refs = refs[:2] + refs[4:]

    @pl.when(info[0] == active)
    def _():
        chain_step(span, batches, chunk, first, info, *refs)

    if kept is not None:

        @pl.when(info[0] != active)
        def _():
            refs[-3][...] = kept[0][...]
            refs[-1][...] = kept[1][...]


def chain_step(span, batches, chunk, first, info, *refs):
    member = info[1]
    batch = own_batch(member, span, batches)
    half = lax.div(member, span)
    if first:
        top_nodes, top_edges = refs[:2]
        others = refs[2 : span + 1]
        hot, hots, slope, node_pack, turned, pay, part_out, keep, came = refs[span + 1 :]
        count = top_edges.shape[1]
        for step in range(span):
            came[step * count : (step + 1) * count] = others[step - 1][...] if step else top_edges[batch]
        grad = top_nodes[batch]
    else:
        came, cross = refs[:2]
        hot, hots, slope, node_pack, turned, pay, part_out, keep = refs[2:]
        total = slope.shape[0]
        grad = (came[total:].astype(F32) + cross[...].astype(F32)).astype(BF)
    total = slope.shape[0]
    node_count = part_out.shape[0]
    node_at = 2 * total
    delta = (matmul(grad, turned[OUT]) * node_pack[2 * node_count :].astype(F32)).astype(BF)
    agg_grad = matmul(delta, turned[AGG]).astype(BF)
    keep[node_at : node_at + node_count] = delta
    keep[node_at + node_count : node_at + 2 * node_count] = grad
    for at in range(0, total, chunk):
        run = slice(at, at + chunk)
        incoming = came[run].astype(F32)
        message_grad = (incoming + matmul(hot[run], agg_grad)).astype(BF)
        keep[run] = message_grad
        edge_delta = (matmul(message_grad, turned[MSG]) * slope[run].astype(F32)).astype(BF)
        keep[total + at : total + at + chunk] = edge_delta
        pay[run] = (incoming + matmul(edge_delta, turned[EDGE])).astype(BF)
    sums = matmul(hots[...], keep[total : 2 * total]).astype(BF)
    keep[node_at + 2 * node_count :] = sums
    own = grad.astype(F32) + matmul(delta, turned[NODE])
    own = own * jnp.where(half == 0, 1.0, 0.0)
    part = matmul(sums[:node_count], turned[SEND]) + matmul(sums[node_count:], turned[RECV])
    part = (own + part).astype(BF)
    pay[total:] = part
    part_out[...] = part


def grads_kernel(span, batches, groups, info, edges_turned, act_turned, feats_turned, node_pack, keep, pay, *refs):
    near, far = refs[:span], refs[span : 2 * span]
    sums = refs[2 * span]
    member = info[1]
    half = lax.div(member, span)
    offset = lax.rem(member, span)
    batch = own_batch(member, span, batches)
    total = edges_turned.shape[1]
    node_count = feats_turned.shape[1]
    width = feats_turned.shape[0]
    count = total // span
    node_at = 2 * total
    delta = keep[node_at : node_at + node_count]
    grad = keep[node_at + node_count : node_at + 2 * node_count]
    sums[0] = matmul(feats_turned[...], keep[node_at + 2 * node_count : node_at + 3 * node_count]).astype(BF)
    sums[1] = matmul(feats_turned[...], keep[node_at + 3 * node_count :]).astype(BF)
    sums[2] = matmul(edges_turned[...], keep[total : 2 * total]).astype(BF)
    sums[3] = matmul(act_turned[...], keep[:total]).astype(BF)
    sums[5] = transposed_times(node_pack[:node_count], delta).astype(BF)

    @pl.when(half == 0)
    def _():
        sums[4] = matmul(feats_turned[...], delta).astype(BF)

    @pl.when(half != 0)
    def _():
        sums[4] = transposed_times(node_pack[node_count : 2 * node_count], grad).astype(BF)

    share = width // groups
    node_share = node_count // groups

    def fill(block, start, owner):
        at = pl.multiple_of(owner * share, share)
        for slot in range(5):
            block[start + slot * share : start + (slot + 1) * share] = sums[slot, pl.ds(at, share)]
        at_half = pl.multiple_of(owner * share + half * (share // 2), share // 2)
        block[start + 5 * share : start + 5 * share + share // 2] = sums[5, pl.ds(at_half, share // 2)]
        at_node = pl.multiple_of(total + owner * node_share, node_share)
        block[start + 5 * share + share // 2 :] = pay[pl.ds(at_node, node_share)]

    for step in range(span):
        near[step][:count] = pay[step * count : (step + 1) * count]
        fill(near[step], count, half * span + lax.rem(offset + step, span))
        fill(far[step], 0, (1 - half) * span + lax.rem(batch + step, span))


def finish_kernel(span, batches, groups, info, *refs):
    near, far = refs[:span], refs[span : 2 * span]
    refs = refs[2 * span :]
    nodes_out, edges_out, send_out, recv_out, edge_out, msg_out, node_out, agg_out, out_out = refs[:9]
    held = refs[9]
    member = info[1]
    half = lax.div(member, span)
    offset = lax.rem(member, span)
    count = edges_out.shape[2]
    for batch in range(batches):
        turn = lax.rem(offset - base_of(half, span, batches) - batch + 2 * span, span)
        turn_far = lax.rem(offset - batch + span, span)
        for step in range(span):

            @pl.when(turn == step)
            def _(step=step, batch=batch):
                edges_out[0, batch] = near[step][:count]
                held[batch, half] = near[step][count:]

            @pl.when(turn_far == step)
            def _(step=step, batch=batch):
                held[batch, 1 - half] = far[step][...]

    share = send_out.shape[1]
    for slot, out in enumerate((send_out, recv_out, edge_out, msg_out)):
        rows = slice(slot * share, (slot + 1) * share)
        value = None
        for batch in range(batches):
            for part in range(PARTS):
                piece = held[batch, part, rows].astype(F32)
                value = piece if value is None else value + piece
        out[0] = value

    def over_batches(part, start, length):
        value = None
        for batch in range(batches):
            piece = held[batch, part, start : start + length].astype(F32)
            value = piece if value is None else value + piece
        return value

    node_out[0] = over_batches(0, 4 * share, share)
    out_out[0] = over_batches(1, 4 * share, share)
    for part in range(PARTS):
        agg_out[0, part * (share // 2) : (part + 1) * (share // 2)] = over_batches(part, 5 * share, share // 2)
    at = 5 * share + share // 2
    for batch in range(batches):
        rows = held[batch, 0, at:].astype(F32) + held[batch, 1, at:].astype(F32)
        nodes_out[0, batch] = rows.astype(BF)


def call(kernel, name, in_specs, out_shapes, scratch, flops, touched, aliases={}, grant=GRANT, passed=0):
    many = isinstance(out_shapes, list)
    return pl.pallas_call(
        kernel,
        name=name,
        out_shape=out_shapes,
        in_specs=in_specs,
        out_specs=[VMEM] * (len(out_shapes) - passed) + [ANY] * passed if many else VMEM,
        scratch_shapes=scratch,
        input_output_aliases=aliases,
        compiler_params=pltpu.CompilerParams(vmem_limit_bytes=grant * 2**20),
        cost_estimate=pl.CostEstimate(flops=flops, bytes_accessed=touched, transcendentals=0),
    )


def body(
    layer_nodes,
    layer_edges,
    top_nodes,
    top_edges,
    tile_blocks,
    senders,
    receivers,
    w_send,
    w_recv,
    w_edge,
    w_msg,
    w_node,
    w_agg,
    w_out,
):
    sections = lax.axis_size("section")
    groups = lax.axis_size("edge")
    section = lax.axis_index("section")
    member = lax.axis_index("edge")
    span = groups // PARTS
    _, batches, node_count, width = layer_nodes.shape
    count = layer_edges.shape[2]
    total = span * count
    chunk = 2 * count
    share = width // groups
    node_share = node_count // groups
    info = jnp.stack([section, member]).astype(jnp.int32)
    axes = ("section", "edge")
    works = [(m, h) for h in range(PARTS) for m in range(batches)]

    def worker(m, h):
        return worker_of(m, h, span, batches)

    def source(m, h, step):
        return h * span + (place_of(m, h, span, batches) + step) % span

    def move(value, layers, links, shift=0):
        pairs = [(s * groups + a, (s + shift) * groups + b) for s in layers for a, b in links]
        return lax.ppermute(value, axes, pairs)

    every = list(range(sections))
    last = [sections - 1]
    collect = [[(source(m, h, step), worker(m, h)) for m, h in works] for step in range(span)]
    deliver = [[(b, a) for a, b in links] for links in collect]

    def like(rows, cols=width, kind=BF):
        return jax.ShapeDtypeStruct((rows, cols), kind)

    packed = call(
        functools.partial(pack_kernel, span, batches),
        "pack",
        [SMEM, ANY, ANY, SMEM, ANY],
        [like(count + PAD)] * (2 * span - 1),
        [
            pltpu.VMEM((batches, count), jnp.int32),
            pltpu.VMEM((batches, count), jnp.int32),
            pltpu.SemaphoreType.DMA((2 + span,)),
        ],
        0,
        2**20,
        grant=62,
    )(info, senders, receivers, tile_blocks, layer_edges)
    own, first_out, second_out = packed[0], packed[1:span], packed[span:]
    groups_of = [list(range(sections - 1 - group, -1, -2)) for group in range(2)]
    first_in = [move(piece, groups_of[0], collect[step + 1]) for step, piece in enumerate(first_out)]
    weights = jnp.concatenate([w_send, w_recv, w_edge, w_msg, w_node, w_agg, w_out], axis=0)
    half = member // span
    offset = member % span
    tops = []
    for step in range(1, span):
        pick = jnp.clip((offset - step) % span - base_of(half, span, batches), 0, batches - 1)
        tops.append(move(lax.dynamic_index_in_dim(top_edges, pick, 0, keepdims=False), last, collect[step]))

    ready = call(
        functools.partial(ready_kernel, span, batches),
        "ready",
        [SMEM, VMEM, VMEM] + [ANY] * (span - 1),
        [
            jax.ShapeDtypeStruct((7, width, width), BF),
            like(2 * node_count),
            like(node_count, kind=F32),
            like(width, node_count),
        ]
        + [like(count + PAD)] * (span - 1),
        [],
        4 * 10**8,
        10 * 2**20,
        {3 + step: 4 + step for step in range(span - 1)},
        passed=span - 1,
    )(info, layer_nodes, weights, *second_out)
    turned, hidden, node_pre, feats_turned = ready[:4]
    second_in = [move(piece, groups_of[1], collect[step + 1]) for step, piece in enumerate(ready[4:])]

    act, slope, part, hot, hots, pieces = call(
        functools.partial(forward_kernel, span, batches, chunk, sections),
        "forward",
        [SMEM] + [VMEM] * (2 * span + 1),
        [like(total), like(total), like(node_count), like(total, node_count), like(2 * node_count, total), like(total)],
        [pltpu.VMEM((total, 2 * node_count), BF), pltpu.VMEM((span, PAD, count), BF)],
        2 * 10**9,
        6 * 2**20,
    )(info, own, *first_in, *second_in, hidden, weights)

    swap = [(worker(m, h), worker(m, 1 - h)) for m, h in works]
    part_other = move(part, every, swap)
    edges_turned, act_turned = call(
        turn_kernel,
        "turn",
        [VMEM] * 2,
        [like(width, total), like(width, total)],
        [],
        0,
        4 * 2**20,
    )(pieces, act)
    node_pack = call(
        node_kernel,
        "node_forward",
        [VMEM] * 4 + [ANY],
        like(3 * node_count),
        [],
        10**5,
        2**10,
    )(node_pre, part, part_other, weights, edges_turned)

    kept = [like(total + node_count), like(node_count), like(2 * total + 4 * node_count)]
    both_ways = [(worker(m, h), worker(m, h)) for m, h in works]
    rows = 5 * share + share // 2 + node_share
    pay = keep = None
    incoming = None
    for moment in range(sections):
        first = moment == 0
        layer = sections - 1 - moment
        in_place = not first
        if first:
            inputs = (top_nodes, top_edges, *tops)
        else:
            inputs = (*incoming, pay, keep)
        pay, part, keep = call(
            functools.partial(chain_kernel, span, batches, chunk, first, layer),
            "chain",
            [SMEM] + [VMEM] * (len(inputs) + 5),
            kept,
            [pltpu.VMEM((total, width), BF)] if first else [],
            3 * 10**9,
            10 * 2**20,
            {3: 0, 4: 2} if in_place else {},
        )(info, *inputs, hot, hots, slope, node_pack, turned)
        if layer > 0:
            cross = move(part, [layer], swap, -1)
            came = move(pay, [layer], both_ways, -1)
            incoming = (came, cross)

    out = call(
        functools.partial(grads_kernel, span, batches, groups),
        "weight_grads",
        [SMEM] + [VMEM] * 6,
        [like(count + rows)] * span + [like(rows)] * span,
        [pltpu.VMEM((6, width, width), BF)],
        2 * 10**9,
        10 * 2**20,
    )(info, edges_turned, act_turned, feats_turned, node_pack, keep, pay)
    across = [[(worker(m, h), (1 - h) * span + (m + step) % span) for m, h in works] for step in range(span)]
    far = [move(block, every, across[step]) for step, block in enumerate(out[span:])]
    near = [out[0]] + [move(out[step], every, deliver[step]) for step in range(1, span)]
    grad_shape = jax.ShapeDtypeStruct((1, share, width), F32)
    return call(
        functools.partial(finish_kernel, span, batches, groups),
        "finish",
        [SMEM] + [VMEM] * (2 * span),
        [
            jax.ShapeDtypeStruct((1, batches, node_share, width), BF),
            jax.ShapeDtypeStruct((1, batches, count, width), BF),
        ]
        + [grad_shape] * 7,
        [pltpu.VMEM((batches, PARTS, rows, width), BF)],
        0,
        5 * 2**20,
    )(info, *near, *far)


def solution(mesh):
    in_specs = (
        P("section", None, None, None),
        P("section", None, "edge", None),
        P(),
        P(None, "edge", None),
        P(None, "edge", None),
        P(None, "edge"),
        P(None, "edge"),
        P("section", None, None),
        P("section", None, None),
        P("section", None, None),
        P("section", None, None),
        P("section", None, None),
        P("section", None, None),
        P("section", None, None),
    )
    out_specs = (
        P("section", None, "edge", None),
        P("section", None, "edge", None),
        P("section", "edge", None),
        P("section", "edge", None),
        P("section", "edge", None),
        P("section", "edge", None),
        P("section", "edge", None),
        P("section", "edge", None),
        P("section", "edge", None),
    )
    return jax.shard_map(body, mesh=mesh, in_specs=in_specs, out_specs=out_specs, check_vma=False)
```

```python
import functools

import jax
import jax.numpy as jnp
from jax import lax
from jax.experimental import pallas as pl
from jax.experimental.pallas import tpu as pltpu
from jax.sharding import PartitionSpec as P

BLOCK = 128
PARTS = 2
PAD = 16
SEND, RECV, EDGE, MSG, NODE, AGG, OUT = range(7)
GRANT = 32
BF = jnp.bfloat16
F32 = jnp.float32
ANY = pl.BlockSpec(memory_space=pl.ANY)
SMEM = pl.BlockSpec(memory_space=pltpu.SMEM)
VMEM = pl.BlockSpec(memory_space=pltpu.VMEM)


def matmul(left, right):
    return jnp.dot(left, right, preferred_element_type=F32)


def times_transposed(left, right):
    return lax.dot_general(left, right, (((1,), (1,)), ((), ())), preferred_element_type=F32)


def transposed_times(left, right):
    return lax.dot_general(left, right, (((0,), (0,)), ((), ())), preferred_element_type=F32)


def base_of(half, span, batches):
    return jnp.where(half == 0, span - batches, 0)


def place_of(batch, half, span, batches):
    return (span - batches if half == 0 else 0) + batch


def worker_of(batch, half, span, batches):
    return half * span + place_of(batch, half, span, batches)


def own_batch(member, span, batches):
    half = lax.div(member, span)
    batch = lax.rem(member, span) - base_of(half, span, batches)
    return jnp.clip(batch, 0, batches - 1)


def pick_row(table, row, lanes):
    value = table[0:1, lanes]
    for other in range(1, table.shape[0]):
        value = jnp.where(row == other, table[other : other + 1, lanes], value)
    return value


def hot_rows(index_rows, row, nodes):
    index = index_rows[row : row + 1, :].astype(F32).astype(jnp.int32)
    rows = lax.broadcasted_iota(jnp.int32, (nodes, index_rows.shape[1]), 0)
    return jnp.where(rows == index, 1.0, 0.0).astype(BF)


def hot_columns(index_rows, row, nodes):
    pick = lax.broadcasted_iota(jnp.int32, (index_rows.shape[0], nodes), 0) == row
    index = transposed_times(index_rows, jnp.where(pick, 1.0, 0.0).astype(BF))
    columns = lax.broadcasted_iota(jnp.int32, index.shape, 1).astype(F32)
    return jnp.where(columns == index, 1.0, 0.0).astype(BF)


def slope_of(pre, sigma):
    return (sigma * (1.0 + pre * (1.0 - sigma))).astype(BF)


def pack_kernel(span, batches, info, senders, receivers, tiles, edges, tops, *refs):
    outs, seconds = refs[:span], refs[span : 2 * span - 1]
    send_in, recv_in, sems = refs[2 * span - 1 :]
    member = info[1]
    half = lax.div(member, span)
    offset = lax.rem(member, span)
    count = senders.shape[1]
    tile_count = tiles.shape[1]
    tile_len = count // tile_count
    gets = [
        pltpu.make_async_copy(senders, send_in, sems.at[0]),
        pltpu.make_async_copy(receivers, recv_in, sems.at[1]),
    ]
    picks, loads, puts = [], [], []
    for step in range(span):
        batch = lax.rem(offset - step + span, span) - base_of(half, span, batches)
        picks.append(jnp.clip(batch, 0, batches - 1))
        latents = outs[step].at[pl.ds(0, count)]
        grads = outs[step].at[pl.ds(count + PAD, count)]
        loads.append(pltpu.make_async_copy(edges.at[0, picks[step]], latents, sems.at[2 + step]))
        puts.append(pltpu.make_async_copy(tops.at[picks[step]], grads, sems.at[2 + span + step]))
    for copy in gets + loads + puts:
        copy.start()
    for copy in gets:
        copy.wait()
    for step in range(span):
        batch = picks[step]
        out = outs[step]
        out[count : count + PAD] = jnp.zeros((PAD, out.shape[1]), BF)
        for tile in range(tile_count):
            lanes = slice(tile * tile_len, (tile + 1) * tile_len)
            send = pick_row(send_in, batch, lanes) + tiles[batch, tile, 0] * BLOCK
            recv = pick_row(recv_in, batch, lanes) + tiles[batch, tile, 1] * BLOCK
            which = lax.broadcasted_iota(jnp.int32, (PAD, tile_len), 0)
            block = jnp.where(which == 0, send, jnp.where(which == 1, recv, 0))
            out[count : count + PAD, lanes] = block.astype(F32).astype(BF)
        loads[step].wait()
        if step:
            copy = pltpu.make_async_copy(
                out.at[pl.ds(0, count + PAD)], seconds[step - 1], sems.at[1 + 2 * span + step]
            )
            copy.start()
            puts.append(copy)
    for copy in puts:
        copy.wait()


def ready_kernel(span, batches, info, nodes, weights, turned, hidden, node_pre, feats_turned):
    batch = own_batch(info[1], span, batches)
    node_count = nodes.shape[2]
    feats = nodes[0, batch]
    hidden[:node_count] = matmul(feats, weights[SEND]).astype(BF)
    hidden[node_count:] = matmul(feats, weights[RECV]).astype(BF)
    node_pre[...] = matmul(feats, weights[NODE])
    feats_turned[...] = feats.T
    for slot in range(weights.shape[0]):
        turned[slot] = weights[slot].T


def forward_kernel(span, batches, chunk, sections, info, own, *refs):
    groups = (refs[: span - 1], refs[span - 1 : 2 * span - 2])
    hidden, weights = refs[2 * span - 2 : 2 * span]
    act_out, slope_out, part_out, hot_out, hots_out, pieces, tops, both, index = refs[2 * span :]
    count = (own.shape[0] - PAD) // 2
    node_count = part_out.shape[0]
    for which, others in enumerate(groups):

        @pl.when(lax.rem(sections - 1 - info[0], 2) == which)
        def _(others=others, which=which):
            for step in range(1, span):
                pieces[step * count : (step + 1) * count] = others[step - 1][:count]
                index[step] = others[step - 1][count : count + PAD, :count]
                if which == 0:
                    tops[step * count : (step + 1) * count] = others[step - 1][count + PAD :]

    pieces[:count] = own[:count]
    tops[:count] = own[count + PAD :]
    index[0] = own[count : count + PAD, :count]
    for step in range(span):
        run = slice(step * count, (step + 1) * count)
        index_rows = index[step]
        hots_out[:node_count, run] = hot_rows(index_rows, 0, node_count)
        hots_out[node_count:, run] = hot_rows(index_rows, 1, node_count)
        both[run, :node_count] = hot_columns(index_rows, 0, node_count)
        recv_hot = hot_columns(index_rows, 1, node_count)
        both[run, node_count:] = recv_hot
        hot_out[run] = recv_hot
    for at in range(0, span * count, chunk):
        run = slice(at, at + chunk)
        pre = matmul(both[run], hidden[...]) + matmul(pieces[run], weights[EDGE])
        sigma = jax.nn.sigmoid(pre)
        act_out[run] = (pre * sigma).astype(BF)
        slope_out[run] = slope_of(pre, sigma)
    total = matmul(hots_out[node_count:], act_out[...])
    part_out[...] = matmul(total.astype(BF), weights[MSG]).astype(BF)


def turn_kernel(pieces, act, edges_turned, act_turned):
    rows = 2 * BLOCK
    for at in range(0, act.shape[0], rows):
        run = slice(at, at + rows)
        edges_turned[:, run] = pieces[run].T
        act_turned[:, run] = act[run].T


def node_kernel(node_pre, part_own, part_other, weights, turned_first, out):
    count = part_own.shape[0]
    agg = (part_own[...].astype(F32) + part_other[...].astype(F32)).astype(BF)
    pre = node_pre[...] + matmul(agg, weights[AGG])
    sigma = jax.nn.sigmoid(pre)
    out[:count] = agg
    out[count : 2 * count] = (pre * sigma).astype(BF)
    out[2 * count :] = slope_of(pre, sigma)


def chain_kernel(span, batches, chunk, first, split, active, info, *refs):
    incoming = refs[:2] if first else refs[:3]
    refs = refs[len(incoming) :]
    kept = ()
    if not first:
        kept, refs = refs[:2], refs[2:]
    common, refs = refs[:5], refs[5:]

    @pl.when(info[0] == active)
    def _():
        chain_step(span, batches, chunk, first, split, info, incoming, *common, *refs)

    if kept:

        @pl.when(info[0] != active)
        def _():
            refs[0][...] = kept[0][...]
            refs[1][...] = kept[1][...]


def chain_step(
    span, batches, chunk, first, split, info, incoming, hot, hots, slope, node_pack, turned, pay, keep, part_out, *rest
):
    member = info[1]
    batch = own_batch(member, span, batches)
    half = lax.div(member, span)
    total = slope.shape[0]
    if first:
        top_nodes, came = incoming
        grad = top_nodes[batch]
    else:
        came, part_own, cross = incoming
        mine = part_own[...] if part_own.shape[0] == cross.shape[0] else came[total:]
        grad = (mine.astype(F32) + cross[...].astype(F32)).astype(BF)
    node_count = part_out.shape[0]
    node_at = 2 * total
    delta = (matmul(grad, turned[OUT]) * node_pack[2 * node_count :].astype(F32)).astype(BF)
    agg_grad = matmul(delta, turned[AGG]).astype(BF)
    keep[node_at : node_at + node_count] = delta
    keep[node_at + node_count : node_at + 2 * node_count] = grad
    for at in range(0, total, chunk):
        run = slice(at, at + chunk)
        before = came[run].astype(F32)
        message_grad = (before + matmul(hot[run], agg_grad)).astype(BF)
        keep[run] = message_grad
        edge_delta = (matmul(message_grad, turned[MSG]) * slope[run].astype(F32)).astype(BF)
        keep[total + at : total + at + chunk] = edge_delta
        below = (before + matmul(edge_delta, turned[EDGE])).astype(BF)
        pay[run] = below
        if split:
            rest[0][run] = below
    sums = matmul(hots[...], keep[total : 2 * total]).astype(BF)
    keep[node_at + 2 * node_count :] = sums
    own = grad.astype(F32) + matmul(delta, turned[NODE])
    own = own * jnp.where(half == 0, 1.0, 0.0)
    part = matmul(sums[:node_count], turned[SEND]) + matmul(sums[node_count:], turned[RECV])
    part = (own + part).astype(BF)
    pay[total:] = part
    part_out[...] = part


def grads_kernel(span, batches, groups, info, edges_turned, act_turned, feats_turned, node_pack, keep, pay, *refs):
    near, far = refs[:span], refs[span : 2 * span]
    sums = refs[2 * span]
    member = info[1]
    half = lax.div(member, span)
    offset = lax.rem(member, span)
    batch = own_batch(member, span, batches)
    total = edges_turned.shape[1]
    node_count = feats_turned.shape[1]
    width = feats_turned.shape[0]
    count = total // span
    node_at = 2 * total
    delta = keep[node_at : node_at + node_count]
    grad = keep[node_at + node_count : node_at + 2 * node_count]
    sums[0] = matmul(feats_turned[...], keep[node_at + 2 * node_count : node_at + 3 * node_count]).astype(BF)
    sums[1] = matmul(feats_turned[...], keep[node_at + 3 * node_count :]).astype(BF)
    sums[2] = matmul(edges_turned[...], keep[total : 2 * total]).astype(BF)
    sums[3] = matmul(act_turned[...], keep[:total]).astype(BF)
    sums[5] = transposed_times(node_pack[:node_count], delta).astype(BF)

    @pl.when(half == 0)
    def _():
        sums[4] = matmul(feats_turned[...], delta).astype(BF)

    @pl.when(half != 0)
    def _():
        sums[4] = transposed_times(node_pack[node_count : 2 * node_count], grad).astype(BF)

    share = width // groups
    node_share = node_count // groups

    def fill(block, start, owner):
        at = pl.multiple_of(owner * share, share)
        for slot in range(5):
            block[start + slot * share : start + (slot + 1) * share] = sums[slot, pl.ds(at, share)]
        at_half = pl.multiple_of(owner * share + half * (share // 2), share // 2)
        block[start + 5 * share : start + 5 * share + share // 2] = sums[5, pl.ds(at_half, share // 2)]
        at_node = pl.multiple_of(total + owner * node_share, node_share)
        block[start + 5 * share + share // 2 :] = pay[pl.ds(at_node, node_share)]

    for step in range(span):
        near[step][:count] = pay[step * count : (step + 1) * count]
        fill(near[step], count, half * span + lax.rem(offset + step, span))
        fill(far[step], 0, (1 - half) * span + lax.rem(batch + step, span))


def finish_kernel(span, batches, groups, info, *refs):
    near, far = refs[:span], refs[span : 2 * span]
    refs = refs[2 * span :]
    nodes_out, edges_out, send_out, recv_out, edge_out, msg_out, node_out, agg_out, out_out = refs[:9]
    held = refs[9]
    member = info[1]
    half = lax.div(member, span)
    offset = lax.rem(member, span)
    count = edges_out.shape[2]
    for batch in range(batches):
        turn = lax.rem(offset - base_of(half, span, batches) - batch + 2 * span, span)
        turn_far = lax.rem(offset - batch + span, span)
        for step in range(span):

            @pl.when(turn == step)
            def _(step=step, batch=batch):
                edges_out[0, batch] = near[step][:count]
                held[batch, half] = near[step][count:]

            @pl.when(turn_far == step)
            def _(step=step, batch=batch):
                held[batch, 1 - half] = far[step][...]

    share = send_out.shape[1]
    for slot, out in enumerate((send_out, recv_out, edge_out, msg_out)):
        rows = slice(slot * share, (slot + 1) * share)
        value = None
        for batch in range(batches):
            for part in range(PARTS):
                piece = held[batch, part, rows].astype(F32)
                value = piece if value is None else value + piece
        out[0] = value

    def over_batches(part, start, length):
        value = None
        for batch in range(batches):
            piece = held[batch, part, start : start + length].astype(F32)
            value = piece if value is None else value + piece
        return value

    node_out[0] = over_batches(0, 4 * share, share)
    out_out[0] = over_batches(1, 4 * share, share)
    for part in range(PARTS):
        agg_out[0, part * (share // 2) : (part + 1) * (share // 2)] = over_batches(part, 5 * share, share // 2)
    at = 5 * share + share // 2
    for batch in range(batches):
        rows = held[batch, 0, at:].astype(F32) + held[batch, 1, at:].astype(F32)
        nodes_out[0, batch] = rows.astype(BF)


def call(kernel, name, in_specs, out_shapes, scratch, flops, touched, aliases={}, grant=GRANT, passed=0):
    many = isinstance(out_shapes, list)
    return pl.pallas_call(
        kernel,
        name=name,
        out_shape=out_shapes,
        in_specs=in_specs,
        out_specs=[VMEM] * (len(out_shapes) - passed) + [ANY] * passed if many else VMEM,
        scratch_shapes=scratch,
        input_output_aliases=aliases,
        compiler_params=pltpu.CompilerParams(vmem_limit_bytes=grant * 2**20),
        cost_estimate=pl.CostEstimate(flops=flops, bytes_accessed=touched, transcendentals=0),
    )


def body(
    layer_nodes,
    layer_edges,
    top_nodes,
    top_edges,
    tile_blocks,
    senders,
    receivers,
    w_send,
    w_recv,
    w_edge,
    w_msg,
    w_node,
    w_agg,
    w_out,
):
    sections = lax.axis_size("section")
    groups = lax.axis_size("edge")
    section = lax.axis_index("section")
    member = lax.axis_index("edge")
    span = groups // PARTS
    _, batches, node_count, width = layer_nodes.shape
    count = layer_edges.shape[2]
    total = span * count
    chunk = 2 * count
    share = width // groups
    node_share = node_count // groups
    info = jnp.stack([section, member]).astype(jnp.int32)
    axes = ("section", "edge")
    works = [(m, h) for h in range(PARTS) for m in range(batches)]

    def worker(m, h):
        return worker_of(m, h, span, batches)

    def source(m, h, step):
        return h * span + (place_of(m, h, span, batches) + step) % span

    def move(value, layers, links, shift=0):
        pairs = [(s * groups + a, (s + shift) * groups + b) for s in layers for a, b in links]
        return lax.ppermute(value, axes, pairs)

    every = list(range(sections))
    last = [sections - 1]
    collect = [[(source(m, h, step), worker(m, h)) for m, h in works] for step in range(span)]
    deliver = [[(b, a) for a, b in links] for links in collect]

    def like(rows, cols=width, kind=BF):
        return jax.ShapeDtypeStruct((rows, cols), kind)

    packed = call(
        functools.partial(pack_kernel, span, batches),
        "pack",
        [SMEM, ANY, ANY, SMEM, ANY, ANY],
        [like(2 * count + PAD)] * span + [like(count + PAD)] * (span - 1),
        [
            pltpu.VMEM((batches, count), jnp.int32),
            pltpu.VMEM((batches, count), jnp.int32),
            pltpu.SemaphoreType.DMA((2 + 3 * span,)),
        ],
        0,
        2**20,
        passed=span - 1,
    )(info, senders, receivers, tile_blocks, layer_edges, top_edges)
    own, first_out, second_out = packed[0], packed[1:span], packed[span:]
    groups_of = [list(range(sections - 1 - group, -1, -2)) for group in range(2)]
    first_in = [move(piece, groups_of[0], collect[step + 1]) for step, piece in enumerate(first_out)]
    own, w_send, w_recv, w_edge, w_msg, w_node, w_agg, w_out = lax.optimization_barrier(
        (own, w_send, w_recv, w_edge, w_msg, w_node, w_agg, w_out)
    )
    weights = jnp.concatenate([w_send, w_recv, w_edge, w_msg, w_node, w_agg, w_out], axis=0)
    ready = call(
        functools.partial(ready_kernel, span, batches),
        "ready",
        [SMEM, VMEM, VMEM],
        [
            jax.ShapeDtypeStruct((7, width, width), BF),
            like(2 * node_count),
            like(node_count, kind=F32),
            like(width, node_count),
        ],
        [],
        4 * 10**8,
        10 * 2**20,
    )(info, layer_nodes, weights)
    turned, hidden, node_pre, feats_turned = ready
    first_in[0], second_out = lax.optimization_barrier((first_in[0], second_out))
    second_in = [move(piece, groups_of[1], collect[step + 1]) for step, piece in enumerate(second_out)]

    act, slope, part, hot, hots, pieces, tops = call(
        functools.partial(forward_kernel, span, batches, chunk, sections),
        "forward",
        [SMEM] + [VMEM] * (2 * span + 1),
        [like(total), like(total), like(node_count), like(total, node_count), like(2 * node_count, total)]
        + [like(total)] * 2,
        [pltpu.VMEM((total, 2 * node_count), BF), pltpu.VMEM((span, PAD, count), BF)],
        2 * 10**9,
        6 * 2**20,
    )(info, own, *first_in, *second_in, hidden, weights)

    swap = [(worker(m, h), worker(m, 1 - h)) for m, h in works]
    part_other = move(part, every, swap)
    edges_turned, act_turned = call(
        turn_kernel,
        "turn",
        [VMEM] * 2,
        [like(width, total), like(width, total)],
        [],
        0,
        4 * 2**20,
    )(pieces, act)
    node_pack = call(
        node_kernel,
        "node_forward",
        [VMEM] * 4 + [ANY],
        like(3 * node_count),
        [],
        10**5,
        2**10,
    )(node_pre, part, part_other, weights, edges_turned)

    both_ways = [(worker(m, h), worker(m, h)) for m, h in works]
    rows = 5 * share + share // 2 + node_share
    pay = keep = None
    incoming = None
    for moment in range(sections):
        first = moment == 0
        layer = sections - 1 - moment
        split = layer > 0 and layer % 2 == 0
        inputs = (top_nodes, tops) if first else (*incoming, pay, keep)
        made = call(
            functools.partial(chain_kernel, span, batches, chunk, first, split, layer),
            "chain",
            [SMEM] + [VMEM] * (len(inputs) + 5),
            [like(total + node_count), like(2 * total + 4 * node_count), like(node_count)]
            + [like(total)] * split,
            [],
            3 * 10**9,
            10 * 2**20,
            {} if first else {4: 0, 5: 1},
        )(info, *inputs, hot, hots, slope, node_pack, turned)
        pay, keep, part = made[:3]
        if split:
            mine = move(part, [layer], both_ways, -1)
            came = move(made[3], [layer], both_ways, -1)
            incoming = (came, mine, move(mine, [layer - 1], swap))
        elif layer > 0:
            cross = move(part, [layer], swap, -1)
            came = move(pay, [layer], both_ways, -1)
            incoming = (came, info, cross)

    out = call(
        functools.partial(grads_kernel, span, batches, groups),
        "weight_grads",
        [SMEM] + [VMEM] * 6,
        [like(count + rows)] * span + [like(rows)] * span,
        [pltpu.VMEM((6, width, width), BF)],
        2 * 10**9,
        10 * 2**20,
    )(info, edges_turned, act_turned, feats_turned, node_pack, keep, pay)
    across = [[(worker(m, h), (1 - h) * span + (m + step) % span) for m, h in works] for step in range(span)]
    far = [move(block, every, across[step]) for step, block in enumerate(out[span:])]
    near = [out[0]] + [move(out[step], every, deliver[step]) for step in range(1, span)]
    grad_shape = jax.ShapeDtypeStruct((1, share, width), F32)
    return call(
        functools.partial(finish_kernel, span, batches, groups),
        "finish",
        [SMEM] + [VMEM] * (2 * span),
        [
            jax.ShapeDtypeStruct((1, batches, node_share, width), BF),
            jax.ShapeDtypeStruct((1, batches, count, width), BF),
        ]
        + [grad_shape] * 7,
        [pltpu.VMEM((batches, PARTS, rows, width), BF)],
        0,
        5 * 2**20,
    )(info, *near, *far)


def solution(mesh):
    in_specs = (
        P("section", None, None, None),
        P("section", None, "edge", None),
        P(),
        P(None, "edge", None),
        P(None, "edge", None),
        P(None, "edge"),
        P(None, "edge"),
        P("section", None, None),
        P("section", None, None),
        P("section", None, None),
        P("section", None, None),
        P("section", None, None),
        P("section", None, None),
        P("section", None, None),
    )
    out_specs = (
        P("section", None, "edge", None),
        P("section", None, "edge", None),
        P("section", "edge", None),
        P("section", "edge", None),
        P("section", "edge", None),
        P("section", "edge", None),
        P("section", "edge", None),
        P("section", "edge", None),
        P("section", "edge", None),
    )
    return jax.shard_map(body, mesh=mesh, in_specs=in_specs, out_specs=out_specs, check_vma=False)
```

```python
import functools

import jax
import jax.numpy as jnp
from jax import lax
from jax.experimental import pallas as pl
from jax.experimental.pallas import tpu as pltpu
from jax.sharding import PartitionSpec as P

BLOCK = 128
PARTS = 2
PAD = 16
SEND, RECV, EDGE, MSG, NODE, AGG, OUT = range(7)
GRANT = 32
BF = jnp.bfloat16
F32 = jnp.float32
ANY = pl.BlockSpec(memory_space=pl.ANY)
SMEM = pl.BlockSpec(memory_space=pltpu.SMEM)
VMEM = pl.BlockSpec(memory_space=pltpu.VMEM)


def matmul(left, right):
    return jnp.dot(left, right, preferred_element_type=F32)


def times_transposed(left, right):
    return lax.dot_general(left, right, (((1,), (1,)), ((), ())), preferred_element_type=F32)


def transposed_times(left, right):
    return lax.dot_general(left, right, (((0,), (0,)), ((), ())), preferred_element_type=F32)


def base_of(half, span, batches):
    return jnp.where(half == 0, span - batches, 0)


def place_of(batch, half, span, batches):
    return (span - batches if half == 0 else 0) + batch


def worker_of(batch, half, span, batches):
    return half * span + place_of(batch, half, span, batches)


def own_batch(member, span, batches):
    half = lax.div(member, span)
    batch = lax.rem(member, span) - base_of(half, span, batches)
    return jnp.clip(batch, 0, batches - 1)


def pick_row(table, row, lanes):
    value = table[0:1, lanes]
    for other in range(1, table.shape[0]):
        value = jnp.where(row == other, table[other : other + 1, lanes], value)
    return value


def hot_rows(index_rows, row, nodes):
    index = index_rows[row : row + 1, :].astype(F32).astype(jnp.int32)
    rows = lax.broadcasted_iota(jnp.int32, (nodes, index_rows.shape[1]), 0)
    return jnp.where(rows == index, 1.0, 0.0).astype(BF)


def hot_columns(index_rows, row, nodes):
    pick = lax.broadcasted_iota(jnp.int32, (index_rows.shape[0], nodes), 0) == row
    index = transposed_times(index_rows, jnp.where(pick, 1.0, 0.0).astype(BF))
    columns = lax.broadcasted_iota(jnp.int32, index.shape, 1).astype(F32)
    return jnp.where(columns == index, 1.0, 0.0).astype(BF)


def slope_of(pre, sigma):
    return (sigma * (1.0 + pre * (1.0 - sigma))).astype(BF)


def pack_kernel(span, batches, sections, info, senders, receivers, tiles, edges, tops, *refs):
    own, own_top = refs[:2]
    outs, seconds = refs[2 : span + 1], refs[span + 1 :]
    member = info[1]
    half = lax.div(member, span)
    offset = lax.rem(member, span)
    count = senders.shape[1]
    tile_count = tiles.shape[1]
    tile_len = count // tile_count
    top = info[0] == sections - 1
    for step in range(span):
        batch = lax.rem(offset - step + span, span) - base_of(half, span, batches)
        batch = jnp.clip(batch, 0, batches - 1)
        out = outs[step - 1] if step else own
        out[:count] = edges[0, batch]
        out[count:] = jnp.zeros((PAD, out.shape[1]), BF)
        for tile in range(tile_count):
            lanes = slice(tile * tile_len, (tile + 1) * tile_len)
            send = pick_row(senders, batch, lanes) + tiles[batch, tile, 0] * BLOCK
            recv = pick_row(receivers, batch, lanes) + tiles[batch, tile, 1] * BLOCK
            which = lax.broadcasted_iota(jnp.int32, (PAD, tile_len), 0)
            block = jnp.where(which == 0, send, jnp.where(which == 1, recv, 0))
            out[count:, lanes] = block.astype(F32).astype(BF)
        if step:
            second = seconds[step - 1]
            second[count:] = out[count:]

            @pl.when(top)
            def _(second=second, batch=batch):
                second[:count] = tops[batch]

            @pl.when(jnp.logical_not(top))
            def _(second=second, out=out):
                second[:count] = out[:count]

        else:
            own_top[...] = tops[batch]


def ready_kernel(span, batches, info, nodes, weights, turned, hidden, node_pre, feats_turned):
    batch = own_batch(info[1], span, batches)
    node_count = nodes.shape[2]
    feats = nodes[0, batch]
    hidden[:node_count] = matmul(feats, weights[SEND]).astype(BF)
    hidden[node_count:] = matmul(feats, weights[RECV]).astype(BF)
    node_pre[...] = matmul(feats, weights[NODE])
    feats_turned[...] = feats.T
    for slot in range(weights.shape[0]):
        turned[slot] = weights[slot].T


def takes_part(info, sections, group):
    return lax.rem(sections - 1 - info[0], 2) == group


def forward_kernel(span, chunk, sections, group, info, *refs):
    @pl.when(takes_part(info, sections, group))
    def _():
        forward_step(span, chunk, *refs)


def forward_step(span, chunk, own, *refs):
    others = refs[: span - 1]
    hidden, weights = refs[span - 1 : span + 1]
    act_out, slope_out, part_out, hot_out, hots_out, pieces, both = refs[span + 1 :]
    count = own.shape[0] - PAD
    node_count = part_out.shape[0]
    for step in range(span):
        piece = others[step - 1] if step else own
        run = slice(step * count, (step + 1) * count)
        pieces[run] = piece[:count]
        index_rows = piece[count:, :count]
        hots_out[:node_count, run] = hot_rows(index_rows, 0, node_count)
        hots_out[node_count:, run] = hot_rows(index_rows, 1, node_count)
        both[run, :node_count] = hot_columns(index_rows, 0, node_count)
        recv_hot = hot_columns(index_rows, 1, node_count)
        both[run, node_count:] = recv_hot
        hot_out[run] = recv_hot
    for at in range(0, span * count, chunk):
        run = slice(at, at + chunk)
        pre = matmul(both[run], hidden[...]) + matmul(pieces[run], weights[EDGE])
        sigma = jax.nn.sigmoid(pre)
        act_out[run] = (pre * sigma).astype(BF)
        slope_out[run] = slope_of(pre, sigma)
    total = matmul(hots_out[node_count:], act_out[...])
    part_out[...] = matmul(total.astype(BF), weights[MSG]).astype(BF)


def turn_kernel(sections, group, info, pieces, act, edges_turned, act_turned):
    @pl.when(takes_part(info, sections, group))
    def _():
        rows = 2 * BLOCK
        for at in range(0, act.shape[0], rows):
            run = slice(at, at + rows)
            edges_turned[:, run] = pieces[run].T
            act_turned[:, run] = act[run].T


def node_kernel(sections, group, info, node_pre, part_own, part_other, weights, turned_first, out):
    @pl.when(takes_part(info, sections, group))
    def _():
        count = part_own.shape[0]
        agg = (part_own[...].astype(F32) + part_other[...].astype(F32)).astype(BF)
        pre = node_pre[...] + matmul(agg, weights[AGG])
        sigma = jax.nn.sigmoid(pre)
        out[:count] = agg
        out[count : 2 * count] = (pre * sigma).astype(BF)
        out[2 * count :] = slope_of(pre, sigma)


def chain_kernel(span, batches, chunk, first, active, info, *refs):
    several = span + 1 if first else 2
    incoming, refs = refs[:several], refs[several:]
    kept = ()
    if not first:
        kept, refs = refs[:2], refs[2:]

    @pl.when(info[0] == active)
    def _():
        chain_step(span, batches, chunk, first, info, incoming, *refs)

    if kept:

        @pl.when(info[0] != active)
        def _():
            refs[5][...] = kept[0][...]
            refs[6][...] = kept[1][...]


def chain_step(
    span, batches, chunk, first, info, incoming, hot, hots, slope, node_pack, turned, pay, keep, part_out, *rest
):
    member = info[1]
    batch = own_batch(member, span, batches)
    half = lax.div(member, span)
    total = slope.shape[0]
    if first:
        top_nodes, pieces = incoming[0], incoming[1:]
        came = rest[-1]
        count = total // span
        for step, piece in enumerate(pieces):
            came[step * count : (step + 1) * count] = piece[:count]
        grad = top_nodes[batch]
    else:
        came, other = incoming
        if came.shape[0] == total:
            grad = other[...]
        else:
            grad = (came[total:].astype(F32) + other[...].astype(F32)).astype(BF)
    node_count = part_out.shape[0]
    node_at = 2 * total
    delta = (matmul(grad, turned[OUT]) * node_pack[2 * node_count :].astype(F32)).astype(BF)
    agg_grad = matmul(delta, turned[AGG]).astype(BF)
    keep[node_at : node_at + node_count] = delta
    keep[node_at + node_count : node_at + 2 * node_count] = grad
    for at in range(0, total, chunk):
        run = slice(at, at + chunk)
        before = came[run].astype(F32)
        message_grad = (before + matmul(hot[run], agg_grad)).astype(BF)
        keep[run] = message_grad
        edge_delta = (matmul(message_grad, turned[MSG]) * slope[run].astype(F32)).astype(BF)
        keep[total + at : total + at + chunk] = edge_delta
        below = (before + matmul(edge_delta, turned[EDGE])).astype(BF)
        pay[run] = below
        if rest and not first:
            rest[0][run] = below
    sums = matmul(hots[...], keep[total : 2 * total]).astype(BF)
    keep[node_at + 2 * node_count :] = sums
    own = grad.astype(F32) + matmul(delta, turned[NODE])
    own = own * jnp.where(half == 0, 1.0, 0.0)
    part = matmul(sums[:node_count], turned[SEND]) + matmul(sums[node_count:], turned[RECV])
    part = (own + part).astype(BF)
    pay[total:] = part
    part_out[...] = part


def grads_kernel(span, batches, groups, sections, info, *refs):
    for group in range(2):

        @pl.when(takes_part(info, sections, group))
        def _(group=group):
            grads_step(span, batches, groups, info, *refs[3 * group : 3 * group + 3], *refs[6:])


def grads_step(span, batches, groups, info, edges_turned, act_turned, node_pack, feats_turned, keep, pay, *refs):
    near, far = refs[:span], refs[span : 2 * span]
    sums = refs[2 * span]
    member = info[1]
    half = lax.div(member, span)
    offset = lax.rem(member, span)
    batch = own_batch(member, span, batches)
    total = edges_turned.shape[1]
    node_count = feats_turned.shape[1]
    width = feats_turned.shape[0]
    count = total // span
    node_at = 2 * total
    delta = keep[node_at : node_at + node_count]
    grad = keep[node_at + node_count : node_at + 2 * node_count]
    sums[0] = matmul(feats_turned[...], keep[node_at + 2 * node_count : node_at + 3 * node_count]).astype(BF)
    sums[1] = matmul(feats_turned[...], keep[node_at + 3 * node_count :]).astype(BF)
    sums[2] = matmul(edges_turned[...], keep[total : 2 * total]).astype(BF)
    sums[3] = matmul(act_turned[...], keep[:total]).astype(BF)
    sums[5] = transposed_times(node_pack[:node_count], delta).astype(BF)

    @pl.when(half == 0)
    def _():
        sums[4] = matmul(feats_turned[...], delta).astype(BF)

    @pl.when(half != 0)
    def _():
        sums[4] = transposed_times(node_pack[node_count : 2 * node_count], grad).astype(BF)

    share = width // groups
    node_share = node_count // groups

    def fill(block, start, owner):
        at = pl.multiple_of(owner * share, share)
        for slot in range(5):
            block[start + slot * share : start + (slot + 1) * share] = sums[slot, pl.ds(at, share)]
        at_half = pl.multiple_of(owner * share + half * (share // 2), share // 2)
        block[start + 5 * share : start + 5 * share + share // 2] = sums[5, pl.ds(at_half, share // 2)]
        at_node = pl.multiple_of(total + owner * node_share, node_share)
        block[start + 5 * share + share // 2 :] = pay[pl.ds(at_node, node_share)]

    for step in range(span):
        near[step][:count] = pay[step * count : (step + 1) * count]
        fill(near[step], count, half * span + lax.rem(offset + step, span))
        fill(far[step], 0, (1 - half) * span + lax.rem(batch + step, span))


def finish_kernel(span, batches, groups, info, *refs):
    near, far = refs[:span], refs[span : 2 * span]
    refs = refs[2 * span :]
    nodes_out, edges_out, send_out, recv_out, edge_out, msg_out, node_out, agg_out, out_out = refs[:9]
    held = refs[9]
    member = info[1]
    half = lax.div(member, span)
    offset = lax.rem(member, span)
    count = edges_out.shape[2]
    for batch in range(batches):
        turn = lax.rem(offset - base_of(half, span, batches) - batch + 2 * span, span)
        turn_far = lax.rem(offset - batch + span, span)
        for step in range(span):

            @pl.when(turn == step)
            def _(step=step, batch=batch):
                edges_out[0, batch] = near[step][:count]
                held[batch, half] = near[step][count:]

            @pl.when(turn_far == step)
            def _(step=step, batch=batch):
                held[batch, 1 - half] = far[step][...]

    share = send_out.shape[1]
    for slot, out in enumerate((send_out, recv_out, edge_out, msg_out)):
        rows = slice(slot * share, (slot + 1) * share)
        value = None
        for batch in range(batches):
            for part in range(PARTS):
                piece = held[batch, part, rows].astype(F32)
                value = piece if value is None else value + piece
        out[0] = value

    def over_batches(part, start, length):
        value = None
        for batch in range(batches):
            piece = held[batch, part, start : start + length].astype(F32)
            value = piece if value is None else value + piece
        return value

    node_out[0] = over_batches(0, 4 * share, share)
    out_out[0] = over_batches(1, 4 * share, share)
    for part in range(PARTS):
        agg_out[0, part * (share // 2) : (part + 1) * (share // 2)] = over_batches(part, 5 * share, share // 2)
    at = 5 * share + share // 2
    for batch in range(batches):
        rows = held[batch, 0, at:].astype(F32) + held[batch, 1, at:].astype(F32)
        nodes_out[0, batch] = rows.astype(BF)


def call(kernel, name, in_specs, out_shapes, scratch, flops, touched, aliases={}, grant=GRANT):
    many = isinstance(out_shapes, list)
    return pl.pallas_call(
        kernel,
        name=name,
        out_shape=out_shapes,
        in_specs=in_specs,
        out_specs=[VMEM] * len(out_shapes) if many else VMEM,
        scratch_shapes=scratch,
        input_output_aliases=aliases,
        compiler_params=pltpu.CompilerParams(vmem_limit_bytes=grant * 2**20),
        cost_estimate=pl.CostEstimate(flops=flops, bytes_accessed=touched, transcendentals=0),
    )


def body(
    layer_nodes,
    layer_edges,
    top_nodes,
    top_edges,
    tile_blocks,
    senders,
    receivers,
    w_send,
    w_recv,
    w_edge,
    w_msg,
    w_node,
    w_agg,
    w_out,
):
    sections = lax.axis_size("section")
    groups = lax.axis_size("edge")
    section = lax.axis_index("section")
    member = lax.axis_index("edge")
    span = groups // PARTS
    _, batches, node_count, width = layer_nodes.shape
    count = layer_edges.shape[2]
    total = span * count
    chunk = 2 * count
    share = width // groups
    node_share = node_count // groups
    info = jnp.stack([section, member]).astype(jnp.int32)
    axes = ("section", "edge")
    works = [(m, h) for h in range(PARTS) for m in range(batches)]

    def worker(m, h):
        return worker_of(m, h, span, batches)

    def source(m, h, step):
        return h * span + (place_of(m, h, span, batches) + step) % span

    def move(value, layers, links, shift=0):
        pairs = [(s * groups + a, (s + shift) * groups + b) for s in layers for a, b in links]
        return lax.ppermute(value, axes, pairs)

    every = list(range(sections))
    last = [sections - 1]
    collect = [[(source(m, h, step), worker(m, h)) for m, h in works] for step in range(span)]
    deliver = [[(b, a) for a, b in links] for links in collect]

    def like(rows, cols=width, kind=BF):
        return jax.ShapeDtypeStruct((rows, cols), kind)

    packed = call(
        functools.partial(pack_kernel, span, batches, sections),
        "pack",
        [SMEM, VMEM, VMEM, SMEM, VMEM, VMEM],
        [like(count + PAD), like(count)] + [like(count + PAD)] * (2 * span - 2),
        [],
        0,
        2**20,
    )(info, senders, receivers, tile_blocks, layer_edges, top_edges)
    own, own_top, first_out, second_out = packed[0], packed[1], packed[2 : span + 1], packed[span + 1 :]
    groups_of = [list(range(sections - 1 - group, -1, -2)) for group in range(2)]
    first_in = [move(piece, groups_of[0], collect[step + 1]) for step, piece in enumerate(first_out)]
    own, w_send, w_recv, w_edge, w_msg, w_node, w_agg, w_out = lax.optimization_barrier(
        (own, w_send, w_recv, w_edge, w_msg, w_node, w_agg, w_out)
    )
    weights = jnp.concatenate([w_send, w_recv, w_edge, w_msg, w_node, w_agg, w_out], axis=0)
    ready = call(
        functools.partial(ready_kernel, span, batches),
        "ready",
        [SMEM, VMEM, VMEM],
        [
            jax.ShapeDtypeStruct((7, width, width), BF),
            like(2 * node_count),
            like(node_count, kind=F32),
            like(width, node_count),
        ],
        [],
        4 * 10**8,
        10 * 2**20,
    )(info, layer_nodes, weights)
    turned, hidden, node_pre, feats_turned = ready
    first_in[0], second_out = lax.optimization_barrier((first_in[0], second_out))
    second_in = [move(piece, groups_of[1] + last, collect[step + 1]) for step, piece in enumerate(second_out)]

    swap = [(worker(m, h), worker(m, 1 - h)) for m, h in works]
    stages, after = [], []
    for group, arrived in enumerate((first_in, second_in)):
        act, slope, part, hot, hots, pieces = call(
            functools.partial(forward_kernel, span, chunk, sections, group),
            "forward",
            [SMEM] + [VMEM] * (span + 2),
            [like(total), like(total), like(node_count), like(total, node_count), like(2 * node_count, total)]
            + [like(total)],
            [pltpu.VMEM((total, 2 * node_count), BF)],
            2 * 10**9,
            6 * 2**20,
        )(info, own, *arrived, hidden, weights)
        part_other = move(part, groups_of[group], swap)
        edges_turned, act_turned = call(
            functools.partial(turn_kernel, sections, group),
            "turn",
            [SMEM] + [VMEM] * 2,
            [like(width, total), like(width, total)],
            [],
            0,
            4 * 2**20,
        )(info, pieces, act)
        node_pack = call(
            functools.partial(node_kernel, sections, group),
            "node_forward",
            [SMEM] + [VMEM] * 4 + [ANY],
            like(3 * node_count),
            [],
            10**5,
            2**10,
        )(info, node_pre, part, part_other, weights, edges_turned)
        stages.append((hot, hots, slope, node_pack))
        after += [edges_turned, act_turned, node_pack]

    both_ways = [(worker(m, h), worker(m, h)) for m, h in works]
    rows = 5 * share + share // 2 + node_share
    pay = keep = None
    incoming = None
    for moment in range(sections):
        first = moment == 0
        layer = sections - 1 - moment
        split = layer > 0 and layer % 2 == 0
        inputs = (top_nodes, own_top, *second_in) if first else (*incoming, pay, keep)
        made = call(
            functools.partial(chain_kernel, span, batches, chunk, first, layer),
            "chain",
            [SMEM] + [VMEM] * (len(inputs) + 5),
            [like(total + node_count), like(2 * total + 4 * node_count), like(node_count)] + [like(total)] * split,
            [pltpu.VMEM((total, width), BF)] if first else [],
            3 * 10**9,
            10 * 2**20,
            {} if first else {3: 0, 4: 1},
        )(info, *inputs, *stages[moment % 2], turned)
        pay, keep, part = made[:3]
        if split:
            came = move(made[3], [layer], both_ways, -1)
            summed = part.astype(F32) + move(part, [layer], swap).astype(F32)
            incoming = (came, move(summed.astype(BF), [layer], both_ways, -1))
        elif layer > 0:
            cross = move(part, [layer], swap, -1)
            came = move(pay, [layer], both_ways, -1)
            incoming = (came, cross)

    out = call(
        functools.partial(grads_kernel, span, batches, groups, sections),
        "weight_grads",
        [SMEM] + [VMEM] * 9,
        [like(count + rows)] * span + [like(rows)] * span,
        [pltpu.VMEM((6, width, width), BF)],
        2 * 10**9,
        10 * 2**20,
    )(info, *after, feats_turned, keep, pay)
    across = [[(worker(m, h), (1 - h) * span + (m + step) % span) for m, h in works] for step in range(span)]
    far = [move(block, every, across[step]) for step, block in enumerate(out[span:])]
    near = [out[0]] + [move(out[step], every, deliver[step]) for step in range(1, span)]
    grad_shape = jax.ShapeDtypeStruct((1, share, width), F32)
    return call(
        functools.partial(finish_kernel, span, batches, groups),
        "finish",
        [SMEM] + [VMEM] * (2 * span),
        [
            jax.ShapeDtypeStruct((1, batches, node_share, width), BF),
            jax.ShapeDtypeStruct((1, batches, count, width), BF),
        ]
        + [grad_shape] * 7,
        [pltpu.VMEM((batches, PARTS, rows, width), BF)],
        0,
        5 * 2**20,
    )(info, *near, *far)


def solution(mesh):
    in_specs = (
        P("section", None, None, None),
        P("section", None, "edge", None),
        P(),
        P(None, "edge", None),
        P(None, "edge", None),
        P(None, "edge"),
        P(None, "edge"),
        P("section", None, None),
        P("section", None, None),
        P("section", None, None),
        P("section", None, None),
        P("section", None, None),
        P("section", None, None),
        P("section", None, None),
    )
    out_specs = (
        P("section", None, "edge", None),
        P("section", None, "edge", None),
        P("section", "edge", None),
        P("section", "edge", None),
        P("section", "edge", None),
        P("section", "edge", None),
        P("section", "edge", None),
        P("section", "edge", None),
        P("section", "edge", None),
    )
    return jax.shard_map(body, mesh=mesh, in_specs=in_specs, out_specs=out_specs, check_vma=False)
```

```python
import functools

import jax
import jax.numpy as jnp
from jax import lax
from jax.experimental import pallas as pl
from jax.experimental.pallas import tpu as pltpu
from jax.sharding import PartitionSpec as P

BLOCK = 128
PARTS = 2
PAD = 16
SEND, RECV, EDGE, MSG, NODE, AGG, OUT = range(7)
GRANT = 32
BF = jnp.bfloat16
F32 = jnp.float32
ANY = pl.BlockSpec(memory_space=pl.ANY)
SMEM = pl.BlockSpec(memory_space=pltpu.SMEM)
VMEM = pl.BlockSpec(memory_space=pltpu.VMEM)


def matmul(left, right):
    return jnp.dot(left, right, preferred_element_type=F32)


def times_transposed(left, right):
    return lax.dot_general(left, right, (((1,), (1,)), ((), ())), preferred_element_type=F32)


def transposed_times(left, right):
    return lax.dot_general(left, right, (((0,), (0,)), ((), ())), preferred_element_type=F32)


def base_of(half, span, batches):
    return jnp.where(half == 0, span - batches, 0)


def place_of(batch, half, span, batches):
    return (span - batches if half == 0 else 0) + batch


def worker_of(batch, half, span, batches):
    return half * span + place_of(batch, half, span, batches)


def own_batch(member, span, batches):
    half = lax.div(member, span)
    batch = lax.rem(member, span) - base_of(half, span, batches)
    return jnp.clip(batch, 0, batches - 1)


def pick_row(table, row, lanes):
    value = table[0:1, lanes]
    for other in range(1, table.shape[0]):
        value = jnp.where(row == other, table[other : other + 1, lanes], value)
    return value


def hot_rows(index_rows, row, nodes):
    index = index_rows[row : row + 1, :].astype(F32).astype(jnp.int32)
    rows = lax.broadcasted_iota(jnp.int32, (nodes, index_rows.shape[1]), 0)
    return jnp.where(rows == index, 1.0, 0.0).astype(BF)


def hot_columns(index_rows, row, nodes):
    pick = lax.broadcasted_iota(jnp.int32, (index_rows.shape[0], nodes), 0) == row
    index = transposed_times(index_rows, jnp.where(pick, 1.0, 0.0).astype(BF))
    columns = lax.broadcasted_iota(jnp.int32, index.shape, 1).astype(F32)
    return jnp.where(columns == index, 1.0, 0.0).astype(BF)


def slope_of(pre, sigma):
    return (sigma * (1.0 + pre * (1.0 - sigma))).astype(BF)


def pack_kernel(span, batches, sections, info, senders, receivers, tiles, edges, tops, *refs):
    own, own_top = refs[:2]
    outs, seconds = refs[2 : span + 1], refs[span + 1 :]
    member = info[1]
    half = lax.div(member, span)
    offset = lax.rem(member, span)
    count = senders.shape[1]
    tile_count = tiles.shape[1]
    tile_len = count // tile_count
    top = info[0] == sections - 1
    for step in range(span):
        batch = lax.rem(offset - step + span, span) - base_of(half, span, batches)
        batch = jnp.clip(batch, 0, batches - 1)
        out = outs[step - 1] if step else own
        out[:count] = edges[0, batch]
        out[count:] = jnp.zeros((PAD, out.shape[1]), BF)
        for tile in range(tile_count):
            lanes = slice(tile * tile_len, (tile + 1) * tile_len)
            send = pick_row(senders, batch, lanes) + tiles[batch, tile, 0] * BLOCK
            recv = pick_row(receivers, batch, lanes) + tiles[batch, tile, 1] * BLOCK
            which = lax.broadcasted_iota(jnp.int32, (PAD, tile_len), 0)
            block = jnp.where(which == 0, send, jnp.where(which == 1, recv, 0))
            out[count:, lanes] = block.astype(F32).astype(BF)
        if step:
            second = seconds[step - 1]
            second[count:] = out[count:]

            @pl.when(top)
            def _(second=second, batch=batch):
                second[:count] = tops[batch]

            @pl.when(jnp.logical_not(top))
            def _(second=second, out=out):
                second[:count] = out[:count]

        else:
            own_top[...] = tops[batch]


def ready_kernel(span, batches, info, nodes, weights, turned, hidden, node_pre, feats_turned):
    batch = own_batch(info[1], span, batches)
    node_count = nodes.shape[2]
    feats = nodes[0, batch]
    hidden[:node_count] = matmul(feats, weights[SEND]).astype(BF)
    hidden[node_count:] = matmul(feats, weights[RECV]).astype(BF)
    node_pre[...] = matmul(feats, weights[NODE])
    feats_turned[...] = feats.T
    for slot in range(weights.shape[0]):
        turned[slot] = weights[slot].T


def takes_part(info, sections, group):
    return lax.rem(sections - 1 - info[0], 2) == group


def forward_kernel(span, chunk, sections, group, info, *refs):
    @pl.when(takes_part(info, sections, group))
    def _():
        forward_step(span, chunk, *refs)


def forward_step(span, chunk, own, *refs):
    others = refs[: span - 1]
    hidden, weights = refs[span - 1 : span + 1]
    act_out, slope_out, part_out, hot_out, hots_out, pieces, both = refs[span + 1 :]
    count = own.shape[0] - PAD
    node_count = part_out.shape[0]
    for step in range(span):
        piece = others[step - 1] if step else own
        run = slice(step * count, (step + 1) * count)
        pieces[run] = piece[:count]
        index_rows = piece[count:, :count]
        hots_out[:node_count, run] = hot_rows(index_rows, 0, node_count)
        hots_out[node_count:, run] = hot_rows(index_rows, 1, node_count)
        both[run, :node_count] = hot_columns(index_rows, 0, node_count)
        recv_hot = hot_columns(index_rows, 1, node_count)
        both[run, node_count:] = recv_hot
        hot_out[run] = recv_hot
    for at in range(0, span * count, chunk):
        run = slice(at, at + chunk)
        pre = matmul(both[run], hidden[...]) + matmul(pieces[run], weights[EDGE])
        sigma = jax.nn.sigmoid(pre)
        act_out[run] = (pre * sigma).astype(BF)
        slope_out[run] = slope_of(pre, sigma)
    total = matmul(hots_out[node_count:], act_out[...])
    part_out[...] = matmul(total.astype(BF), weights[MSG]).astype(BF)


def turn_kernel(sections, group, info, pieces, act, edges_turned, act_turned):
    @pl.when(takes_part(info, sections, group))
    def _():
        rows = 2 * BLOCK
        for at in range(0, act.shape[0], rows):
            run = slice(at, at + rows)
            edges_turned[:, run] = pieces[run].T
            act_turned[:, run] = act[run].T


def node_kernel(sections, group, info, node_pre, part_own, part_other, weights, turned_first, out):
    @pl.when(takes_part(info, sections, group))
    def _():
        count = part_own.shape[0]
        agg = (part_own[...].astype(F32) + part_other[...].astype(F32)).astype(BF)
        pre = node_pre[...] + matmul(agg, weights[AGG])
        sigma = jax.nn.sigmoid(pre)
        out[:count] = agg
        out[count : 2 * count] = (pre * sigma).astype(BF)
        out[2 * count :] = slope_of(pre, sigma)


def chain_kernel(span, batches, chunk, first, active, info, *refs):
    several = span + 1 if first else 2
    incoming, refs = refs[:several], refs[several:]
    kept = ()
    if len(refs) > 8 and not first:
        kept, refs = refs[:2], refs[2:]

    @pl.when(info[0] == active)
    def _():
        chain_step(span, batches, chunk, first, info, incoming, *refs)

    if kept:

        @pl.when(info[0] != active)
        def _():
            refs[5][...] = kept[0][...]
            refs[6][...] = kept[1][...]


def chain_step(
    span, batches, chunk, first, info, incoming, hot, hots, slope, node_pack, turned, pay, keep, part_out, *rest
):
    member = info[1]
    batch = own_batch(member, span, batches)
    half = lax.div(member, span)
    total = slope.shape[0]
    if first:
        top_nodes, pieces = incoming[0], incoming[1:]
        came = rest[-1]
        count = total // span
        for step, piece in enumerate(pieces):
            came[step * count : (step + 1) * count] = piece[:count]
        grad = top_nodes[batch]
    else:
        came, other = incoming
        if came.shape[0] == total:
            grad = other[...]
        else:
            grad = (came[total:].astype(F32) + other[...].astype(F32)).astype(BF)
    node_count = part_out.shape[0]
    node_at = 2 * total
    delta = (matmul(grad, turned[OUT]) * node_pack[2 * node_count :].astype(F32)).astype(BF)
    agg_grad = matmul(delta, turned[AGG]).astype(BF)
    keep[node_at : node_at + node_count] = delta
    keep[node_at + node_count : node_at + 2 * node_count] = grad
    for at in range(0, total, chunk):
        run = slice(at, at + chunk)
        before = came[run].astype(F32)
        message_grad = (before + matmul(hot[run], agg_grad)).astype(BF)
        keep[run] = message_grad
        edge_delta = (matmul(message_grad, turned[MSG]) * slope[run].astype(F32)).astype(BF)
        keep[total + at : total + at + chunk] = edge_delta
        below = (before + matmul(edge_delta, turned[EDGE])).astype(BF)
        pay[run] = below
        if rest and not first:
            rest[0][run] = below
    sums = matmul(hots[...], keep[total : 2 * total]).astype(BF)
    keep[node_at + 2 * node_count :] = sums
    own = grad.astype(F32) + matmul(delta, turned[NODE])
    own = own * jnp.where(half == 0, 1.0, 0.0)
    part = matmul(sums[:node_count], turned[SEND]) + matmul(sums[node_count:], turned[RECV])
    part = (own + part).astype(BF)
    pay[total:] = part
    part_out[...] = part


def grads_kernel(span, batches, groups, sections, low, high, info, *refs):
    for group in range(2):

        @pl.when(takes_part(info, sections, group) & (info[0] >= low) & (info[0] < high))
        def _(group=group):
            grads_step(span, batches, groups, info, *refs[3 * group : 3 * group + 3], *refs[6:])


def grads_step(span, batches, groups, info, edges_turned, act_turned, node_pack, feats_turned, keep, pay, *refs):
    near, far = refs[:span], refs[span : 2 * span]
    sums = refs[2 * span]
    member = info[1]
    half = lax.div(member, span)
    offset = lax.rem(member, span)
    batch = own_batch(member, span, batches)
    total = edges_turned.shape[1]
    node_count = feats_turned.shape[1]
    width = feats_turned.shape[0]
    count = total // span
    node_at = 2 * total
    delta = keep[node_at : node_at + node_count]
    grad = keep[node_at + node_count : node_at + 2 * node_count]
    sums[0] = matmul(feats_turned[...], keep[node_at + 2 * node_count : node_at + 3 * node_count]).astype(BF)
    sums[1] = matmul(feats_turned[...], keep[node_at + 3 * node_count :]).astype(BF)
    sums[2] = matmul(edges_turned[...], keep[total : 2 * total]).astype(BF)
    sums[3] = matmul(act_turned[...], keep[:total]).astype(BF)
    sums[5] = transposed_times(node_pack[:node_count], delta).astype(BF)

    @pl.when(half == 0)
    def _():
        sums[4] = matmul(feats_turned[...], delta).astype(BF)

    @pl.when(half != 0)
    def _():
        sums[4] = transposed_times(node_pack[node_count : 2 * node_count], grad).astype(BF)

    share = width // groups
    node_share = node_count // groups

    def fill(block, start, owner):
        at = pl.multiple_of(owner * share, share)
        for slot in range(5):
            block[start + slot * share : start + (slot + 1) * share] = sums[slot, pl.ds(at, share)]
        at_half = pl.multiple_of(owner * share + half * (share // 2), share // 2)
        block[start + 5 * share : start + 5 * share + share // 2] = sums[5, pl.ds(at_half, share // 2)]
        at_node = pl.multiple_of(total + owner * node_share, node_share)
        block[start + 5 * share + share // 2 :] = pay[pl.ds(at_node, node_share)]

    for step in range(span):
        near[step][:count] = pay[step * count : (step + 1) * count]
        fill(near[step], count, half * span + lax.rem(offset + step, span))
        fill(far[step], 0, (1 - half) * span + lax.rem(batch + step, span))


def finish_kernel(span, batches, groups, info, *refs):
    sets = (refs[: 2 * span], refs[2 * span : 4 * span])
    refs = refs[4 * span :]
    nodes_out, edges_out, send_out, recv_out, edge_out, msg_out, node_out, agg_out, out_out = refs[:9]
    held = refs[9]
    member = info[1]
    half = lax.div(member, span)
    offset = lax.rem(member, span)
    count = edges_out.shape[2]
    for which in range(2):

        @pl.when((info[0] == 0) == (which == 1))
        def _(which=which):
            near, far = sets[which][:span], sets[which][span:]
            for batch in range(batches):
                turn = lax.rem(offset - base_of(half, span, batches) - batch + 2 * span, span)
                turn_far = lax.rem(offset - batch + span, span)
                for step in range(span):

                    @pl.when(turn == step)
                    def _(step=step, batch=batch):
                        edges_out[0, batch] = near[step][:count]
                        held[batch, half] = near[step][count:]

                    @pl.when(turn_far == step)
                    def _(step=step, batch=batch):
                        held[batch, 1 - half] = far[step][...]

    share = send_out.shape[1]
    for slot, out in enumerate((send_out, recv_out, edge_out, msg_out)):
        rows = slice(slot * share, (slot + 1) * share)
        value = None
        for batch in range(batches):
            for part in range(PARTS):
                piece = held[batch, part, rows].astype(F32)
                value = piece if value is None else value + piece
        out[0] = value

    def over_batches(part, start, length):
        value = None
        for batch in range(batches):
            piece = held[batch, part, start : start + length].astype(F32)
            value = piece if value is None else value + piece
        return value

    node_out[0] = over_batches(0, 4 * share, share)
    out_out[0] = over_batches(1, 4 * share, share)
    for part in range(PARTS):
        agg_out[0, part * (share // 2) : (part + 1) * (share // 2)] = over_batches(part, 5 * share, share // 2)
    at = 5 * share + share // 2
    for batch in range(batches):
        rows = held[batch, 0, at:].astype(F32) + held[batch, 1, at:].astype(F32)
        nodes_out[0, batch] = rows.astype(BF)


def call(kernel, name, in_specs, out_shapes, scratch, flops, touched, aliases={}, grant=GRANT):
    many = isinstance(out_shapes, list)
    return pl.pallas_call(
        kernel,
        name=name,
        out_shape=out_shapes,
        in_specs=in_specs,
        out_specs=[VMEM] * len(out_shapes) if many else VMEM,
        scratch_shapes=scratch,
        input_output_aliases=aliases,
        compiler_params=pltpu.CompilerParams(vmem_limit_bytes=grant * 2**20),
        cost_estimate=pl.CostEstimate(flops=flops, bytes_accessed=touched, transcendentals=0),
    )


def body(
    layer_nodes,
    layer_edges,
    top_nodes,
    top_edges,
    tile_blocks,
    senders,
    receivers,
    w_send,
    w_recv,
    w_edge,
    w_msg,
    w_node,
    w_agg,
    w_out,
):
    sections = lax.axis_size("section")
    groups = lax.axis_size("edge")
    section = lax.axis_index("section")
    member = lax.axis_index("edge")
    span = groups // PARTS
    _, batches, node_count, width = layer_nodes.shape
    count = layer_edges.shape[2]
    total = span * count
    chunk = 2 * count
    share = width // groups
    node_share = node_count // groups
    info = jnp.stack([section, member]).astype(jnp.int32)
    axes = ("section", "edge")
    works = [(m, h) for h in range(PARTS) for m in range(batches)]

    def worker(m, h):
        return worker_of(m, h, span, batches)

    def source(m, h, step):
        return h * span + (place_of(m, h, span, batches) + step) % span

    def move(value, layers, links, shift=0):
        pairs = [(s * groups + a, (s + shift) * groups + b) for s in layers for a, b in links]
        return lax.ppermute(value, axes, pairs)

    every = list(range(sections))
    last = [sections - 1]
    collect = [[(source(m, h, step), worker(m, h)) for m, h in works] for step in range(span)]
    deliver = [[(b, a) for a, b in links] for links in collect]

    def like(rows, cols=width, kind=BF):
        return jax.ShapeDtypeStruct((rows, cols), kind)

    packed = call(
        functools.partial(pack_kernel, span, batches, sections),
        "pack",
        [SMEM, VMEM, VMEM, SMEM, VMEM, VMEM],
        [like(count + PAD), like(count)] + [like(count + PAD)] * (2 * span - 2),
        [],
        0,
        2**20,
    )(info, senders, receivers, tile_blocks, layer_edges, top_edges)
    own, own_top, first_out, second_out = packed[0], packed[1], packed[2 : span + 1], packed[span + 1 :]
    groups_of = [list(range(sections - 1 - group, -1, -2)) for group in range(2)]
    first_in = [move(piece, groups_of[0], collect[step + 1]) for step, piece in enumerate(first_out)]
    own, w_send, w_recv, w_edge, w_msg, w_node, w_agg, w_out = lax.optimization_barrier(
        (own, w_send, w_recv, w_edge, w_msg, w_node, w_agg, w_out)
    )
    weights = jnp.concatenate([w_send, w_recv, w_edge, w_msg, w_node, w_agg, w_out], axis=0)
    ready = call(
        functools.partial(ready_kernel, span, batches),
        "ready",
        [SMEM, VMEM, VMEM],
        [
            jax.ShapeDtypeStruct((7, width, width), BF),
            like(2 * node_count),
            like(node_count, kind=F32),
            like(width, node_count),
        ],
        [],
        4 * 10**8,
        10 * 2**20,
    )(info, layer_nodes, weights)
    turned, hidden, node_pre, feats_turned = ready
    first_in[0], second_out = lax.optimization_barrier((first_in[0], second_out))
    second_in = [move(piece, groups_of[1] + last, collect[step + 1]) for step, piece in enumerate(second_out)]

    swap = [(worker(m, h), worker(m, 1 - h)) for m, h in works]
    stages, after = [], []
    for group, arrived in enumerate((first_in, second_in)):
        act, slope, part, hot, hots, pieces = call(
            functools.partial(forward_kernel, span, chunk, sections, group),
            "forward",
            [SMEM] + [VMEM] * (span + 2),
            [like(total), like(total), like(node_count), like(total, node_count), like(2 * node_count, total)]
            + [like(total)],
            [pltpu.VMEM((total, 2 * node_count), BF)],
            2 * 10**9,
            6 * 2**20,
        )(info, own, *arrived, hidden, weights)
        part_other = move(part, groups_of[group], swap)
        edges_turned, act_turned = call(
            functools.partial(turn_kernel, sections, group),
            "turn",
            [SMEM] + [VMEM] * 2,
            [like(width, total), like(width, total)],
            [],
            0,
            4 * 2**20,
        )(info, pieces, act)
        node_pack = call(
            functools.partial(node_kernel, sections, group),
            "node_forward",
            [SMEM] + [VMEM] * 4 + [ANY],
            like(3 * node_count),
            [],
            10**5,
            2**10,
        )(info, node_pre, part, part_other, weights, edges_turned)
        stages.append((hot, hots, slope, node_pack))
        after += [edges_turned, act_turned, node_pack]

    both_ways = [(worker(m, h), worker(m, h)) for m, h in works]
    rows = 5 * share + share // 2 + node_share
    pay = keep = None
    incoming = None
    across = [[(worker(m, h), (1 - h) * span + (m + step) % span) for m, h in works] for step in range(span)]

    def weight_grads(low, high, keep, pay):
        out = call(
            functools.partial(grads_kernel, span, batches, groups, sections, low, high),
            "weight_grads",
            [SMEM] + [VMEM] * 9,
            [like(count + rows)] * span + [like(rows)] * span,
            [pltpu.VMEM((6, width, width), BF)],
            2 * 10**10,
            100 * 2**20,
        )(info, *after, feats_turned, keep, pay)
        layers = list(range(low, high))
        far = [move(block, layers, across[step]) for step, block in enumerate(out[span:])]
        near = [out[0]] + [move(out[step], layers, deliver[step]) for step in range(1, span)]
        return near + far

    sets = []
    for moment in range(sections):
        first = moment == 0
        layer = sections - 1 - moment
        split = layer > 0 and layer % 2 == 0
        in_place = 0 < moment < sections - 1
        inputs = (top_nodes, own_top, *second_in) if first else incoming
        if in_place:
            inputs = (*inputs, pay, keep)
        made = call(
            functools.partial(chain_kernel, span, batches, chunk, first, layer),
            "chain",
            [SMEM] + [VMEM] * (len(inputs) + 5),
            [like(total + node_count), like(2 * total + 4 * node_count), like(node_count)] + [like(total)] * split,
            [pltpu.VMEM((total, width), BF)] if first else [],
            3 * 10**9,
            10 * 2**20,
            {3: 0, 4: 1} if in_place else {},
        )(info, *inputs, *stages[moment % 2], turned)
        pay, keep, part = made[:3]
        if split:
            came = move(made[3], [layer], both_ways, -1)
            summed = part.astype(F32) + move(part, [layer], swap).astype(F32)
            incoming = (came, move(summed.astype(BF), [layer], both_ways, -1))
        elif layer > 0:
            cross = move(part, [layer], swap, -1)
            came = move(pay, [layer], both_ways, -1)
            incoming = (came, cross)
        if layer <= 1:
            sets.append(weight_grads(layer, sections if layer else 1, keep, pay))

    grad_shape = jax.ShapeDtypeStruct((1, share, width), F32)
    return call(
        functools.partial(finish_kernel, span, batches, groups),
        "finish",
        [SMEM] + [VMEM] * (4 * span),
        [
            jax.ShapeDtypeStruct((1, batches, node_share, width), BF),
            jax.ShapeDtypeStruct((1, batches, count, width), BF),
        ]
        + [grad_shape] * 7,
        [pltpu.VMEM((batches, PARTS, rows, width), BF)],
        0,
        5 * 2**20,
    )(info, *sets[0], *sets[1])


def solution(mesh):
    in_specs = (
        P("section", None, None, None),
        P("section", None, "edge", None),
        P(),
        P(None, "edge", None),
        P(None, "edge", None),
        P(None, "edge"),
        P(None, "edge"),
        P("section", None, None),
        P("section", None, None),
        P("section", None, None),
        P("section", None, None),
        P("section", None, None),
        P("section", None, None),
        P("section", None, None),
    )
    out_specs = (
        P("section", None, "edge", None),
        P("section", None, "edge", None),
        P("section", "edge", None),
        P("section", "edge", None),
        P("section", "edge", None),
        P("section", "edge", None),
        P("section", "edge", None),
        P("section", "edge", None),
        P("section", "edge", None),
    )
    return jax.shard_map(body, mesh=mesh, in_specs=in_specs, out_specs=out_specs, check_vma=False)
```

```python
import functools

import jax
import jax.numpy as jnp
from jax import lax
from jax.experimental import pallas as pl
from jax.experimental.pallas import tpu as pltpu
from jax.sharding import PartitionSpec as P

BLOCK = 128
PARTS = 2
PAD = 16
SEND, RECV, EDGE, MSG, NODE, AGG, OUT = range(7)
GRANT = 32
BF = jnp.bfloat16
F32 = jnp.float32
ANY = pl.BlockSpec(memory_space=pl.ANY)
SMEM = pl.BlockSpec(memory_space=pltpu.SMEM)
VMEM = pl.BlockSpec(memory_space=pltpu.VMEM)


def matmul(left, right):
    return jnp.dot(left, right, preferred_element_type=F32)


def times_transposed(left, right):
    return lax.dot_general(left, right, (((1,), (1,)), ((), ())), preferred_element_type=F32)


def transposed_times(left, right):
    return lax.dot_general(left, right, (((0,), (0,)), ((), ())), preferred_element_type=F32)


def base_of(half, span, batches):
    return jnp.where(half == 0, span - batches, 0)


def place_of(batch, half, span, batches):
    return (span - batches if half == 0 else 0) + batch


def worker_of(batch, half, span, batches):
    return half * span + place_of(batch, half, span, batches)


def far_order(span):
    return sorted(range(span), key=lambda step: (1 - step % 2, step))


def near_order(span):
    return [0] + [step for step in far_order(span) if step]


def own_batch(member, span, batches):
    half = lax.div(member, span)
    batch = lax.rem(member, span) - base_of(half, span, batches)
    return jnp.clip(batch, 0, batches - 1)


def pick_row(table, row, lanes):
    value = table[0:1, lanes]
    for other in range(1, table.shape[0]):
        value = jnp.where(row == other, table[other : other + 1, lanes], value)
    return value


def hot_rows(index_rows, row, nodes):
    index = index_rows[row : row + 1, :].astype(F32).astype(jnp.int32)
    rows = lax.broadcasted_iota(jnp.int32, (nodes, index_rows.shape[1]), 0)
    return jnp.where(rows == index, 1.0, 0.0).astype(BF)


def hot_columns(index_rows, row, nodes):
    pick = lax.broadcasted_iota(jnp.int32, (index_rows.shape[0], nodes), 0) == row
    index = transposed_times(index_rows, jnp.where(pick, 1.0, 0.0).astype(BF))
    columns = lax.broadcasted_iota(jnp.int32, index.shape, 1).astype(F32)
    return jnp.where(columns == index, 1.0, 0.0).astype(BF)


def slope_of(pre, sigma):
    return (sigma * (1.0 + pre * (1.0 - sigma))).astype(BF)


def pack_kernel(span, batches, sections, info, senders, receivers, tiles, edges, tops, *refs):
    own, own_top = refs[:2]
    outs, seconds = refs[2 : span + 1], refs[span + 1 :]
    member = info[1]
    half = lax.div(member, span)
    offset = lax.rem(member, span)
    count = senders.shape[1]
    tile_count = tiles.shape[1]
    tile_len = count // tile_count
    top = info[0] == sections - 1
    for step in range(span):
        batch = lax.rem(offset - step + span, span) - base_of(half, span, batches)
        batch = jnp.clip(batch, 0, batches - 1)
        out = outs[step - 1] if step else own
        out[:count] = edges[0, batch]
        out[count:] = jnp.zeros((PAD, out.shape[1]), BF)
        for tile in range(tile_count):
            lanes = slice(tile * tile_len, (tile + 1) * tile_len)
            send = pick_row(senders, batch, lanes) + tiles[batch, tile, 0] * BLOCK
            recv = pick_row(receivers, batch, lanes) + tiles[batch, tile, 1] * BLOCK
            which = lax.broadcasted_iota(jnp.int32, (PAD, tile_len), 0)
            block = jnp.where(which == 0, send, jnp.where(which == 1, recv, 0))
            out[count:, lanes] = block.astype(F32).astype(BF)
        if step:
            second = seconds[step - 1]
            second[count:] = out[count:]

            @pl.when(top)
            def _(second=second, batch=batch):
                second[:count] = tops[batch]

            @pl.when(jnp.logical_not(top))
            def _(second=second, out=out):
                second[:count] = out[:count]

        else:
            own_top[...] = tops[batch]


def ready_kernel(span, batches, info, nodes, weights, turned, hidden, node_pre, feats_turned):
    batch = own_batch(info[1], span, batches)
    node_count = nodes.shape[2]
    feats = nodes[0, batch]
    hidden[:node_count] = matmul(feats, weights[SEND]).astype(BF)
    hidden[node_count:] = matmul(feats, weights[RECV]).astype(BF)
    node_pre[...] = matmul(feats, weights[NODE])
    feats_turned[...] = feats.T
    for slot in range(weights.shape[0]):
        turned[slot] = weights[slot].T


def takes_part(info, sections, group):
    return lax.rem(sections - 1 - info[0], 2) == group


def forward_kernel(span, chunk, sections, group, info, *refs):
    @pl.when(takes_part(info, sections, group))
    def _():
        forward_step(span, chunk, *refs)


def forward_step(span, chunk, own, *refs):
    others = refs[: span - 1]
    hidden, weights = refs[span - 1 : span + 1]
    act_out, slope_out, part_out, hot_out, hots_out, pieces, both = refs[span + 1 :]
    count = own.shape[0] - PAD
    node_count = part_out.shape[0]
    for step in range(span):
        piece = others[step - 1] if step else own
        run = slice(step * count, (step + 1) * count)
        pieces[run] = piece[:count]
        index_rows = piece[count:, :count]
        hots_out[:node_count, run] = hot_rows(index_rows, 0, node_count)
        hots_out[node_count:, run] = hot_rows(index_rows, 1, node_count)
        both[run, :node_count] = hot_columns(index_rows, 0, node_count)
        recv_hot = hot_columns(index_rows, 1, node_count)
        both[run, node_count:] = recv_hot
        hot_out[run] = recv_hot
    for at in range(0, span * count, chunk):
        run = slice(at, at + chunk)
        pre = matmul(both[run], hidden[...]) + matmul(pieces[run], weights[EDGE])
        sigma = jax.nn.sigmoid(pre)
        act_out[run] = (pre * sigma).astype(BF)
        slope_out[run] = slope_of(pre, sigma)
    total = matmul(hots_out[node_count:], act_out[...])
    part_out[...] = matmul(total.astype(BF), weights[MSG]).astype(BF)


def turn_kernel(sections, group, info, pieces, act, edges_turned, act_turned):
    @pl.when(takes_part(info, sections, group))
    def _():
        rows = 2 * BLOCK
        for at in range(0, act.shape[0], rows):
            run = slice(at, at + rows)
            edges_turned[:, run] = pieces[run].T
            act_turned[:, run] = act[run].T


def node_kernel(sections, group, info, node_pre, part_own, part_other, weights, turned_first, out):
    @pl.when(takes_part(info, sections, group))
    def _():
        count = part_own.shape[0]
        agg = (part_own[...].astype(F32) + part_other[...].astype(F32)).astype(BF)
        pre = node_pre[...] + matmul(agg, weights[AGG])
        sigma = jax.nn.sigmoid(pre)
        out[:count] = agg
        out[count : 2 * count] = (pre * sigma).astype(BF)
        out[2 * count :] = slope_of(pre, sigma)


def chain_kernel(span, batches, chunk, first, active, info, *refs):
    several = span + 1 if first else 2
    incoming, refs = refs[:several], refs[several:]
    kept = ()
    if len(refs) > 8 and not first:
        kept, refs = refs[:2], refs[2:]

    @pl.when(info[0] == active)
    def _():
        chain_step(span, batches, chunk, first, info, incoming, *refs)

    if kept:

        @pl.when(info[0] != active)
        def _():
            refs[5][...] = kept[0][...]
            refs[6][...] = kept[1][...]


def chain_step(
    span, batches, chunk, first, info, incoming, hot, hots, slope, node_pack, turned, pay, keep, part_out, *rest
):
    member = info[1]
    batch = own_batch(member, span, batches)
    half = lax.div(member, span)
    total = slope.shape[0]
    if first:
        top_nodes, pieces = incoming[0], incoming[1:]
        came = rest[-1]
        count = total // span
        for step, piece in enumerate(pieces):
            came[step * count : (step + 1) * count] = piece[:count]
        grad = top_nodes[batch]
    else:
        came, other = incoming
        if came.shape[0] == total:
            grad = other[...]
        else:
            grad = (came[total:].astype(F32) + other[...].astype(F32)).astype(BF)
    node_count = part_out.shape[0]
    node_at = 2 * total
    delta = (matmul(grad, turned[OUT]) * node_pack[2 * node_count :].astype(F32)).astype(BF)
    agg_grad = matmul(delta, turned[AGG]).astype(BF)
    keep[node_at : node_at + node_count] = delta
    keep[node_at + node_count : node_at + 2 * node_count] = grad
    for at in range(0, total, chunk):
        run = slice(at, at + chunk)
        before = came[run].astype(F32)
        message_grad = (before + matmul(hot[run], agg_grad)).astype(BF)
        keep[run] = message_grad
        edge_delta = (matmul(message_grad, turned[MSG]) * slope[run].astype(F32)).astype(BF)
        keep[total + at : total + at + chunk] = edge_delta
        below = (before + matmul(edge_delta, turned[EDGE])).astype(BF)
        pay[run] = below
        if rest and not first:
            rest[0][run] = below
    sums = matmul(hots[...], keep[total : 2 * total]).astype(BF)
    keep[node_at + 2 * node_count :] = sums
    own = grad.astype(F32) + matmul(delta, turned[NODE])
    own = own * jnp.where(half == 0, 1.0, 0.0)
    part = matmul(sums[:node_count], turned[SEND]) + matmul(sums[node_count:], turned[RECV])
    part = (own + part).astype(BF)
    pay[total:] = part
    part_out[...] = part


def grads_kernel(span, batches, groups, sections, low, high, info, *refs):
    for group in range(2):

        @pl.when(takes_part(info, sections, group) & (info[0] >= low) & (info[0] < high))
        def _(group=group):
            grads_step(span, batches, groups, info, *refs[3 * group : 3 * group + 3], *refs[6:])


def grads_step(span, batches, groups, info, edges_turned, act_turned, node_pack, feats_turned, keep, pay, *refs):
    near, far = refs[:span], refs[span : 2 * span]
    sums = refs[2 * span]
    member = info[1]
    half = lax.div(member, span)
    offset = lax.rem(member, span)
    batch = own_batch(member, span, batches)
    total = edges_turned.shape[1]
    node_count = feats_turned.shape[1]
    width = feats_turned.shape[0]
    count = total // span
    node_at = 2 * total
    delta = keep[node_at : node_at + node_count]
    grad = keep[node_at + node_count : node_at + 2 * node_count]
    sums[0] = matmul(feats_turned[...], keep[node_at + 2 * node_count : node_at + 3 * node_count]).astype(BF)
    sums[1] = matmul(feats_turned[...], keep[node_at + 3 * node_count :]).astype(BF)
    sums[2] = matmul(edges_turned[...], keep[total : 2 * total]).astype(BF)
    sums[3] = matmul(act_turned[...], keep[:total]).astype(BF)
    sums[5] = transposed_times(node_pack[:node_count], delta).astype(BF)

    @pl.when(half == 0)
    def _():
        sums[4] = matmul(feats_turned[...], delta).astype(BF)

    @pl.when(half != 0)
    def _():
        sums[4] = transposed_times(node_pack[node_count : 2 * node_count], grad).astype(BF)

    share = width // groups
    node_share = node_count // groups

    def fill(block, start, owner):
        at = pl.multiple_of(owner * share, share)
        for slot in range(5):
            block[start + slot * share : start + (slot + 1) * share] = sums[slot, pl.ds(at, share)]
        at_half = pl.multiple_of(owner * share + half * (share // 2), share // 2)
        block[start + 5 * share : start + 5 * share + share // 2] = sums[5, pl.ds(at_half, share // 2)]
        at_node = pl.multiple_of(total + owner * node_share, node_share)
        block[start + 5 * share + share // 2 :] = pay[pl.ds(at_node, node_share)]

    for block, step in zip(near, near_order(span)):
        block[:count] = pay[step * count : (step + 1) * count]
        fill(block, count, half * span + lax.rem(offset + step, span))
    for block, step in zip(far, far_order(span)):
        fill(block, 0, (1 - half) * span + lax.rem(batch + step, span))


def finish_kernel(span, batches, groups, info, *refs):
    sets = (refs[: 2 * span], refs[2 * span : 4 * span])
    refs = refs[4 * span :]
    nodes_out, edges_out, send_out, recv_out, edge_out, msg_out, node_out, agg_out, out_out = refs[:9]
    held = refs[9]
    member = info[1]
    half = lax.div(member, span)
    offset = lax.rem(member, span)
    count = edges_out.shape[2]
    for which in range(2):

        @pl.when((info[0] == 0) == (which == 1))
        def _(which=which):
            near, far = sets[which][:span], sets[which][span:]
            for batch in range(batches):
                turn = lax.rem(offset - base_of(half, span, batches) - batch + 2 * span, span)
                turn_far = lax.rem(offset - batch + span, span)
                for block, step in zip(near, near_order(span)):

                    @pl.when(turn == step)
                    def _(block=block, batch=batch):
                        edges_out[0, batch] = block[:count]
                        held[batch, half] = block[count:]

                for block, step in zip(far, far_order(span)):

                    @pl.when(turn_far == step)
                    def _(block=block, batch=batch):
                        held[batch, 1 - half] = block[...]

    share = send_out.shape[1]
    for slot, out in enumerate((send_out, recv_out, edge_out, msg_out)):
        rows = slice(slot * share, (slot + 1) * share)
        value = None
        for batch in range(batches):
            for part in range(PARTS):
                piece = held[batch, part, rows].astype(F32)
                value = piece if value is None else value + piece
        out[0] = value

    def over_batches(part, start, length):
        value = None
        for batch in range(batches):
            piece = held[batch, part, start : start + length].astype(F32)
            value = piece if value is None else value + piece
        return value

    node_out[0] = over_batches(0, 4 * share, share)
    out_out[0] = over_batches(1, 4 * share, share)
    for part in range(PARTS):
        agg_out[0, part * (share // 2) : (part + 1) * (share // 2)] = over_batches(part, 5 * share, share // 2)
    at = 5 * share + share // 2
    for batch in range(batches):
        rows = held[batch, 0, at:].astype(F32) + held[batch, 1, at:].astype(F32)
        nodes_out[0, batch] = rows.astype(BF)


def call(kernel, name, in_specs, out_shapes, scratch, flops, touched, aliases={}, grant=GRANT):
    many = isinstance(out_shapes, list)
    return pl.pallas_call(
        kernel,
        name=name,
        out_shape=out_shapes,
        in_specs=in_specs,
        out_specs=[VMEM] * len(out_shapes) if many else VMEM,
        scratch_shapes=scratch,
        input_output_aliases=aliases,
        compiler_params=pltpu.CompilerParams(vmem_limit_bytes=grant * 2**20),
        cost_estimate=pl.CostEstimate(flops=flops, bytes_accessed=touched, transcendentals=0),
    )


def body(
    layer_nodes,
    layer_edges,
    top_nodes,
    top_edges,
    tile_blocks,
    senders,
    receivers,
    w_send,
    w_recv,
    w_edge,
    w_msg,
    w_node,
    w_agg,
    w_out,
):
    sections = lax.axis_size("section")
    groups = lax.axis_size("edge")
    section = lax.axis_index("section")
    member = lax.axis_index("edge")
    span = groups // PARTS
    _, batches, node_count, width = layer_nodes.shape
    count = layer_edges.shape[2]
    total = span * count
    chunk = 2 * count
    share = width // groups
    node_share = node_count // groups
    info = jnp.stack([section, member]).astype(jnp.int32)
    axes = ("section", "edge")
    works = [(m, h) for h in range(PARTS) for m in range(batches)]

    def worker(m, h):
        return worker_of(m, h, span, batches)

    def source(m, h, step):
        return h * span + (place_of(m, h, span, batches) + step) % span

    def move(value, layers, links, shift=0):
        pairs = [(s * groups + a, (s + shift) * groups + b) for s in layers for a, b in links]
        return lax.ppermute(value, axes, pairs)

    every = list(range(sections))
    last = [sections - 1]
    collect = [[(source(m, h, step), worker(m, h)) for m, h in works] for step in range(span)]
    deliver = [[(b, a) for a, b in links] for links in collect]

    def like(rows, cols=width, kind=BF):
        return jax.ShapeDtypeStruct((rows, cols), kind)

    packed = call(
        functools.partial(pack_kernel, span, batches, sections),
        "pack",
        [SMEM, VMEM, VMEM, SMEM, VMEM, VMEM],
        [like(count + PAD), like(count)] + [like(count + PAD)] * (2 * span - 2),
        [],
        0,
        2**20,
    )(info, senders, receivers, tile_blocks, layer_edges, top_edges)
    own, own_top, first_out, second_out = packed[0], packed[1], packed[2 : span + 1], packed[span + 1 :]
    groups_of = [list(range(sections - 1 - group, -1, -2)) for group in range(2)]
    first_in = [move(piece, groups_of[0], collect[step + 1]) for step, piece in enumerate(first_out)]
    own, w_send, w_recv, w_edge, w_msg, w_node, w_agg, w_out = lax.optimization_barrier(
        (own, w_send, w_recv, w_edge, w_msg, w_node, w_agg, w_out)
    )
    weights = jnp.concatenate([w_send, w_recv, w_edge, w_msg, w_node, w_agg, w_out], axis=0)
    ready = call(
        functools.partial(ready_kernel, span, batches),
        "ready",
        [SMEM, VMEM, VMEM],
        [
            jax.ShapeDtypeStruct((7, width, width), BF),
            like(2 * node_count),
            like(node_count, kind=F32),
            like(width, node_count),
        ],
        [],
        4 * 10**8,
        10 * 2**20,
    )(info, layer_nodes, weights)
    turned, hidden, node_pre, feats_turned = ready
    first_in[0], second_out = lax.optimization_barrier((first_in[0], second_out))
    second_in = [move(piece, groups_of[1] + last, collect[step + 1]) for step, piece in enumerate(second_out)]

    swap = [(worker(m, h), worker(m, 1 - h)) for m, h in works]
    stages, after = [], []
    for group, arrived in enumerate((first_in, second_in)):
        act, slope, part, hot, hots, pieces = call(
            functools.partial(forward_kernel, span, chunk, sections, group),
            "forward",
            [SMEM] + [VMEM] * (span + 2),
            [like(total), like(total), like(node_count), like(total, node_count), like(2 * node_count, total)]
            + [like(total)],
            [pltpu.VMEM((total, 2 * node_count), BF)],
            2 * 10**9,
            6 * 2**20,
        )(info, own, *arrived, hidden, weights)
        part_other = move(part, groups_of[group], swap)
        edges_turned, act_turned = call(
            functools.partial(turn_kernel, sections, group),
            "turn",
            [SMEM] + [VMEM] * 2,
            [like(width, total), like(width, total)],
            [],
            0,
            4 * 2**20,
        )(info, pieces, act)
        node_pack = call(
            functools.partial(node_kernel, sections, group),
            "node_forward",
            [SMEM] + [VMEM] * 4 + [ANY],
            like(3 * node_count),
            [],
            10**5,
            2**10,
        )(info, node_pre, part, part_other, weights, edges_turned)
        stages.append((hot, hots, slope, node_pack))
        after += [edges_turned, act_turned, node_pack]

    both_ways = [(worker(m, h), worker(m, h)) for m, h in works]
    rows = 5 * share + share // 2 + node_share
    pay = keep = None
    incoming = None
    across = [[(worker(m, h), (1 - h) * span + (m + step) % span) for m, h in works] for step in range(span)]

    def weight_grads(low, high, keep, pay):
        out = call(
            functools.partial(grads_kernel, span, batches, groups, sections, low, high),
            "weight_grads",
            [SMEM] + [VMEM] * 9,
            [like(count + rows)] * span + [like(rows)] * span,
            [pltpu.VMEM((6, width, width), BF)],
            2 * 10**10,
            100 * 2**20,
        )(info, *after, feats_turned, keep, pay)
        layers = list(range(low, high))
        far = [move(block, layers, across[step]) for block, step in zip(out[span:], far_order(span))]
        near = [out[0]]
        near += [move(block, layers, deliver[step]) for block, step in zip(out[1:span], near_order(span)[1:])]
        return near + far

    sets = []
    for moment in range(sections):
        first = moment == 0
        layer = sections - 1 - moment
        split = layer > 0 and layer % 2 == 0
        in_place = 0 < moment < sections - 1
        inputs = (top_nodes, own_top, *second_in) if first else incoming
        if in_place:
            inputs = (*inputs, pay, keep)
        made = call(
            functools.partial(chain_kernel, span, batches, chunk, first, layer),
            "chain",
            [SMEM] + [VMEM] * (len(inputs) + 5),
            [like(total + node_count), like(2 * total + 4 * node_count), like(node_count)] + [like(total)] * split,
            [pltpu.VMEM((total, width), BF)] if first else [],
            3 * 10**9,
            10 * 2**20,
            {3: 0, 4: 1} if in_place else {},
        )(info, *inputs, *stages[moment % 2], turned)
        pay, keep, part = made[:3]
        if split:
            came = move(made[3], [layer], both_ways, -1)
            summed = part.astype(F32) + move(part, [layer], swap).astype(F32)
            incoming = (came, move(summed.astype(BF), [layer], both_ways, -1))
        elif layer > 0:
            cross = move(part, [layer], swap, -1)
            came = move(pay, [layer], both_ways, -1)
            incoming = (came, cross)
        if layer <= 1:
            sets.append(weight_grads(layer, sections if layer else 1, keep, pay))

    grad_shape = jax.ShapeDtypeStruct((1, share, width), F32)
    return call(
        functools.partial(finish_kernel, span, batches, groups),
        "finish",
        [SMEM] + [VMEM] * (4 * span),
        [
            jax.ShapeDtypeStruct((1, batches, node_share, width), BF),
            jax.ShapeDtypeStruct((1, batches, count, width), BF),
        ]
        + [grad_shape] * 7,
        [pltpu.VMEM((batches, PARTS, rows, width), BF)],
        0,
        5 * 2**20,
    )(info, *sets[0], *sets[1])


def solution(mesh):
    in_specs = (
        P("section", None, None, None),
        P("section", None, "edge", None),
        P(),
        P(None, "edge", None),
        P(None, "edge", None),
        P(None, "edge"),
        P(None, "edge"),
        P("section", None, None),
        P("section", None, None),
        P("section", None, None),
        P("section", None, None),
        P("section", None, None),
        P("section", None, None),
        P("section", None, None),
    )
    out_specs = (
        P("section", None, "edge", None),
        P("section", None, "edge", None),
        P("section", "edge", None),
        P("section", "edge", None),
        P("section", "edge", None),
        P("section", "edge", None),
        P("section", "edge", None),
        P("section", "edge", None),
        P("section", "edge", None),
    )
    return jax.shard_map(body, mesh=mesh, in_specs=in_specs, out_specs=out_specs, check_vma=False)
```

```python
import functools

import jax
import jax.numpy as jnp
from jax import lax
from jax.experimental import pallas as pl
from jax.experimental.pallas import tpu as pltpu
from jax.sharding import PartitionSpec as P

BLOCK = 128
PARTS = 2
PAD = 16
SEND, RECV, EDGE, MSG, NODE, AGG, OUT = range(7)
GRANT = 32
BF = jnp.bfloat16
F32 = jnp.float32
ANY = pl.BlockSpec(memory_space=pl.ANY)
SMEM = pl.BlockSpec(memory_space=pltpu.SMEM)
VMEM = pl.BlockSpec(memory_space=pltpu.VMEM)


def matmul(left, right):
    return jnp.dot(left, right, preferred_element_type=F32)


def times_transposed(left, right):
    return lax.dot_general(left, right, (((1,), (1,)), ((), ())), preferred_element_type=F32)


def transposed_times(left, right):
    return lax.dot_general(left, right, (((0,), (0,)), ((), ())), preferred_element_type=F32)


def base_of(half, span, batches):
    return jnp.where(half == 0, span - batches, 0)


def place_of(batch, half, span, batches):
    return (span - batches if half == 0 else 0) + batch


def worker_of(batch, half, span, batches):
    return half * span + place_of(batch, half, span, batches)


def own_batch(member, span, batches):
    half = lax.div(member, span)
    batch = lax.rem(member, span) - base_of(half, span, batches)
    return jnp.clip(batch, 0, batches - 1)


def pick_row(table, row, lanes):
    value = table[0:1, lanes]
    for other in range(1, table.shape[0]):
        value = jnp.where(row == other, table[other : other + 1, lanes], value)
    return value


def hot_rows(index_rows, row, nodes):
    index = index_rows[row : row + 1, :].astype(F32).astype(jnp.int32)
    rows = lax.broadcasted_iota(jnp.int32, (nodes, index_rows.shape[1]), 0)
    return jnp.where(rows == index, 1.0, 0.0).astype(BF)


def hot_columns(index_rows, row, nodes):
    pick = lax.broadcasted_iota(jnp.int32, (index_rows.shape[0], nodes), 0) == row
    index = transposed_times(index_rows, jnp.where(pick, 1.0, 0.0).astype(BF))
    columns = lax.broadcasted_iota(jnp.int32, index.shape, 1).astype(F32)
    return jnp.where(columns == index, 1.0, 0.0).astype(BF)


def slope_of(pre, sigma):
    return (sigma * (1.0 + pre * (1.0 - sigma))).astype(BF)


def pack_kernel(span, batches, sections, info, senders, receivers, tiles, edges, tops, *refs):
    own, own_top = refs[:2]
    outs, seconds = refs[2 : span + 1], refs[span + 1 :]
    member = info[1]
    half = lax.div(member, span)
    offset = lax.rem(member, span)
    count = senders.shape[1]
    tile_count = tiles.shape[1]
    tile_len = count // tile_count
    top = info[0] == sections - 1
    for step in range(span):
        batch = lax.rem(offset - step + span, span) - base_of(half, span, batches)
        batch = jnp.clip(batch, 0, batches - 1)
        out = outs[step - 1] if step else own
        out[:count] = edges[0, batch]
        out[count:] = jnp.zeros((PAD, out.shape[1]), BF)
        for tile in range(tile_count):
            lanes = slice(tile * tile_len, (tile + 1) * tile_len)
            send = pick_row(senders, batch, lanes) + tiles[batch, tile, 0] * BLOCK
            recv = pick_row(receivers, batch, lanes) + tiles[batch, tile, 1] * BLOCK
            which = lax.broadcasted_iota(jnp.int32, (PAD, tile_len), 0)
            block = jnp.where(which == 0, send, jnp.where(which == 1, recv, 0))
            out[count:, lanes] = block.astype(F32).astype(BF)
        if step:
            second = seconds[step - 1]
            second[count:] = out[count:]

            @pl.when(top)
            def _(second=second, batch=batch):
                second[:count] = tops[batch]

            @pl.when(jnp.logical_not(top))
            def _(second=second, out=out):
                second[:count] = out[:count]

        else:
            own_top[...] = tops[batch]


def ready_kernel(span, batches, info, nodes, weights, turned, hidden, node_pre, feats_turned):
    batch = own_batch(info[1], span, batches)
    node_count = nodes.shape[2]
    feats = nodes[0, batch]
    hidden[:node_count] = matmul(feats, weights[SEND]).astype(BF)
    hidden[node_count:] = matmul(feats, weights[RECV]).astype(BF)
    node_pre[...] = matmul(feats, weights[NODE])
    feats_turned[...] = feats.T
    for slot in range(weights.shape[0]):
        turned[slot] = weights[slot].T


def takes_part(info, sections, group):
    return lax.rem(sections - 1 - info[0], 2) == group


def forward_kernel(span, chunk, sections, group, info, *refs):
    @pl.when(takes_part(info, sections, group))
    def _():
        forward_step(span, chunk, *refs)


def forward_step(span, chunk, own, *refs):
    others = refs[: span - 1]
    hidden, weights = refs[span - 1 : span + 1]
    act_out, slope_out, part_out, hot_out, hots_out, pieces, both = refs[span + 1 :]
    count = own.shape[0] - PAD
    node_count = part_out.shape[0]
    for step in range(span):
        piece = others[step - 1] if step else own
        run = slice(step * count, (step + 1) * count)
        pieces[run] = piece[:count]
        index_rows = piece[count:, :count]
        hots_out[:node_count, run] = hot_rows(index_rows, 0, node_count)
        hots_out[node_count:, run] = hot_rows(index_rows, 1, node_count)
        both[run, :node_count] = hot_columns(index_rows, 0, node_count)
        recv_hot = hot_columns(index_rows, 1, node_count)
        both[run, node_count:] = recv_hot
        hot_out[run] = recv_hot
    for at in range(0, span * count, chunk):
        run = slice(at, at + chunk)
        pre = matmul(both[run], hidden[...]) + matmul(pieces[run], weights[EDGE])
        sigma = jax.nn.sigmoid(pre)
        act_out[run] = (pre * sigma).astype(BF)
        slope_out[run] = slope_of(pre, sigma)
    total = matmul(hots_out[node_count:], act_out[...])
    part_out[...] = matmul(total.astype(BF), weights[MSG]).astype(BF)


def turn_kernel(sections, group, info, pieces, act, edges_turned, act_turned):
    @pl.when(takes_part(info, sections, group))
    def _():
        rows = 2 * BLOCK
        for at in range(0, act.shape[0], rows):
            run = slice(at, at + rows)
            edges_turned[:, run] = pieces[run].T
            act_turned[:, run] = act[run].T


def node_kernel(sections, group, info, node_pre, part_own, part_other, weights, turned_first, out):
    @pl.when(takes_part(info, sections, group))
    def _():
        count = part_own.shape[0]
        agg = (part_own[...].astype(F32) + part_other[...].astype(F32)).astype(BF)
        pre = node_pre[...] + matmul(agg, weights[AGG])
        sigma = jax.nn.sigmoid(pre)
        out[:count] = agg
        out[count : 2 * count] = (pre * sigma).astype(BF)
        out[2 * count :] = slope_of(pre, sigma)


def chain_kernel(span, batches, chunk, first, active, info, *refs):
    several = span + 1 if first else 2
    incoming, refs = refs[:several], refs[several:]
    kept = ()
    if len(refs) > 8 and not first:
        kept, refs = refs[:2], refs[2:]

    @pl.when(info[0] == active)
    def _():
        chain_step(span, batches, chunk, first, info, incoming, *refs)

    if kept:

        @pl.when(info[0] != active)
        def _():
            refs[5][...] = kept[0][...]
            refs[6][...] = kept[1][...]


def chain_step(
    span, batches, chunk, first, info, incoming, hot, hots, slope, node_pack, turned, pay, keep, part_out, *rest
):
    member = info[1]
    batch = own_batch(member, span, batches)
    half = lax.div(member, span)
    total = slope.shape[0]
    if first:
        top_nodes, pieces = incoming[0], incoming[1:]
        came = rest[-1]
        count = total // span
        for step, piece in enumerate(pieces):
            came[step * count : (step + 1) * count] = piece[:count]
        grad = top_nodes[batch]
    else:
        came, other = incoming
        if came.shape[0] == total:
            grad = other[...]
        else:
            grad = (came[total:].astype(F32) + other[...].astype(F32)).astype(BF)
    node_count = part_out.shape[0]
    node_at = 2 * total
    delta = (matmul(grad, turned[OUT]) * node_pack[2 * node_count :].astype(F32)).astype(BF)
    agg_grad = matmul(delta, turned[AGG]).astype(BF)
    keep[node_at : node_at + node_count] = delta
    keep[node_at + node_count : node_at + 2 * node_count] = grad
    for at in range(0, total, chunk):
        run = slice(at, at + chunk)
        before = came[run].astype(F32)
        message_grad = (before + matmul(hot[run], agg_grad)).astype(BF)
        keep[run] = message_grad
        edge_delta = (matmul(message_grad, turned[MSG]) * slope[run].astype(F32)).astype(BF)
        keep[total + at : total + at + chunk] = edge_delta
        below = (before + matmul(edge_delta, turned[EDGE])).astype(BF)
        pay[run] = below
        if rest and not first:
            rest[0][run] = below
    sums = matmul(hots[...], keep[total : 2 * total]).astype(BF)
    keep[node_at + 2 * node_count :] = sums
    own = grad.astype(F32) + matmul(delta, turned[NODE])
    own = own * jnp.where(half == 0, 1.0, 0.0)
    part = matmul(sums[:node_count], turned[SEND]) + matmul(sums[node_count:], turned[RECV])
    part = (own + part).astype(BF)
    pay[total:] = part
    part_out[...] = part


def grads_kernel(span, batches, groups, sections, low, high, info, *refs):
    for group in range(2):

        @pl.when(takes_part(info, sections, group) & (info[0] >= low) & (info[0] < high))
        def _(group=group):
            grads_step(span, batches, groups, info, *refs[3 * group : 3 * group + 3], *refs[6:])


def grads_step(span, batches, groups, info, edges_turned, act_turned, node_pack, feats_turned, keep, pay, *refs):
    near, far = refs[:span], refs[span : 2 * span]
    sums = refs[2 * span]
    member = info[1]
    half = lax.div(member, span)
    offset = lax.rem(member, span)
    batch = own_batch(member, span, batches)
    total = edges_turned.shape[1]
    node_count = feats_turned.shape[1]
    width = feats_turned.shape[0]
    count = total // span
    node_at = 2 * total
    delta = keep[node_at : node_at + node_count]
    grad = keep[node_at + node_count : node_at + 2 * node_count]
    sums[0] = matmul(feats_turned[...], keep[node_at + 2 * node_count : node_at + 3 * node_count]).astype(BF)
    sums[1] = matmul(feats_turned[...], keep[node_at + 3 * node_count :]).astype(BF)
    sums[2] = matmul(edges_turned[...], keep[total : 2 * total]).astype(BF)
    sums[3] = matmul(act_turned[...], keep[:total]).astype(BF)
    sums[5] = transposed_times(node_pack[:node_count], delta).astype(BF)

    @pl.when(half == 0)
    def _():
        sums[4] = matmul(feats_turned[...], delta).astype(BF)

    @pl.when(half != 0)
    def _():
        sums[4] = transposed_times(node_pack[node_count : 2 * node_count], grad).astype(BF)

    share = width // groups
    node_share = node_count // groups

    def fill(block, start, owner):
        at = pl.multiple_of(owner * share, share)
        for slot in range(5):
            block[start + slot * share : start + (slot + 1) * share] = sums[slot, pl.ds(at, share)]
        at_half = pl.multiple_of(owner * share + half * (share // 2), share // 2)
        block[start + 5 * share : start + 5 * share + share // 2] = sums[5, pl.ds(at_half, share // 2)]
        at_node = pl.multiple_of(total + owner * node_share, node_share)
        block[start + 5 * share + share // 2 :] = pay[pl.ds(at_node, node_share)]

    for step in range(span):
        near[step][:count] = pay[step * count : (step + 1) * count]
        fill(near[step], count, half * span + lax.rem(offset + step, span))
        fill(far[step], 0, (1 - half) * span + lax.rem(batch + step, span))


def finish_kernel(span, batches, groups, info, *refs):
    sets = (refs[: 2 * span], refs[2 * span : 4 * span])
    refs = refs[4 * span :]
    nodes_out, edges_out, send_out, recv_out, edge_out, msg_out, node_out, agg_out, out_out = refs[:9]
    held = refs[9]
    member = info[1]
    half = lax.div(member, span)
    offset = lax.rem(member, span)
    count = edges_out.shape[2]
    for which in range(2):

        @pl.when((info[0] == 0) == (which == 1))
        def _(which=which):
            near, far = sets[which][:span], sets[which][span:]
            for batch in range(batches):
                turn = lax.rem(offset - base_of(half, span, batches) - batch + 2 * span, span)
                turn_far = lax.rem(offset - batch + span, span)
                for step in range(span):

                    @pl.when(turn == step)
                    def _(step=step, batch=batch):
                        edges_out[0, batch] = near[step][:count]
                        held[batch, half] = near[step][count:]

                    @pl.when(turn_far == step)
                    def _(step=step, batch=batch):
                        held[batch, 1 - half] = far[step][...]

    share = send_out.shape[1]
    for slot, out in enumerate((send_out, recv_out, edge_out, msg_out)):
        rows = slice(slot * share, (slot + 1) * share)
        value = None
        for batch in range(batches):
            for part in range(PARTS):
                piece = held[batch, part, rows].astype(F32)
                value = piece if value is None else value + piece
        out[0] = value

    def over_batches(part, start, length):
        value = None
        for batch in range(batches):
            piece = held[batch, part, start : start + length].astype(F32)
            value = piece if value is None else value + piece
        return value

    node_out[0] = over_batches(0, 4 * share, share)
    out_out[0] = over_batches(1, 4 * share, share)
    for part in range(PARTS):
        agg_out[0, part * (share // 2) : (part + 1) * (share // 2)] = over_batches(part, 5 * share, share // 2)
    at = 5 * share + share // 2
    for batch in range(batches):
        rows = held[batch, 0, at:].astype(F32) + held[batch, 1, at:].astype(F32)
        nodes_out[0, batch] = rows.astype(BF)


def call(kernel, name, in_specs, out_shapes, scratch, flops, touched, aliases={}, grant=GRANT):
    many = isinstance(out_shapes, list)
    return pl.pallas_call(
        kernel,
        name=name,
        out_shape=out_shapes,
        in_specs=in_specs,
        out_specs=[VMEM] * len(out_shapes) if many else VMEM,
        scratch_shapes=scratch,
        input_output_aliases=aliases,
        compiler_params=pltpu.CompilerParams(vmem_limit_bytes=grant * 2**20),
        cost_estimate=pl.CostEstimate(flops=flops, bytes_accessed=touched, transcendentals=0),
    )


def body(
    layer_nodes,
    layer_edges,
    top_nodes,
    top_edges,
    tile_blocks,
    senders,
    receivers,
    w_send,
    w_recv,
    w_edge,
    w_msg,
    w_node,
    w_agg,
    w_out,
):
    sections = lax.axis_size("section")
    groups = lax.axis_size("edge")
    section = lax.axis_index("section")
    member = lax.axis_index("edge")
    span = groups // PARTS
    _, batches, node_count, width = layer_nodes.shape
    count = layer_edges.shape[2]
    total = span * count
    chunk = 2 * count
    share = width // groups
    node_share = node_count // groups
    info = jnp.stack([section, member]).astype(jnp.int32)
    axes = ("section", "edge")
    works = [(m, h) for h in range(PARTS) for m in range(batches)]

    def worker(m, h):
        return worker_of(m, h, span, batches)

    def source(m, h, step):
        return h * span + (place_of(m, h, span, batches) + step) % span

    def move(value, layers, links, shift=0):
        pairs = [(s * groups + a, (s + shift) * groups + b) for s in layers for a, b in links]
        return lax.ppermute(value, axes, pairs)

    every = list(range(sections))
    last = [sections - 1]
    collect = [[(source(m, h, step), worker(m, h)) for m, h in works] for step in range(span)]
    deliver = [[(b, a) for a, b in links] for links in collect]

    def like(rows, cols=width, kind=BF):
        return jax.ShapeDtypeStruct((rows, cols), kind)

    packed = call(
        functools.partial(pack_kernel, span, batches, sections),
        "pack",
        [SMEM, VMEM, VMEM, SMEM, VMEM, VMEM],
        [like(count + PAD), like(count)] + [like(count + PAD)] * (2 * span - 2),
        [],
        0,
        2**20,
    )(info, senders, receivers, tile_blocks, layer_edges, top_edges)
    own, own_top, first_out, second_out = packed[0], packed[1], packed[2 : span + 1], packed[span + 1 :]
    groups_of = [list(range(sections - 1 - group, -1, -2)) for group in range(2)]
    first_in = [move(piece, groups_of[0], collect[step + 1]) for step, piece in enumerate(first_out)]
    own, w_send, w_recv, w_edge, w_msg, w_node, w_agg, w_out = lax.optimization_barrier(
        (own, w_send, w_recv, w_edge, w_msg, w_node, w_agg, w_out)
    )
    weights = jnp.concatenate([w_send, w_recv, w_edge, w_msg, w_node, w_agg, w_out], axis=0)
    ready = call(
        functools.partial(ready_kernel, span, batches),
        "ready",
        [SMEM, VMEM, VMEM],
        [
            jax.ShapeDtypeStruct((7, width, width), BF),
            like(2 * node_count),
            like(node_count, kind=F32),
            like(width, node_count),
        ],
        [],
        4 * 10**8,
        10 * 2**20,
    )(info, layer_nodes, weights)
    turned, hidden, node_pre, feats_turned = ready
    first_in[0], second_out = lax.optimization_barrier((first_in[0], second_out))
    second_in = [move(piece, groups_of[1] + last, collect[step + 1]) for step, piece in enumerate(second_out)]

    swap = [(worker(m, h), worker(m, 1 - h)) for m, h in works]
    stages, after = [], []
    for group, arrived in enumerate((first_in, second_in)):
        act, slope, part, hot, hots, pieces = call(
            functools.partial(forward_kernel, span, chunk, sections, group),
            "forward",
            [SMEM] + [VMEM] * (span + 2),
            [like(total), like(total), like(node_count), like(total, node_count), like(2 * node_count, total)]
            + [like(total)],
            [pltpu.VMEM((total, 2 * node_count), BF)],
            2 * 10**9,
            6 * 2**20,
        )(info, own, *arrived, hidden, weights)
        part_other = move(part, groups_of[group], swap)
        edges_turned, act_turned = call(
            functools.partial(turn_kernel, sections, group),
            "turn",
            [SMEM] + [VMEM] * 2,
            [like(width, total), like(width, total)],
            [],
            0,
            4 * 2**20,
        )(info, pieces, act)
        node_pack = call(
            functools.partial(node_kernel, sections, group),
            "node_forward",
            [SMEM] + [VMEM] * 4 + [ANY],
            like(3 * node_count),
            [],
            10**5,
            2**10,
        )(info, node_pre, part, part_other, weights, edges_turned)
        stages.append((hot, hots, slope, node_pack))
        after += [edges_turned, act_turned, node_pack]

    both_ways = [(worker(m, h), worker(m, h)) for m, h in works]
    rows = 5 * share + share // 2 + node_share
    pay = keep = None
    incoming = None
    across = [[(worker(m, h), (1 - h) * span + (m + step) % span) for m, h in works] for step in range(span)]

    def weight_grads(low, high, keep, pay):
        out = call(
            functools.partial(grads_kernel, span, batches, groups, sections, low, high),
            "weight_grads",
            [SMEM] + [VMEM] * 9,
            [like(count + rows)] * span + [like(rows)] * span,
            [pltpu.VMEM((6, width, width), BF)],
            2 * 10**10,
            100 * 2**20,
        )(info, *after, feats_turned, keep, pay)
        layers = list(range(low, high))
        near = [out[0]] + [move(out[step], layers, deliver[step]) for step in range(1, span)]
        return near, list(out[span:]), layers

    sets = []
    for moment in range(sections):
        first = moment == 0
        layer = sections - 1 - moment
        split = layer > 0 and layer % 2 == 0
        in_place = 0 < moment < sections - 1
        inputs = (top_nodes, own_top, *second_in) if first else incoming
        if in_place:
            inputs = (*inputs, pay, keep)
        made = call(
            functools.partial(chain_kernel, span, batches, chunk, first, layer),
            "chain",
            [SMEM] + [VMEM] * (len(inputs) + 5),
            [like(total + node_count), like(2 * total + 4 * node_count), like(node_count)] + [like(total)] * split,
            [pltpu.VMEM((total, width), BF)] if first else [],
            3 * 10**9,
            10 * 2**20,
            {3: 0, 4: 1} if in_place else {},
        )(info, *inputs, *stages[moment % 2], turned)
        pay, keep, part = made[:3]
        if split:
            came = move(made[3], [layer], both_ways, -1)
            summed = part.astype(F32) + move(part, [layer], swap).astype(F32)
            incoming = (came, move(summed.astype(BF), [layer], both_ways, -1))
        elif layer > 0:
            cross = move(part, [layer], swap, -1)
            came = move(pay, [layer], both_ways, -1)
            incoming = (came, cross)
        if layer <= 1:
            if sets:
                pay, sets[0][1][:] = lax.optimization_barrier((pay, sets[0][1]))
            sets.append(weight_grads(layer, sections if layer else 1, keep, pay))

    blocks = []
    for near, far, layers in sets:
        blocks += near + [move(block, layers, across[step]) for step, block in enumerate(far)]
    grad_shape = jax.ShapeDtypeStruct((1, share, width), F32)
    return call(
        functools.partial(finish_kernel, span, batches, groups),
        "finish",
        [SMEM] + [VMEM] * (4 * span),
        [
            jax.ShapeDtypeStruct((1, batches, node_share, width), BF),
            jax.ShapeDtypeStruct((1, batches, count, width), BF),
        ]
        + [grad_shape] * 7,
        [pltpu.VMEM((batches, PARTS, rows, width), BF)],
        0,
        5 * 2**20,
    )(info, *blocks)


def solution(mesh):
    in_specs = (
        P("section", None, None, None),
        P("section", None, "edge", None),
        P(),
        P(None, "edge", None),
        P(None, "edge", None),
        P(None, "edge"),
        P(None, "edge"),
        P("section", None, None),
        P("section", None, None),
        P("section", None, None),
        P("section", None, None),
        P("section", None, None),
        P("section", None, None),
        P("section", None, None),
    )
    out_specs = (
        P("section", None, "edge", None),
        P("section", None, "edge", None),
        P("section", "edge", None),
        P("section", "edge", None),
        P("section", "edge", None),
        P("section", "edge", None),
        P("section", "edge", None),
        P("section", "edge", None),
        P("section", "edge", None),
    )
    return jax.shard_map(body, mesh=mesh, in_specs=in_specs, out_specs=out_specs, check_vma=False)
```
